512 devices in a mesh: node: 16 (over z_hi, y, core), local: 8 (over z_lo), rep: 4 (over x).
Axes of the slice: x: 4, y: 4, z: 16 (z_hi: 2, z_lo: 8; z = z_hi * 8 + z_lo), core: 2. Of those that a mesh axis runs over, the one named last changes fastest.
Arguments:
- tokens: bfloat16 [8192, 2048], P(('node', 'local', 'rep')), may hold values from -6 to 6
- out_grad: bfloat16 [8192, 2048], P(('node', 'local', 'rep')), may hold values from -6 to 6
- expert_ids: int32 [8192, 8], P(('node', 'local', 'rep')), may hold values from 0 to 127, all different within a row; in each aligned block of 16 rows (0 to 15, 16 to 31, ...) at most 2 rows name the same one
- keep_flags: int32 [8192, 8], P(('node', 'local', 'rep')), may hold values 0 or 1
- route_weights: bfloat16 [8192, 8], P(('node', 'local', 'rep')), may hold values from 0.049804688 to 0.59765625
- gate_w: bfloat16 [128, 768, 2048], P(('node', 'local'), 'rep'), may hold values from -0.125 to 0.125
- up_w: bfloat16 [128, 768, 2048], P(('node', 'local'), 'rep'), may hold values from -0.125 to 0.125
- down_w: bfloat16 [128, 768, 2048], P(('node', 'local'), 'rep'), may hold values from -0.21875 to 0.21875
Outputs:
- input_grad: bfloat16 [8192, 2048], P(('node', 'local', 'rep'))
- route_grad: bfloat16 [8192, 8], P(('node', 'local', 'rep'))
- gate_grad: bfloat16 [128, 768, 2048], P(('node', 'local'), 'rep')
- up_grad: bfloat16 [128, 768, 2048], P(('node', 'local'), 'rep')
- down_grad: bfloat16 [128, 768, 2048], P(('node', 'local'), 'rep')
The draws below stay inside these ranges and needn't reach their ends.
Inputs may be any that keep to these rules, and one draw needn't show every extreme that they name: `expert_ids`: among the tokens of one device (each aligned block of 16 tokens) no expert is named more than 2 times, a bound that some block reaches. A token names 8 different experts.
All inputs are finite; a program needn't handle non-finite values. No bound on the sum of `keep_flags` on one device may be relied on, other than what follows from the above.
Results may differ from the reference program's by a relative error of at most 0.019.
Values may be sent and summed in bfloat16 or wider, within the bound.
No kernel may reach another device: no remote copies, remote signals or barrier semaphores. Data moves between devices by JAX's collectives and lax.ppermute only.
A program may use at most 64 MiB of HBM per device.

```python
import math
import jax
import jax.numpy as jnp
import numpy as np
from jax import lax

D = 2048
HID = 768
TOP = 8
TOK_DEV = 16
EXPERTS = 128
CAP = 2
ROWS = 1024
TOKENS = 8192
N_REP = 4


def place_ends(entries, key, least, top_value):
    longest = entries.shape.index(max(entries.shape))
    spots = []
    for shift in (0, 1):
        where = [jax.random.randint(jax.random.fold_in(key, axis), (), 0, length) for axis, length in enumerate(entries.shape)]
        where[longest] = (where[longest] + shift) % entries.shape[longest]
        spots.append(tuple(where))
    return entries.at[spots[0]].set(least).at[spots[1]].set(top_value)


def level_of(own_key, dims, split, least, largest):
    def one(dim, shards_of):
        steps = jax.random.uniform(jax.random.fold_in(jax.random.fold_in(own_key, 6), dim), (shards_of,), jnp.float32, least / len(split), largest / len(split))
        return jnp.repeat(jnp.exp(steps), dims[dim] // shards_of).reshape((-1,) + (1,) * (len(dims) - dim - 1))

    level = one(*split[0])
    for cut in split[1:]:
        level = level * one(*cut)
    return level


def routed_block(key, own, number, rows, number_of, top, limit, lean):
    order = jax.random.permutation(key, number_of)
    crowded, ordinary = portions_of(number_of, rows * top, limit, lean, True), portions_of(number_of, rows * top, limit, lean, False)
    places = jnp.arange(number_of)

    def named(tallies, rotation):
        used = int((tallies > 0).sum())
        fixed = max(1, used // 4)
        shifted = fixed + (places - fixed + rotation * (used - fixed)) % max(1, number_of - fixed)
        return jnp.zeros((number_of,), jnp.int32).at[order[jnp.where(places < fixed, places, shifted)]].set(jnp.asarray(tallies, jnp.int32))

    tallies = jnp.where(number % 4 == 0, named(crowded, number // 4), named(ordinary, number - number // 4 - 1))
    mixed = jax.random.permutation(jax.random.fold_in(own, 3), number_of)
    source_of, sink = mixed[0:number_of // 2 * 2:2], mixed[1:number_of // 2 * 2:2]
    slack = jnp.minimum(tallies[source_of] - 1, limit - tallies[sink]) // 2
    slack = jnp.where((source_of == order[0]) | (sink == order[0]) | (tallies[sink] == 0), 0, jnp.maximum(slack, 0))
    shifted = jax.random.randint(jax.random.fold_in(own, 4), (number_of // 2,), 0, 1 << 20) % (slack + 1)
    tallies = tallies.at[source_of].add(-shifted).at[sink].add(shifted)
    members = jnp.searchsorted(jnp.cumsum(tallies), jnp.arange(rows * top), side="right").astype(jnp.int32)
    grid = members.reshape(top, rows).T
    grid = grid[jax.random.permutation(jax.random.fold_in(own, 1), rows)]
    rotation = jax.random.randint(jax.random.fold_in(own, 2), (rows, 1), 0, top)
    return jnp.take_along_axis(grid, (jnp.arange(top)[None, :] + rotation) % top, axis=1)


def portions_of(count, total, most, skew, full):
    portions = [(1 << 20) // math.isqrt(grade ** skew) + 1 for grade in range(1, count + 1)]
    largest = most if full else min(most, max(-(-total // count), total * portions[0] // sum(portions)))
    least = 1 if total - largest >= count - 1 else 0
    holding, surplus = [largest] + [least] * (count - 1), total - largest - least * (count - 1)
    while surplus > 0:
        candidates = [i for i in range(1, count) if holding[i] < largest] or [i for i in range(1, count) if holding[i] < most]
        whole, remaining = sum([portions[i] for i in candidates]), surplus
        for i in candidates:
            addition = min(most - holding[i], max(1, remaining * portions[i] // whole), surplus)
            holding[i] = holding[i] + addition
            surplus = surplus - addition
    return np.array(holding)


def noise(rng, dims, deviation, bound, pieces=(), held_as=jnp.bfloat16):
    level = level_of(rng, dims, pieces, -0.22, 0.18) if pieces else 1.0
    result = jax.random.normal(rng, dims, jnp.float32) * deviation * level
    return jnp.minimum(jnp.maximum(result, -bound), bound).astype(held_as)


def setup_inputs(seed: int = 0) -> dict:
    splits = jax.random.split(jax.random.key(seed), 9)
    tokens = noise(splits[0], (TOKENS, D), 1.0, 6.0, ((0, 512),))
    out_grad = noise(splits[1], (TOKENS, D), 1.0, 6.0, ((0, 512),))
    expert_ids_keys = jax.random.split(jax.random.fold_in(splits[2], 1), TOKENS // TOK_DEV)
    expert_ids_turns = jax.random.permutation(jax.random.fold_in(splits[2], 3), TOKENS // TOK_DEV)
    expert_ids = jax.vmap(lambda own, number: routed_block(jax.random.fold_in(splits[2], 2), own, number, TOK_DEV, EXPERTS, TOP, CAP, 2))(expert_ids_keys, expert_ids_turns).reshape((TOKENS, TOP))
    keep_flags = place_ends((jax.random.randint(splits[3], (TOKENS, TOP), 0, 8) < 7).astype(jnp.int32), jax.random.fold_in(splits[3], 1), 0, 1)
    route_weights = jnp.clip(0.049804688 + 0.54785156 * jax.random.uniform(splits[4], (TOKENS, TOP), jnp.float32) ** level_of(splits[4], (TOKENS, TOP), ((0, 512),), -0.2, 0.2), 0.049804688, 0.59765625).astype(jnp.bfloat16)
    gate_w = noise(splits[5], (EXPERTS, HID, D), D ** -0.5, 0.125, ((0, 128), (1, 4)))
    up_w = noise(splits[6], (EXPERTS, HID, D), D ** -0.5, 0.125, ((0, 128), (1, 4)))
    down_w = noise(splits[7], (EXPERTS, HID, D), HID ** -0.5, 0.21875, ((0, 128), (1, 4)))
    return dict(tokens=tokens, out_grad=out_grad, expert_ids=expert_ids, keep_flags=keep_flags, route_weights=route_weights, gate_w=gate_w, up_w=up_w, down_w=down_w)


def reference(tokens, out_grad, expert_ids, keep_flags, route_weights, gate_w, up_w, down_w):
    blocks = TOKENS // TOK_DEV
    width = TOK_DEV * TOP
    quarter = HID // N_REP
    chosen = expert_ids.reshape(blocks, width)
    kept = keep_flags.reshape(blocks, width)
    order = jnp.arange(width, dtype=jnp.int32)
    before = order[None, :] < order[:, None]
    matches = (chosen[:, :, None] == chosen[:, None, :]) & before[None] & (kept[:, None, :] > 0)
    position = jnp.sum(matches.astype(jnp.int32), axis=2)
    block_ids = jnp.arange(blocks, dtype=jnp.int32)[:, None]
    target_row = (block_ids * CAP + position).reshape(-1).astype(jnp.int32)
    target_expert = jnp.where(kept > 0, chosen, EXPERTS).reshape(-1).astype(jnp.int32)
    token_of = (jnp.arange(TOKENS * TOP, dtype=jnp.int32) // TOP).astype(jnp.int32)
    table = jnp.zeros((EXPERTS, ROWS), jnp.int32).at[target_expert, target_row].set(token_of, mode="drop")
    valid = jnp.zeros((EXPERTS, ROWS), jnp.float32).at[target_expert, target_row].set(1.0, mode="drop")
    coefs = jnp.zeros((EXPERTS, ROWS), jnp.float32).at[target_expert, target_row].set(
        route_weights.reshape(-1).astype(jnp.float32), mode="drop")
    high = lax.Precision.HIGHEST

    def rounded(value):
        return lax.optimization_barrier(value.astype(jnp.bfloat16)).astype(jnp.float32)

    def expert_step(carry, packed):
        table_e, valid_e, coef_e, gate_e, up_e, down_e = packed
        present = valid_e[:, None] > 0
        inputs = jnp.where(present, tokens[table_e].astype(jnp.float32), 0.0)
        grads_in = jnp.where(present, out_grad[table_e].astype(jnp.float32), 0.0)
        coef_col = coef_e[:, None]
        gate_q = gate_e.astype(jnp.float32).reshape(N_REP, quarter, D)
        up_q = up_e.astype(jnp.float32).reshape(N_REP, quarter, D)
        down_q = down_e.astype(jnp.float32).reshape(N_REP, quarter, D)
        gate_pre = jnp.einsum('rd,qhd->qrh', inputs, gate_q, precision=high)
        up_pre = jnp.einsum('rd,qhd->qrh', inputs, up_q, precision=high)
        sigma = jax.nn.sigmoid(gate_pre)
        active = gate_pre * sigma
        hidden = rounded(active * up_pre)
        scaled_grad = rounded(coef_col * grads_in)
        back_hidden = jnp.einsum('rd,qhd->qrh', grads_in, down_q, precision=high)
        scores = rounded(jnp.sum(hidden * back_hidden, axis=2))
        d_hidden = coef_col[None] * back_hidden
        d_gate = rounded(d_hidden * up_pre * sigma * (1.0 + gate_pre * (1.0 - sigma)))
        d_up = rounded(d_hidden * active)
        grad_down = jnp.einsum('qrh,rd->qhd', hidden, scaled_grad, precision=high).reshape(HID, D)
        grad_gate = jnp.einsum('qrh,rd->qhd', d_gate, inputs, precision=high).reshape(HID, D)
        grad_up = jnp.einsum('qrh,rd->qhd', d_up, inputs, precision=high).reshape(HID, D)
        partial_value = jnp.einsum('qrh,qhd->qrd', d_gate, gate_q, precision=high)
        partial_value = partial_value + jnp.einsum('qrh,qhd->qrd', d_up, up_q, precision=high)
        partial_sum = jnp.sum(rounded(partial_value), axis=0) * valid_e[:, None]
        carry = carry.at[table_e].add(partial_sum)
        return carry, (jnp.sum(scores, axis=0), grad_gate.astype(jnp.bfloat16),
                       grad_up.astype(jnp.bfloat16), grad_down.astype(jnp.bfloat16))

    start = jnp.zeros((TOKENS, D), jnp.float32)
    total, outs = lax.scan(expert_step, start, (table, valid, coefs, gate_w, up_w, down_w))
    score_all, gate_grad, up_grad, down_grad = outs
    picked = score_all[jnp.minimum(target_expert, EXPERTS - 1), target_row]
    route_grad = jnp.where(target_expert < EXPERTS, picked, 0.0).reshape(TOKENS, TOP)
    return (total.astype(jnp.bfloat16), route_grad.astype(jnp.bfloat16), gate_grad, up_grad, down_grad)
```

```python
import jax
import jax.numpy as jnp
from jax import lax
from jax.sharding import PartitionSpec as P

BF = jnp.bfloat16
F32 = jnp.float32


def dot(a, b, da, db):
    return lax.dot_general(a, b, (((da,), (db,)), ((), ())), preferred_element_type=F32)


def slots_of(ids, keep, capacity):
    width = ids.shape[0] * ids.shape[1]
    chosen = ids.reshape(width)
    kept = keep.reshape(width) > 0
    other = lax.broadcasted_iota(jnp.int32, (width, width), 1)
    own = lax.broadcasted_iota(jnp.int32, (width, width), 0)
    earlier = (other < own) & (chosen[:, None] == chosen[None, :]) & kept[None, :]
    position = jnp.sum(earlier.astype(jnp.int32), axis=1)
    return jnp.where(kept, chosen * capacity + position, -1)


def ring(step, n):
    return [(i, (i + step) % n) for i in range(n)]


def spread(block, axis, n):
    half = block.shape[0] // 2
    left = lax.ppermute(block, axis, ring(1, n))
    right = lax.ppermute(block, axis, ring(-1, n))
    far_a = lax.ppermute(right[:half], axis, ring(-1, n))
    far_b = lax.ppermute(left[half:], axis, ring(1, n))
    return block, left, right, jnp.concatenate([far_a, far_b], axis=0)


def collect(own, to_left, to_right, to_far, axis, n):
    half = own.shape[0] // 2
    far_a = lax.ppermute(to_far[:half], axis, ring(1, n))
    far_b = lax.ppermute(to_far[half:], axis, ring(-1, n))
    to_right = jnp.concatenate(
        [(to_right[:half].astype(F32) + far_a.astype(F32)).astype(BF), to_right[half:]], axis=0
    )
    to_left = jnp.concatenate(
        [to_left[:half], (to_left[half:].astype(F32) + far_b.astype(F32)).astype(BF)], axis=0
    )
    from_left = lax.ppermute(to_right, axis, ring(1, n))
    from_right = lax.ppermute(to_left, axis, ring(-1, n))
    return (own + from_left.astype(F32) + from_right.astype(F32)).astype(BF)


def local(tokens, out_grad, expert_ids, keep_flags, route_weights, gate_w, up_w, down_w):
    experts = lax.axis_size("node") * lax.axis_size("local")
    n = lax.axis_size("rep")
    tok_rows, top = expert_ids.shape
    features = tokens.shape[1]
    capacity = 2
    places = experts * capacity
    hidden_dev = gate_w.shape[1]
    slots = tok_rows * top

    target = slots_of(expert_ids, keep_flags, capacity)
    hits = lax.broadcasted_iota(jnp.int32, (places, slots), 0) == target[None, :]
    by_slot = hits.astype(BF)
    by_token = jnp.sum(hits.reshape(places, tok_rows, top).astype(F32), axis=2).astype(BF)

    rows = dot(by_token, jnp.concatenate([tokens, out_grad], axis=1), 1, 0).astype(BF)
    coef = jnp.sum(
        jnp.where(hits, route_weights.reshape(1, slots).astype(F32), 0.0), axis=1, keepdims=True
    ).astype(BF)
    packed = jnp.concatenate([rows, jnp.broadcast_to(coef, (places, 128))], axis=1)
    sent = lax.all_to_all(
        packed.reshape(experts, capacity, 2 * features + 128),
        ("node", "local"),
        split_axis=0,
        concat_axis=0,
        tiled=True,
    )

    gu_own = jnp.concatenate([gate_w[0], up_w[0]], axis=0)
    gu = jnp.concatenate(spread(gu_own, "rep", n), axis=0)
    dn = jnp.concatenate(spread(down_w[0], "rep", n), axis=0)

    flat = sent.reshape(places, 2 * features + 128)
    inputs = flat[:, :features]
    grads_in = flat[:, features : 2 * features]
    coef_col = flat[:, 2 * features : 2 * features + 1].astype(F32)
    scaled = (coef_col * grads_in.astype(F32)).astype(BF)

    pre = dot(inputs, gu, 1, 1).reshape(places, n, 2, hidden_dev)
    back = dot(grads_in, dn, 1, 1).reshape(places, n, hidden_dev)
    gate_pre, up_pre = pre[:, :, 0], pre[:, :, 1]
    sigma = jax.nn.sigmoid(gate_pre)
    active = gate_pre * sigma
    hidden = (active * up_pre).astype(BF)
    score = jnp.sum(hidden.astype(F32) * back, axis=(1, 2)).astype(BF)
    d_hidden = coef_col[:, :, None] * back
    d_gate = (d_hidden * up_pre * sigma * (1.0 + gate_pre * (1.0 - sigma))).astype(BF)
    d_up = (d_hidden * active).astype(BF)
    d_gu = jnp.stack([d_gate, d_up], axis=2)

    def gu_grad(i):
        return dot(d_gu[:, i].reshape(places, 2 * hidden_dev), inputs, 0, 0)

    def down_grad(i):
        return dot(hidden[:, i], scaled, 0, 0)

    part = [gu_grad(i) for i in range(n)]
    part_d = [down_grad(i) for i in range(n)]
    grad_gu = collect(part[0], *[p.astype(BF) for p in part[1:]], "rep", n)
    grad_dn = collect(part_d[0], *[p.astype(BF) for p in part_d[1:]], "rep", n)

    back_rows = dot(d_gu.reshape(places, n * 2 * hidden_dev), gu, 1, 0).astype(BF)
    back_pack = jnp.concatenate(
        [back_rows, jnp.broadcast_to(score[:, None], (places, 128))], axis=1
    )
    home = lax.all_to_all(
        back_pack.reshape(experts, capacity, features + 128),
        ("node", "local"),
        split_axis=0,
        concat_axis=0,
        tiled=True,
    ).reshape(places, features + 128)
    token_grad = dot(by_token, home[:, :features], 0, 0).astype(BF)
    slot_score = dot(by_slot, home[:, features:], 0, 0)[:, 0].reshape(tok_rows, top).astype(BF)
    return (
        token_grad,
        slot_score,
        grad_gu[:hidden_dev][None],
        grad_gu[hidden_dev:][None],
        grad_dn[None],
    )


def solution(mesh):
    by_row = P(("node", "local", "rep"), None)
    by_expert = P(("node", "local"), "rep", None)
    return jax.shard_map(
        local,
        mesh=mesh,
        in_specs=(by_row,) * 5 + (by_expert,) * 3,
        out_specs=(by_row,) * 2 + (by_expert,) * 3,
        check_vma=False,
    )
```

```python
import jax
import jax.numpy as jnp
from jax import lax
from jax.experimental import pallas as pl
from jax.experimental.pallas import tpu as pltpu
from jax.sharding import PartitionSpec as P

BF = jnp.bfloat16
F32 = jnp.float32
LANES = 128


def dot(a, b, da, db):
    return lax.dot_general(a, b, (((da,), (db,)), ((), ())), preferred_element_type=F32)


def slots_of(ids, keep, capacity):
    width = ids.shape[0] * ids.shape[1]
    chosen = ids.reshape(width)
    kept = keep.reshape(width) > 0
    other = lax.broadcasted_iota(jnp.int32, (width, width), 1)
    own = lax.broadcasted_iota(jnp.int32, (width, width), 0)
    earlier = (other < own) & (chosen[:, None] == chosen[None, :]) & kept[None, :]
    position = jnp.sum(earlier.astype(jnp.int32), axis=1)
    return jnp.where(kept, chosen * capacity + position, -1)


def shift(block, step, n):
    return lax.ppermute(block, "rep", [(i, (i + step) % n) for i in range(n)])


def spread(block, n):
    half = block.shape[0] // 2
    left = shift(block, 1, n)
    right = shift(block, -1, n)
    return left, right, shift(right[:half], -1, n), shift(left[half:], 1, n)


def rows_kernel(*refs):
    srcs, (p_ref, *d_refs), (gu, dn, x, g, sems) = refs[:13], refs[13:18], refs[18:]
    hid = dn.shape[1]
    half = hid // 2
    features = x.shape[1]
    targets = [
        x,
        g,
        gu.at[0, pl.ds(0, hid)],
        gu.at[0, pl.ds(hid, hid)],
        dn.at[0],
        gu.at[1],
        dn.at[1],
        gu.at[2],
        dn.at[2],
        gu.at[3, pl.ds(0, hid)],
        gu.at[3, pl.ds(hid, hid)],
        dn.at[3, pl.ds(0, half)],
        dn.at[3, pl.ds(half, half)],
    ]
    order = [(0, 1, 2, 3, 4), (5, 6), (7, 8), (9, 10, 11, 12)]
    copies = [pltpu.make_async_copy(s, t, sems.at[i]) for i, (s, t) in enumerate(zip(srcs, targets))]
    for copy in copies:
        copy.start()
    score = None
    for q, needed in enumerate(order):
        for i in needed:
            copies[i].wait()
        if q == 0:
            coef = g[:, features:].astype(F32).T[0:1, :]
        pre = dot(gu[q], x[...], 1, 1)
        back = dot(dn[q], g[:, :features], 1, 1)
        gate_pre, up_pre = pre[:hid], pre[hid:]
        sigma = jax.nn.sigmoid(gate_pre)
        active = gate_pre * sigma
        hidden = active * up_pre
        part = jnp.sum(hidden.astype(BF).astype(F32) * back, axis=0, keepdims=True)
        score = part if score is None else score + part
        d_hidden = coef * back
        d_refs[q][0:hid, :] = (
            d_hidden * up_pre * sigma * (1.0 + gate_pre * (1.0 - sigma))
        ).astype(BF)
        d_refs[q][hid : 2 * hid, :] = (d_hidden * active).astype(BF)
        d_refs[q][2 * hid :, :] = (coef * hidden).astype(BF)
    tile = 512
    for j in range(0, features, tile):
        total = None
        for q in range(4):
            part = dot(d_refs[q][: 2 * hid, :], gu[q, :, j : j + tile], 0, 0)
            total = part if total is None else total + part
        p_ref[:, j : j + tile] = total.astype(BF)
    p_ref[:, features:] = jnp.broadcast_to(score, (LANES, score.shape[1])).T.astype(BF)


def rows_call(x, g, gate, up, down, gu_far, dn_far):
    rows, features = x.shape
    hid = gate.shape[0]
    gu_left, gu_right, gu_a, gu_b = gu_far
    dn_left, dn_right, dn_a, dn_b = dn_far
    srcs = [x, g, gate, up, down, gu_left, dn_left, gu_right, dn_right, gu_a, gu_b, dn_a, dn_b]
    return pl.pallas_call(
        rows_kernel,
        out_shape=[jax.ShapeDtypeStruct((rows, features + LANES), BF)]
        + [jax.ShapeDtypeStruct((3 * hid, rows), BF)] * 4,
        in_specs=[pl.BlockSpec(memory_space=pl.ANY)] * len(srcs),
        out_specs=[pl.BlockSpec(memory_space=pltpu.VMEM)] * 5,
        scratch_shapes=[
            pltpu.VMEM((4, 2 * hid, features), BF),
            pltpu.VMEM((4, hid, features), BF),
            pltpu.VMEM((rows, features), BF),
            pltpu.VMEM((rows, features + LANES), BF),
            pltpu.SemaphoreType.DMA((len(srcs),)),
        ],
        compiler_params=pltpu.CompilerParams(vmem_limit_bytes=36 * 1024 * 1024),
        cost_estimate=pl.CostEstimate(
            flops=2 * rows * features * hid * 4 * 5,
            bytes_accessed=2 * features * hid * 12 + 6 * rows * features,
            transcendentals=rows * hid * 4,
        ),
        name="rows",
    )(*srcs)


def weights_kernel(*refs):
    d_refs, x_refs, g_refs, outs = refs[:4], refs[4:9], refs[9:14], refs[14:]
    hid = outs[0].shape[0]
    half = d_refs[3].shape[1] // 2

    def total(first, last, row_refs):
        parts = [dot(d[first:last, :], r[...], 1, 0) for d, r in zip(d_refs[:3], row_refs[:3])]
        parts.append(dot(d_refs[3][first:last, :half], row_refs[3][...], 1, 0))
        parts.append(dot(d_refs[3][first:last, half:], row_refs[4][...], 1, 0))
        return sum(parts[1:], parts[0]).astype(BF)

    gu = total(0, 2 * hid, x_refs)
    outs[0][...] = gu[:hid]
    outs[1][...] = gu[hid:]
    outs[2][...] = total(2 * hid, 3 * hid, g_refs)


def weights_call(ds, xs, gs, features):
    tile = 512
    hid = ds[0].shape[0] // 3
    whole = [pl.BlockSpec(d.shape, lambda j: (0, 0)) for d in ds]
    tiled = [pl.BlockSpec((a.shape[0], tile), lambda j: (0, j)) for a in [*xs, *gs]]
    rows = sum(d.shape[1] for d in ds)
    return pl.pallas_call(
        weights_kernel,
        grid=(features // tile,),
        out_shape=[jax.ShapeDtypeStruct((hid, features), BF)] * 3,
        in_specs=whole + tiled,
        out_specs=[pl.BlockSpec((hid, tile), lambda j: (0, j))] * 3,
        compiler_params=pltpu.CompilerParams(vmem_limit_bytes=24 * 1024 * 1024),
        cost_estimate=pl.CostEstimate(
            flops=2 * rows * features * hid * 3,
            bytes_accessed=2 * features * (2 * rows + 3 * hid),
            transcendentals=0,
        ),
        name="weight_grads",
    )(*ds, *xs, *gs)


def local(tokens, out_grad, expert_ids, keep_flags, route_weights, gate_w, up_w, down_w):
    experts = lax.axis_size("node") * lax.axis_size("local")
    n = lax.axis_size("rep")
    tok_rows, top = expert_ids.shape
    features = tokens.shape[1]
    capacity = 2
    places = experts * capacity
    slots = tok_rows * top

    target = slots_of(expert_ids, keep_flags, capacity)
    hits = lax.broadcasted_iota(jnp.int32, (places, slots), 0) == target[None, :]
    by_slot = hits.astype(BF)
    by_token = jnp.sum(hits.reshape(places, tok_rows, top).astype(F32), axis=2).astype(BF)

    def exchange(block):
        width = block.shape[1]
        return lax.all_to_all(
            block.reshape(experts, capacity, width),
            ("node", "local"),
            split_axis=0,
            concat_axis=0,
            tiled=True,
        ).reshape(places, width)

    x = exchange(dot(by_token, tokens, 1, 0).astype(BF))
    coef = jnp.sum(
        jnp.where(hits, route_weights.reshape(1, slots).astype(F32), 0.0), axis=1, keepdims=True
    ).astype(BF)
    g = exchange(
        jnp.concatenate(
            [dot(by_token, out_grad, 1, 0).astype(BF), jnp.broadcast_to(coef, (places, LANES))],
            axis=1,
        )
    )

    gate, up, down = gate_w[0], up_w[0], down_w[0]
    gu_far = spread(jnp.concatenate([gate, up], axis=0), n)
    dn_far = spread(down, n)
    x_far = spread(x, n)
    g_far = spread(g, n)

    rows, d_own, d_left, d_right, d_two = rows_call(x, g, gate, up, down, gu_far, dn_far)
    home = exchange(rows)
    ds = [d_own, shift(d_right, 1, n), shift(d_left, -1, n), shift(d_two, 2, n)]
    grad_gate, grad_up, grad_down = weights_call(ds, [x, *x_far], [g, *g_far], features)

    token_grad = dot(by_token, home[:, :features], 0, 0).astype(BF)
    slot_score = dot(by_slot, home[:, features:], 0, 0)[:, 0].reshape(tok_rows, top).astype(BF)
    return (token_grad, slot_score, grad_gate[None], grad_up[None], grad_down[None])


def solution(mesh):
    by_row = P(("node", "local", "rep"), None)
    by_expert = P(("node", "local"), "rep", None)
    return jax.shard_map(
        local,
        mesh=mesh,
        in_specs=(by_row,) * 5 + (by_expert,) * 3,
        out_specs=(by_row,) * 2 + (by_expert,) * 3,
        check_vma=False,
    )
```

```python
import jax
import jax.numpy as jnp
from jax import lax
from jax.experimental import pallas as pl
from jax.experimental.pallas import tpu as pltpu
from jax.sharding import Mesh, PartitionSpec as P

BF = jnp.bfloat16
F32 = jnp.float32
LANES = 128
CAPACITY = 2
MIB = 1024 * 1024
Z = ("zh", "zl")
YC = ("y", "c")
PLACE = ("zh", "y", "c", "zl")


def dot(a, b, da, db):
    return lax.dot_general(a, b, (((da,), (db,)), ((), ())), preferred_element_type=F32)


def iota(shape, axis):
    return lax.broadcasted_iota(jnp.int32, shape, axis)


def shift(block, step, axes, n):
    return lax.ppermute(block, axes, [(i, (i + step) % n) for i in range(n)])


def tied(*values):
    return lax.optimization_barrier(values)


def vmem():
    return pl.BlockSpec(memory_space=pltpu.VMEM)


def payload_kernel(tok_ref, grad_ref, ids_ref, keep_ref, weight_ref, out_ref, code_ref):
    features = tok_ref.shape[1]
    top, rows = ids_ref.shape
    experts = LANES
    ids, kept = ids_ref[...], keep_ref[...] > 0
    names = iota((experts, rows), 0)
    named = [names == ids[k : k + 1, :] for k in range(top)]
    tally = sum(jnp.where(named[k] & kept[k : k + 1, :], 1.0, 0.0) for k in range(top))
    before = (iota((rows, rows), 0) < iota((rows, rows), 1)).astype(BF)
    earlier = dot(tally.astype(BF), before, 1, 0)
    position = jnp.concatenate(
        [jnp.sum(jnp.where(named[k], earlier, 0.0), axis=0, keepdims=True) for k in range(top)],
        axis=0,
    )
    code = jnp.where(kept, ids.astype(F32) * CAPACITY + position + 1.0, 0.0)
    code_ref[...] = code
    spread = (iota((rows, LANES), 0) == iota((rows, LANES), 1)).astype(BF)
    both = jnp.concatenate([code.astype(BF), weight_ref[...]], axis=0)
    out_ref[:, :features] = tok_ref[...]
    out_ref[:, features : 2 * features] = grad_ref[...]
    out_ref[:, 2 * features :] = dot(both, spread, 1, 0).astype(BF)


def payload_call(tokens, out_grad, ids, keep, weights):
    rows, features = tokens.shape
    return pl.pallas_call(
        payload_kernel,
        out_shape=[
            jax.ShapeDtypeStruct((rows, 2 * features + LANES), BF),
            jax.ShapeDtypeStruct(ids.shape, F32),
        ],
        in_specs=[vmem()] * 5,
        out_specs=[vmem()] * 2,
        name="payload",
    )(tokens, out_grad, ids, keep, weights)


def pack_kernel(step, zs_ref, *refs):
    blocks, out_ref = refs[:-1], refs[-1]
    count = sum(b.shape[0] for b in blocks)
    zn = count // step
    rows, width = out_ref.shape
    features = (width - LANES) // 2
    half = step // 2
    codes = jnp.zeros((half, count), F32)
    weights = jnp.zeros((half, count), F32)
    at = 0
    for block in blocks:
        for first in range(0, block.shape[0], step):
            place = (iota((LANES, count), 0) + at == iota((LANES, count), 1)) & (
                iota((LANES, count), 0) < step
            )
            both = dot(
                block[first : first + step, 2 * features :], place.astype(BF), 1, 0
            )
            codes = codes + both[:half]
            weights = weights + both[half:]
            at += step
    zh, zl = zs_ref[0], zs_ref[1]
    row, col = iota((rows, count), 0), iota((rows, count), 1)
    dest = row // (zn * CAPACITY)
    wanted = ((zh * 64 + dest * 8 + zl) * CAPACITY + row % CAPACITY + 1).astype(F32)
    wanted = jnp.where((row // CAPACITY) % zn == col // step, wanted, -1.0)
    pick = jnp.zeros((rows, count), F32)
    coef = jnp.zeros((rows, count), F32)
    for k in range(half):
        hit = wanted == codes[k : k + 1, :]
        pick = pick + jnp.where(hit, 1.0, 0.0)
        coef = coef + jnp.where(hit, weights[k : k + 1, :], 0.0)
    pick = pick.astype(BF)
    tile = 1024
    for j in range(0, 2 * features, tile):
        total, at = None, 0
        for block in blocks:
            size = block.shape[0]
            part = dot(pick[:, at : at + size], block[:, j : j + tile], 1, 0)
            total = part if total is None else total + part
            at += size
        out_ref[:, j : j + tile] = total.astype(BF)
    out_ref[:, 2 * features :] = jnp.broadcast_to(
        jnp.sum(coef, axis=1, keepdims=True), (rows, LANES)
    ).astype(BF)


def pack_call(zs, blocks, step):
    count, width = sum(b.shape[0] for b in blocks), blocks[0].shape[1]
    rows = 8 * (count // step) * CAPACITY

    def body(*refs):
        pack_kernel(step, *refs)

    return pl.pallas_call(
        body,
        out_shape=jax.ShapeDtypeStruct((rows, width), BF),
        in_specs=[pl.BlockSpec(memory_space=pltpu.SMEM)] + [vmem()] * len(blocks),
        out_specs=vmem(),
        name="pack",
    )(zs, *blocks)


def homes(z, rows):
    row, place = iota((rows, rows), 0), iota((rows, rows), 1)
    quarter = rows // 4
    first, last = row < quarter, row >= 3 * quarter
    inside = jnp.where(first, row, jnp.where(last, row - 3 * quarter, row - quarter))
    zn = jnp.where(first | last, 4, 8)
    source = inside // (zn * CAPACITY)
    zi = (inside // CAPACITY) % zn
    near = jnp.where(zi < 4, -1 - 4 * zi, 17 - 4 * zi)
    offset = jnp.where(first, -4 * zi, jnp.where(last, 2 - 4 * zi, near))
    zed = (z + offset + 32) % 16
    home = ((zed // 8) * 64 + source * 8 + zed % 8) * CAPACITY + inside % CAPACITY
    return (home == place).astype(BF)


def rows_kernel(zs_ref, *refs):
    srcs, p_ref, dgu_refs, pd_refs = refs[:14], refs[14], refs[15:19], refs[19:23]
    gu, dn, rows, sems = refs[23:]
    hid = dn.shape[1]
    half = hid // 2
    count, width = rows.shape
    features = (width - LANES) // 2
    quarter = count // 4
    targets = [
        rows.at[pl.ds(0, quarter)],
        rows.at[pl.ds(quarter, 2 * quarter)],
        rows.at[pl.ds(3 * quarter, quarter)],
        gu.at[0, pl.ds(0, hid)],
        gu.at[0, pl.ds(hid, hid)],
        dn.at[0],
        gu.at[1],
        dn.at[1],
        gu.at[2],
        dn.at[2],
        gu.at[3, pl.ds(0, hid)],
        gu.at[3, pl.ds(hid, hid)],
        dn.at[3, pl.ds(0, half)],
        dn.at[3, pl.ds(half, half)],
    ]
    order = [(0, 1, 2, 3, 4, 5), (6, 7), (8, 9), (10, 11, 12, 13)]
    copies = [pltpu.make_async_copy(s, t, sems.at[i]) for i, (s, t) in enumerate(zip(srcs, targets))]
    for copy in copies:
        copy.start()
    home = homes(zs_ref[0] * 8 + zs_ref[1], count)
    score = None
    scaled = []
    for q, needed in enumerate(order):
        for i in needed:
            copies[i].wait()
        if q == 0:
            coef = rows[:, 2 * features :].astype(F32).T[0:1, :]
        pre = dot(gu[q], rows[:, :features], 1, 1)
        back = dot(dn[q], rows[:, features : 2 * features], 1, 1)
        gate_pre, up_pre = pre[:hid], pre[hid:]
        sigma = jax.nn.sigmoid(gate_pre)
        active = gate_pre * sigma
        hidden = active * up_pre
        part = jnp.sum(hidden.astype(BF).astype(F32) * back, axis=0, keepdims=True)
        score = part if score is None else score + part
        d_hidden = coef * back
        dgu_refs[q][0:hid, :] = (
            d_hidden * up_pre * sigma * (1.0 + gate_pre * (1.0 - sigma))
        ).astype(BF)
        dgu_refs[q][hid:, :] = (d_hidden * active).astype(BF)
        scaled.append((coef * hidden).astype(BF))
    moved = [dot(d[...], home, 1, 0).astype(BF) for d in dgu_refs]
    tile = 512
    for j in range(0, features, tile):
        total = None
        for q in range(4):
            part = dot(moved[q], gu[q, :, j : j + tile], 0, 0)
            total = part if total is None else total + part
        p_ref[:, j : j + tile] = total.astype(BF)
    score = dot(jnp.broadcast_to(score, (LANES, count)).astype(BF), home, 1, 0)
    p_ref[:, features:] = score.T.astype(BF)
    for j in range(0, features, tile):
        grads = rows[:, features + j : features + j + tile]
        for q in range(4):
            pd_refs[q][:, j : j + tile] = dot(scaled[q], grads, 1, 0).astype(pd_refs[q].dtype)


def rows_call(zs, chunks, gate, up, down, gu_far, dn_far):
    count = sum(c.shape[0] for c in chunks)
    width = chunks[0].shape[1]
    hid, features = gate.shape
    gu_left, gu_right, gu_a, gu_b = gu_far
    dn_left, dn_right, dn_a, dn_b = dn_far
    srcs = [*chunks, gate, up, down, gu_left, dn_left, gu_right, dn_right, gu_a, gu_b, dn_a, dn_b]
    return pl.pallas_call(
        rows_kernel,
        out_shape=[jax.ShapeDtypeStruct((count, features + LANES), BF)]
        + [jax.ShapeDtypeStruct((2 * hid, count), BF)] * 4
        + [jax.ShapeDtypeStruct((hid, features), F32)]
        + [jax.ShapeDtypeStruct((hid, features), BF)] * 3,
        in_specs=[pl.BlockSpec(memory_space=pltpu.SMEM)]
        + [pl.BlockSpec(memory_space=pl.ANY)] * len(srcs),
        out_specs=[vmem()] * 9,
        scratch_shapes=[
            pltpu.VMEM((4, 2 * hid, features), BF),
            pltpu.VMEM((4, hid, features), BF),
            pltpu.VMEM((count, width), BF),
            pltpu.SemaphoreType.DMA((len(srcs),)),
        ],
        compiler_params=pltpu.CompilerParams(vmem_limit_bytes=58 * MIB),
        cost_estimate=pl.CostEstimate(
            flops=2 * count * features * hid * 4 * 6,
            bytes_accessed=2 * features * hid * 18 + 6 * count * features,
            transcendentals=count * hid * 4,
        ),
        name="rows",
    )(zs, *srcs)


def weights_kernel(*refs):
    d_refs, x_refs, (gate_ref, up_ref) = refs[:4], refs[4:9], refs[9:]
    hid = gate_ref.shape[0]
    half = d_refs[3].shape[1] // 2
    parts = [dot(d[...], x[...], 1, 0) for d, x in zip(d_refs[:3], x_refs[:3])]
    parts.append(dot(d_refs[3][:, :half], x_refs[3][...], 1, 0))
    parts.append(dot(d_refs[3][:, half:], x_refs[4][...], 1, 0))
    total = sum(parts[1:], parts[0]).astype(BF)
    gate_ref[...] = total[:hid]
    up_ref[...] = total[hid:]


def weights_call(ds, xs):
    tile = 512
    hid, features = ds[0].shape[0] // 2, xs[0].shape[1]
    whole = [pl.BlockSpec(d.shape, lambda j: (0, 0)) for d in ds]
    tiled = [pl.BlockSpec((x.shape[0], tile), lambda j: (0, j)) for x in xs]
    rows = sum(d.shape[1] for d in ds)
    return pl.pallas_call(
        weights_kernel,
        grid=(features // tile,),
        out_shape=[jax.ShapeDtypeStruct((hid, features), BF)] * 2,
        in_specs=whole + tiled,
        out_specs=[pl.BlockSpec((hid, tile), lambda j: (0, j))] * 2,
        compiler_params=pltpu.CompilerParams(vmem_limit_bytes=24 * MIB),
        cost_estimate=pl.CostEstimate(
            flops=4 * rows * features * hid,
            bytes_accessed=2 * features * (rows + 2 * hid),
            transcendentals=0,
        ),
        name="weight_grads",
    )(*ds, *xs)


def home_kernel(code_ref, home_ref, grad_ref, score_ref):
    top, rows = code_ref.shape
    places = home_ref.shape[0]
    features = grad_ref.shape[1]
    wanted = (iota((places, rows), 0) + 1).astype(F32)
    hits = [jnp.where(wanted == code_ref[k : k + 1, :], 1.0, 0.0) for k in range(top)]
    score = home_ref[:, features : features + 1].astype(F32)
    score_ref[...] = jnp.concatenate(
        [jnp.sum(hit * score, axis=0, keepdims=True) for hit in hits], axis=0
    ).astype(BF)
    pick = sum(hits).astype(BF)
    grad_ref[...] = dot(pick, home_ref[:, :features], 0, 0).astype(BF)


def home_call(code, home, features):
    return pl.pallas_call(
        home_kernel,
        out_shape=[
            jax.ShapeDtypeStruct((code.shape[1], features), BF),
            jax.ShapeDtypeStruct(code.shape, BF),
        ],
        in_specs=[vmem()] * 2,
        out_specs=[vmem()] * 2,
        name="home",
    )(code, home)


def local(tokens, out_grad, expert_ids, keep_flags, route_weights, gate_w, up_w, down_w):
    nz, n = lax.axis_size(Z), lax.axis_size("x")
    step, features = tokens.shape
    zs = jnp.stack([lax.axis_index("zh"), lax.axis_index("zl")]).astype(jnp.int32)
    gate, up, down = gate_w[0], up_w[0], down_w[0]
    half = gate.shape[0] // 2

    own, code = payload_call(tokens, out_grad, expert_ids.T, keep_flags.T, route_weights.T)

    gu = jnp.concatenate([gate, up], axis=0)
    gu_left, gu_right = shift(gu, 1, "x", n), shift(gu, -1, "x", n)
    dn_left, dn_right = shift(down, 1, "x", n), shift(down, -1, "x", n)

    far = [shift(own, s, Z, nz) for s in (4, 8, 12)]
    chunk = jnp.concatenate([own, *far], axis=0)
    left, right = shift(chunk, 1, Z, nz), shift(chunk, -1, Z, nz)

    def exchange(packed):
        rows, width = packed.shape
        return lax.all_to_all(
            packed.reshape(8, rows // 8, width), YC, split_axis=0, concat_axis=0, tiled=True
        ).reshape(rows, width)

    rows_a = exchange(pack_call(zs, [chunk], step))
    rest_a = shift(right[: 2 * step], -1, Z, nz)
    rest_b = shift(left[step : 3 * step], 1, Z, nz)
    left, right, rows_a = tied(left, right, rows_a)
    packed = pack_call(zs, [left, right], step)

    hid = gate.shape[0]
    gu_a, gu_b = shift(gu_right[:hid], -1, "x", n), shift(gu_left[hid:], 1, "x", n)
    rows_b = exchange(packed)
    rest_a, rest_b, rows_b, dn_left, dn_right = tied(rest_a, rest_b, rows_b, dn_left, dn_right)
    dn_a, dn_b = shift(dn_right[:half], -1, "x", n), shift(dn_left[half:], 1, "x", n)
    rows_c = exchange(pack_call(zs, [rest_a, rest_b], step))

    chunks = [rows_a, rows_b, rows_c]
    x = jnp.concatenate([c[:, :features] for c in chunks], axis=0)
    mid = x.shape[0] // 2
    x_left, x_right = shift(x, 1, "x", n), shift(x, -1, "x", n)
    x_a, x_b = shift(x_right[:mid], -1, "x", n), shift(x_left[mid:], 1, "x", n)

    result = rows_call(
        zs,
        chunks,
        gate,
        up,
        down,
        (gu_left, gu_right, gu_a, gu_b),
        (dn_left, dn_right, dn_a, dn_b),
    )
    back, (d_own, d_left, d_right, d_two) = result[0], result[1:5]
    p_own, p_left, p_right, p_two = result[5:]
    home = lax.all_to_all(
        back.reshape(-1, CAPACITY, back.shape[1]), PLACE, split_axis=0, concat_axis=0, tiled=True
    ).reshape(back.shape)

    ds = [d_own, shift(d_right, 1, "x", n), shift(d_left, -1, "x", n), shift(d_two, 2, "x", n)]
    grad_gate, grad_up = weights_call(ds, [x, x_left, x_right, x_a, x_b])

    via_a = shift(p_two[:half], 1, "x", n)
    via_b = shift(p_two[half:], -1, "x", n)
    left_low = shift(p_right[half:], 1, "x", n)
    right_top = shift(p_left[:half], -1, "x", n)
    left_top = shift((p_right[:half].astype(F32) + via_a.astype(F32)).astype(BF), 1, "x", n)
    right_low = shift((p_left[half:].astype(F32) + via_b.astype(F32)).astype(BF), -1, "x", n)
    grad_down = jnp.concatenate(
        [
            (p_own[:half] + left_top.astype(F32) + right_top.astype(F32)).astype(BF),
            (p_own[half:] + left_low.astype(F32) + right_low.astype(F32)).astype(BF),
        ],
        axis=0,
    )

    token_grad, slot_score = home_call(code, home, features)
    return (token_grad, slot_score.T, grad_gate[None], grad_up[None], grad_down[None])


def solution(mesh):
    fine = Mesh(mesh.devices.reshape(2, 4, 2, 8, 4), ("zh", "y", "c", "zl", "x"))
    by_row = P(("zh", "y", "c", "zl", "x"), None)
    by_expert = P(PLACE, "x", None)
    return jax.shard_map(
        local,
        mesh=fine,
        in_specs=(by_row,) * 5 + (by_expert,) * 3,
        out_specs=(by_row,) * 2 + (by_expert,) * 3,
        check_vma=False,
    )
```

```python
import jax
import jax.numpy as jnp
from jax import lax
from jax.experimental import pallas as pl
from jax.experimental.pallas import tpu as pltpu
from jax.sharding import Mesh, PartitionSpec as P

BF = jnp.bfloat16
F32 = jnp.float32
LANES = 128
CAPACITY = 2
MIB = 1024 * 1024
Z = ("zh", "zl")
YC = ("y", "c")
PLACE = ("zh", "y", "c", "zl")


def dot(a, b, da, db):
    return lax.dot_general(a, b, (((da,), (db,)), ((), ())), preferred_element_type=F32)


def iota(shape, axis):
    return lax.broadcasted_iota(jnp.int32, shape, axis)


def shift(block, step, axes, n):
    return lax.ppermute(block, axes, [(i, (i + step) % n) for i in range(n)])


def vmem():
    return pl.BlockSpec(memory_space=pltpu.VMEM)


def payload_kernel(tok_ref, grad_ref, ids_ref, keep_ref, weight_ref, out_ref, code_ref):
    features = tok_ref.shape[1]
    top, rows = ids_ref.shape
    experts = LANES
    ids, kept = ids_ref[...], keep_ref[...] > 0
    names = iota((experts, rows), 0)
    named = [names == ids[k : k + 1, :] for k in range(top)]
    tally = sum(jnp.where(named[k] & kept[k : k + 1, :], 1.0, 0.0) for k in range(top))
    before = (iota((rows, rows), 0) < iota((rows, rows), 1)).astype(BF)
    earlier = dot(tally.astype(BF), before, 1, 0)
    position = jnp.concatenate(
        [jnp.sum(jnp.where(named[k], earlier, 0.0), axis=0, keepdims=True) for k in range(top)],
        axis=0,
    )
    code = jnp.where(kept, ids.astype(F32) * CAPACITY + position + 1.0, 0.0)
    code_ref[...] = code
    spread = (iota((rows, LANES), 0) == iota((rows, LANES), 1)).astype(BF)
    both = jnp.concatenate([code.astype(BF), weight_ref[...]], axis=0)
    out_ref[:, :features] = tok_ref[...]
    out_ref[:, features : 2 * features] = grad_ref[...]
    out_ref[:, 2 * features :] = dot(both, spread, 1, 0).astype(BF)


def payload_call(tokens, out_grad, ids, keep, weights):
    rows, features = tokens.shape
    return pl.pallas_call(
        payload_kernel,
        out_shape=[
            jax.ShapeDtypeStruct((rows, 2 * features + LANES), BF),
            jax.ShapeDtypeStruct(ids.shape, F32),
        ],
        in_specs=[vmem()] * 5,
        out_specs=[vmem()] * 2,
        name="payload",
    )(tokens, out_grad, ids, keep, weights)


def pack_kernel(step, zs_ref, *refs):
    blocks, out_ref = refs[:-1], refs[-1]
    count = sum(b.shape[0] for b in blocks)
    zn = count // step
    rows, width = out_ref.shape
    features = (width - LANES) // 2
    half = step // 2
    codes = jnp.zeros((half, count), F32)
    weights = jnp.zeros((half, count), F32)
    at = 0
    for block in blocks:
        for first in range(0, block.shape[0], step):
            place = (iota((LANES, count), 0) + at == iota((LANES, count), 1)) & (
                iota((LANES, count), 0) < step
            )
            both = dot(
                block[first : first + step, 2 * features :], place.astype(BF), 1, 0
            )
            codes = codes + both[:half]
            weights = weights + both[half:]
            at += step
    zh, zl = zs_ref[0], zs_ref[1]
    row, col = iota((rows, count), 0), iota((rows, count), 1)
    dest = row // (zn * CAPACITY)
    wanted = ((zh * 64 + dest * 8 + zl) * CAPACITY + row % CAPACITY + 1).astype(F32)
    wanted = jnp.where((row // CAPACITY) % zn == col // step, wanted, -1.0)
    pick = jnp.zeros((rows, count), F32)
    coef = jnp.zeros((rows, count), F32)
    for k in range(half):
        hit = wanted == codes[k : k + 1, :]
        pick = pick + jnp.where(hit, 1.0, 0.0)
        coef = coef + jnp.where(hit, weights[k : k + 1, :], 0.0)
    pick = pick.astype(BF)
    tile = 1024
    for j in range(0, 2 * features, tile):
        total, at = None, 0
        for block in blocks:
            size = block.shape[0]
            part = dot(pick[:, at : at + size], block[:, j : j + tile], 1, 0)
            total = part if total is None else total + part
            at += size
        out_ref[:, j : j + tile] = total.astype(BF)
    out_ref[:, 2 * features :] = jnp.broadcast_to(
        jnp.sum(coef, axis=1, keepdims=True), (rows, LANES)
    ).astype(BF)


def pack_call(zs, blocks, step):
    count, width = sum(b.shape[0] for b in blocks), blocks[0].shape[1]
    rows = 8 * (count // step) * CAPACITY

    def body(*refs):
        pack_kernel(step, *refs)

    return pl.pallas_call(
        body,
        out_shape=jax.ShapeDtypeStruct((rows, width), BF),
        in_specs=[pl.BlockSpec(memory_space=pltpu.SMEM)] + [vmem()] * len(blocks),
        out_specs=vmem(),
        name="pack",
    )(zs, *blocks)


def homes(z, rows):
    row, place = iota((rows, rows), 0), iota((rows, rows), 1)
    quarter = rows // 4
    first, last = row < quarter, row >= 3 * quarter
    inside = jnp.where(first, row, jnp.where(last, row - 3 * quarter, row - quarter))
    zn = jnp.where(first | last, 4, 8)
    source = inside // (zn * CAPACITY)
    zi = (inside // CAPACITY) % zn
    near = jnp.where(zi < 4, -1 - 4 * zi, 17 - 4 * zi)
    offset = jnp.where(first, -4 * zi, jnp.where(last, 2 - 4 * zi, near))
    zed = (z + offset + 32) % 16
    home = ((zed // 8) * 64 + source * 8 + zed % 8) * CAPACITY + inside % CAPACITY
    return (home == place).astype(BF)


def rows_kernel(zs_ref, a_ref, b_ref, c_ref, w_ref, p_ref, *refs):
    d_refs, s_ref, (gu, dn, rows, sems) = refs[:4], refs[4], refs[5:]
    hid = dn.shape[1]
    count, width = rows.shape
    features = (width - LANES) // 2
    quarter = count // 4
    me = zs_ref[2]
    places = [(me + offset) % 4 for offset in (0, 3, 1, 2)]
    pairs = [
        (a_ref, rows.at[pl.ds(0, quarter)]),
        (b_ref, rows.at[pl.ds(quarter, 2 * quarter)]),
        (c_ref, rows.at[pl.ds(3 * quarter, quarter)]),
    ]
    for q, place in enumerate(places):
        pairs.append((w_ref.at[place, pl.ds(0, 2 * hid)], gu.at[q]))
        pairs.append((w_ref.at[place, pl.ds(2 * hid, hid)], dn.at[q]))
    copies = [pltpu.make_async_copy(s, t, sems.at[i]) for i, (s, t) in enumerate(pairs)]
    for copy in copies:
        copy.start()
    for copy in copies[:3]:
        copy.wait()
    home = homes(zs_ref[0] * 8 + zs_ref[1], count)
    coef = rows[:, 2 * features :].astype(F32).T[0:1, :]
    score = None
    for q in range(4):
        copies[3 + 2 * q].wait()
        copies[4 + 2 * q].wait()
        pre = dot(gu[q], rows[:, :features], 1, 1)
        back = dot(dn[q], rows[:, features : 2 * features], 1, 1)
        gate_pre, up_pre = pre[:hid], pre[hid:]
        sigma = jax.nn.sigmoid(gate_pre)
        active = gate_pre * sigma
        hidden = active * up_pre
        part = jnp.sum(hidden.astype(BF).astype(F32) * back, axis=0, keepdims=True)
        score = part if score is None else score + part
        d_hidden = coef * back
        d_gate = d_hidden * up_pre * sigma * (1.0 + gate_pre * (1.0 - sigma))
        d_refs[q][0:hid, :] = d_gate.astype(BF)
        d_refs[q][hid:, :] = (d_hidden * active).astype(BF)
        s_ref[q] = (coef * hidden).astype(BF)
    moved = [dot(d[...], home, 1, 0).astype(BF) for d in d_refs]
    tile = 512
    for j in range(0, features, tile):
        total = None
        for q in range(4):
            part = dot(moved[q], gu[q, :, j : j + tile], 0, 0)
            total = part if total is None else total + part
        p_ref[:, j : j + tile] = total.astype(BF)
    score = dot(jnp.broadcast_to(score, (LANES, count)).astype(BF), home, 1, 0)
    p_ref[:, features:] = score.T.astype(BF)


def rows_call(zs, chunks, weights):
    count = sum(c.shape[0] for c in chunks)
    width = chunks[0].shape[1]
    n, hid, features = weights.shape[0], weights.shape[1] // 3, weights.shape[2]
    return pl.pallas_call(
        rows_kernel,
        out_shape=[
            jax.ShapeDtypeStruct((count, features + LANES), BF),
            *[jax.ShapeDtypeStruct((2 * hid, count), BF)] * n,
            jax.ShapeDtypeStruct((n, hid, count), BF),
        ],
        in_specs=[pl.BlockSpec(memory_space=pltpu.SMEM)] + [pl.BlockSpec(memory_space=pl.ANY)] * 4,
        out_specs=[vmem()] * (n + 2),
        scratch_shapes=[
            pltpu.VMEM((n, 2 * hid, features), BF),
            pltpu.VMEM((n, hid, features), BF),
            pltpu.VMEM((count, width), BF),
            pltpu.SemaphoreType.DMA((3 + 2 * n,)),
        ],
        compiler_params=pltpu.CompilerParams(vmem_limit_bytes=56 * MIB),
        cost_estimate=pl.CostEstimate(
            flops=2 * count * features * hid * n * 5,
            bytes_accessed=2 * features * hid * 12 + 6 * count * features,
            transcendentals=count * hid * n,
        ),
        name="rows",
    )(zs, *chunks, weights)


def down_kernel(s_ref, a_ref, b_ref, c_ref, own_ref, left_ref, right_ref, two_ref, rows):
    quarter = a_ref.shape[0]
    rows[0:quarter, :] = a_ref[...]
    rows[quarter : 3 * quarter, :] = b_ref[...]
    rows[3 * quarter :, :] = c_ref[...]
    grads = rows[...]
    for q, out in enumerate((own_ref, left_ref, right_ref, two_ref)):
        out[...] = dot(s_ref[q], grads, 1, 0).astype(out.dtype)


def down_call(scaled, chunks, features):
    tile = 512
    n, hid, count = scaled.shape
    first = features // tile
    tiled = [pl.BlockSpec((c.shape[0], tile), lambda j: (0, first + j)) for c in chunks]
    return pl.pallas_call(
        down_kernel,
        grid=(features // tile,),
        out_shape=[jax.ShapeDtypeStruct((hid, features), F32)]
        + [jax.ShapeDtypeStruct((hid, features), BF)] * 3,
        in_specs=[pl.BlockSpec(scaled.shape, lambda j: (0, 0, 0))] + tiled,
        out_specs=[pl.BlockSpec((hid, tile), lambda j: (0, j))] * 4,
        scratch_shapes=[pltpu.VMEM((count, tile), BF)],
        compiler_params=pltpu.CompilerParams(vmem_limit_bytes=24 * MIB),
        cost_estimate=pl.CostEstimate(
            flops=2 * n * count * features * hid,
            bytes_accessed=2 * features * (count + 5 * hid),
            transcendentals=0,
        ),
        name="down_parts",
    )(scaled, *chunks)


def weights_kernel(zs_ref, *refs):
    d_refs, x_refs, (gate_ref, up_ref) = refs[:4], refs[4:8], refs[8:]
    hid = gate_ref.shape[0]
    total = sum(dot(d[...], x[0], 1, 0) for d, x in zip(d_refs, x_refs)).astype(BF)
    gate_ref[...] = total[:hid]
    up_ref[...] = total[hid:]


def weights_call(zs, ds, xs):
    tile = 512
    n, count, features = xs.shape
    hid = ds[0].shape[0] // 2
    whole = [pl.BlockSpec(d.shape, lambda j, zs: (0, 0)) for d in ds]
    tiled = [
        pl.BlockSpec((1, count, tile), lambda j, zs, at=at: ((zs[2] + at) % 4, 0, j))
        for at in (0, 3, 1, 2)
    ]
    return pl.pallas_call(
        weights_kernel,
        grid_spec=pltpu.PrefetchScalarGridSpec(
            num_scalar_prefetch=1,
            grid=(features // tile,),
            in_specs=whole + tiled,
            out_specs=[pl.BlockSpec((hid, tile), lambda j, zs: (0, j))] * 2,
        ),
        out_shape=[jax.ShapeDtypeStruct((hid, features), BF)] * 2,
        compiler_params=pltpu.CompilerParams(vmem_limit_bytes=24 * MIB),
        cost_estimate=pl.CostEstimate(
            flops=4 * n * count * features * hid,
            bytes_accessed=2 * features * (n * count + 2 * hid),
            transcendentals=0,
        ),
        name="weight_grads",
    )(zs, *ds, *[xs] * n)


def home_kernel(code_ref, home_ref, grad_ref, score_ref):
    top, rows = code_ref.shape
    places = home_ref.shape[0]
    features = grad_ref.shape[1]
    wanted = (iota((places, rows), 0) + 1).astype(F32)
    hits = [jnp.where(wanted == code_ref[k : k + 1, :], 1.0, 0.0) for k in range(top)]
    score = home_ref[:, features : features + 1].astype(F32)
    score_ref[...] = jnp.concatenate(
        [jnp.sum(hit * score, axis=0, keepdims=True) for hit in hits], axis=0
    ).astype(BF)
    pick = sum(hits).astype(BF)
    grad_ref[...] = dot(pick, home_ref[:, :features], 0, 0).astype(BF)


def home_call(code, home, features):
    return pl.pallas_call(
        home_kernel,
        out_shape=[
            jax.ShapeDtypeStruct((code.shape[1], features), BF),
            jax.ShapeDtypeStruct(code.shape, BF),
        ],
        in_specs=[vmem()] * 2,
        out_specs=[vmem()] * 2,
        name="home",
    )(code, home)


def local(tokens, out_grad, expert_ids, keep_flags, route_weights, gate_w, up_w, down_w):
    nz, n = lax.axis_size(Z), lax.axis_size("x")
    step, features = tokens.shape
    zs = jnp.stack([lax.axis_index(a) for a in ("zh", "zl", "x")]).astype(jnp.int32)
    half = gate_w.shape[1] // 2

    joined = jnp.concatenate([gate_w[0], up_w[0], down_w[0]], axis=0)
    weights = lax.all_gather(joined, "x", axis=0)
    own, code = payload_call(tokens, out_grad, expert_ids.T, keep_flags.T, route_weights.T)

    far = [shift(own, s, Z, nz) for s in (4, 8, 12)]
    chunk = jnp.concatenate([own, *far], axis=0)
    left, right = shift(chunk, 1, Z, nz), shift(chunk, -1, Z, nz)

    def exchange(packed):
        rows, width = packed.shape
        return lax.all_to_all(
            packed.reshape(8, rows // 8, width), YC, split_axis=0, concat_axis=0, tiled=True
        ).reshape(rows, width)

    rows_a = exchange(pack_call(zs, [chunk], step))
    rest_a = shift(right[: 2 * step], -1, Z, nz)
    rest_b = shift(left[step : 3 * step], 1, Z, nz)
    packed_b = pack_call(zs, [left, right], step)
    rest_a, rest_b, _ = lax.optimization_barrier((rest_a, rest_b, packed_b))
    rows_b = exchange(packed_b)
    rows_c = exchange(pack_call(zs, [rest_a, rest_b], step))

    chunks = [rows_a, rows_b, rows_c]
    x = lax.all_gather(jnp.concatenate([c[:, :features] for c in chunks], axis=0), "x", axis=0)

    back, d_own, d_left, d_right, d_two, scaled = rows_call(zs, chunks, weights)
    home = lax.all_to_all(
        back.reshape(-1, CAPACITY, back.shape[1]), PLACE, split_axis=0, concat_axis=0, tiled=True
    ).reshape(back.shape)
    ds = [d_own, shift(d_right, 1, "x", n), shift(d_left, -1, "x", n), shift(d_two, 2, "x", n)]
    grad_gate, grad_up = weights_call(zs, ds, x)

    p_own, p_left, p_right, p_two = down_call(scaled, chunks, features)
    via_a = shift(p_two[:half], 1, "x", n)
    via_b = shift(p_two[half:], -1, "x", n)
    left_low = shift(p_right[half:], 1, "x", n)
    right_top = shift(p_left[:half], -1, "x", n)
    left_top = shift((p_right[:half].astype(F32) + via_a.astype(F32)).astype(BF), 1, "x", n)
    right_low = shift((p_left[half:].astype(F32) + via_b.astype(F32)).astype(BF), -1, "x", n)
    grad_down = jnp.concatenate(
        [
            (p_own[:half] + left_top.astype(F32) + right_top.astype(F32)).astype(BF),
            (p_own[half:] + left_low.astype(F32) + right_low.astype(F32)).astype(BF),
        ],
        axis=0,
    )

    token_grad, slot_score = home_call(code, home, features)
    return (token_grad, slot_score.T, grad_gate[None], grad_up[None], grad_down[None])


def solution(mesh):
    fine = Mesh(mesh.devices.reshape(2, 4, 2, 8, 4), ("zh", "y", "c", "zl", "x"))
    by_row = P(("zh", "y", "c", "zl", "x"), None)
    by_expert = P(PLACE, "x", None)
    return jax.shard_map(
        local,
        mesh=fine,
        in_specs=(by_row,) * 5 + (by_expert,) * 3,
        out_specs=(by_row,) * 2 + (by_expert,) * 3,
        check_vma=False,
    )
```

```python
import jax
import jax.numpy as jnp
from jax import lax
from jax.experimental import pallas as pl
from jax.experimental.pallas import tpu as pltpu
from jax.sharding import Mesh, PartitionSpec as P

BF = jnp.bfloat16
F32 = jnp.float32
LANES = 128
CAPACITY = 2
MIB = 1024 * 1024
FAR = ("zh", "zq")
Z = ("zh", "zq", "zr")
YC = ("y", "c")
PLACE = ("zh", "y", "c", "zq", "zr")


def dot(a, b, da, db):
    return lax.dot_general(a, b, (((da,), (db,)), ((), ())), preferred_element_type=F32)


def iota(shape, axis):
    return lax.broadcasted_iota(jnp.int32, shape, axis)


def shift(block, step, axes, n):
    return lax.ppermute(block, axes, [(i, (i + step) % n) for i in range(n)])


def vmem():
    return pl.BlockSpec(memory_space=pltpu.VMEM)


def payload_kernel(tok_ref, grad_ref, ids_ref, keep_ref, weight_ref, out_ref, code_ref):
    features = tok_ref.shape[1]
    top, rows = ids_ref.shape
    experts = LANES
    ids, kept = ids_ref[...], keep_ref[...] > 0
    names = iota((experts, rows), 0)
    named = [names == ids[k : k + 1, :] for k in range(top)]
    tally = sum(jnp.where(named[k] & kept[k : k + 1, :], 1.0, 0.0) for k in range(top))
    before = (iota((rows, rows), 0) < iota((rows, rows), 1)).astype(BF)
    earlier = dot(tally.astype(BF), before, 1, 0)
    position = jnp.concatenate(
        [jnp.sum(jnp.where(named[k], earlier, 0.0), axis=0, keepdims=True) for k in range(top)],
        axis=0,
    )
    code = jnp.where(kept, ids.astype(F32) * CAPACITY + position + 1.0, 0.0)
    code_ref[...] = code
    spread = (iota((rows, LANES), 0) == iota((rows, LANES), 1)).astype(BF)
    both = jnp.concatenate([code.astype(BF), weight_ref[...]], axis=0)
    out_ref[:, :features] = tok_ref[...]
    out_ref[:, features : 2 * features] = grad_ref[...]
    out_ref[:, 2 * features :] = dot(both, spread, 1, 0).astype(BF)


def payload_call(tokens, out_grad, ids, keep, weights):
    rows, features = tokens.shape
    return pl.pallas_call(
        payload_kernel,
        out_shape=[
            jax.ShapeDtypeStruct((rows, 2 * features + LANES), BF),
            jax.ShapeDtypeStruct(ids.shape, F32),
        ],
        in_specs=[vmem()] * 5,
        out_specs=[vmem()] * 2,
        name="payload",
    )(tokens, out_grad, ids, keep, weights)


def pack_kernel(step, zs_ref, *refs):
    blocks, out_ref = refs[:-1], refs[-1]
    count = sum(b.shape[0] for b in blocks)
    zn = count // step
    rows, width = out_ref.shape
    features = (width - LANES) // 2
    half = step // 2
    codes = jnp.zeros((half, count), F32)
    weights = jnp.zeros((half, count), F32)
    at = 0
    for block in blocks:
        for first in range(0, block.shape[0], step):
            place = (iota((LANES, count), 0) + at == iota((LANES, count), 1)) & (
                iota((LANES, count), 0) < step
            )
            both = dot(
                block[first : first + step, 2 * features :], place.astype(BF), 1, 0
            )
            codes = codes + both[:half]
            weights = weights + both[half:]
            at += step
    zh, zl = zs_ref[0], zs_ref[1]
    row, col = iota((rows, count), 0), iota((rows, count), 1)
    dest = row // (zn * CAPACITY)
    wanted = ((zh * 64 + dest * 8 + zl) * CAPACITY + row % CAPACITY + 1).astype(F32)
    wanted = jnp.where((row // CAPACITY) % zn == col // step, wanted, -1.0)
    pick = jnp.zeros((rows, count), F32)
    coef = jnp.zeros((rows, count), F32)
    for k in range(half):
        hit = wanted == codes[k : k + 1, :]
        pick = pick + jnp.where(hit, 1.0, 0.0)
        coef = coef + jnp.where(hit, weights[k : k + 1, :], 0.0)
    pick = pick.astype(BF)
    tile = 1024
    for j in range(0, 2 * features, tile):
        total, at = None, 0
        for block in blocks:
            size = block.shape[0]
            part = dot(pick[:, at : at + size], block[:, j : j + tile], 1, 0)
            total = part if total is None else total + part
            at += size
        out_ref[:, j : j + tile] = total.astype(BF)
    out_ref[:, 2 * features :] = jnp.broadcast_to(
        jnp.sum(coef, axis=1, keepdims=True), (rows, LANES)
    ).astype(BF)


def pack_call(zs, blocks, step):
    count, width = sum(b.shape[0] for b in blocks), blocks[0].shape[1]
    rows = 8 * (count // step) * CAPACITY

    def body(*refs):
        pack_kernel(step, *refs)

    return pl.pallas_call(
        body,
        out_shape=jax.ShapeDtypeStruct((rows, width), BF),
        in_specs=[pl.BlockSpec(memory_space=pltpu.SMEM)] + [vmem()] * len(blocks),
        out_specs=vmem(),
        name="pack",
    )(zs, *blocks)


def homes(z, rows):
    row, place = iota((rows, rows), 0), iota((rows, rows), 1)
    quarter = rows // 4
    first, last = row < quarter, row >= 3 * quarter
    inside = jnp.where(first, row, jnp.where(last, row - 3 * quarter, row - quarter))
    zn = jnp.where(first | last, 4, 8)
    source = inside // (zn * CAPACITY)
    zi = (inside // CAPACITY) % zn
    turn = jnp.where(first, 0, jnp.where(last, 2, jnp.where(zi < 4, 3, 1)))
    zed = 4 * (zi % 4) + (z + turn) % 4
    home = ((zed // 8) * 64 + source * 8 + zed % 8) * CAPACITY + inside % CAPACITY
    return (home == place).astype(BF)


def rows_kernel(zs_ref, a_ref, b_ref, c_ref, w_ref, p_ref, *refs):
    d_refs, s_ref, (gu, dn, rows, d_all, sems) = refs[:4], refs[4], refs[5:]
    hid = dn.shape[1]
    count, width = rows.shape
    features = (width - LANES) // 2
    quarter = count // 4
    me = zs_ref[2]
    places = [(me + offset) % 4 for offset in (0, 3, 1, 2)]
    pairs = [
        (a_ref, rows.at[pl.ds(0, quarter)]),
        (b_ref, rows.at[pl.ds(quarter, 2 * quarter)]),
        (c_ref, rows.at[pl.ds(3 * quarter, quarter)]),
    ]
    for q, place in enumerate(places):
        pairs.append((w_ref.at[place, pl.ds(0, 2 * hid)], gu.at[pl.ds(q * 2 * hid, 2 * hid)]))
        pairs.append((w_ref.at[place, pl.ds(2 * hid, hid)], dn.at[q]))
    copies = [pltpu.make_async_copy(s, t, sems.at[i]) for i, (s, t) in enumerate(pairs)]
    for copy in copies:
        copy.start()
    for copy in copies[:3]:
        copy.wait()
    home = homes(zs_ref[0] * 8 + zs_ref[1], count)
    coef = rows[:, 2 * features :].astype(F32).T[0:1, :]
    score = None
    for q in range(4):
        copies[3 + 2 * q].wait()
        copies[4 + 2 * q].wait()
        first = q * 2 * hid
        pre = dot(gu[first : first + 2 * hid, :], rows[:, :features], 1, 1)
        back = dot(dn[q], rows[:, features : 2 * features], 1, 1)
        gate_pre, up_pre = pre[:hid], pre[hid:]
        sigma = jax.nn.sigmoid(gate_pre)
        active = gate_pre * sigma
        hidden = active * up_pre
        part = jnp.sum(hidden.astype(BF).astype(F32) * back, axis=0, keepdims=True)
        score = part if score is None else score + part
        d_hidden = coef * back
        d_gate = d_hidden * up_pre * sigma * (1.0 + gate_pre * (1.0 - sigma))
        d_all[first : first + hid, :] = d_gate.astype(BF)
        d_all[first + hid : first + 2 * hid, :] = (d_hidden * active).astype(BF)
        d_refs[q][...] = d_all[first : first + 2 * hid, :]
        s_ref[q] = (coef * hidden).astype(BF)
    moved = dot(d_all[...], home, 1, 0).astype(BF)
    tile = 512
    for j in range(0, features, tile):
        p_ref[:, j : j + tile] = dot(moved, gu[:, j : j + tile], 0, 0).astype(BF)
    score = dot(jnp.broadcast_to(score, (LANES, count)).astype(BF), home, 1, 0)
    p_ref[:, features:] = score.T.astype(BF)


def rows_call(zs, chunks, weights):
    count = sum(c.shape[0] for c in chunks)
    width = chunks[0].shape[1]
    n, hid, features = weights.shape[0], weights.shape[1] // 3, weights.shape[2]
    return pl.pallas_call(
        rows_kernel,
        out_shape=[
            jax.ShapeDtypeStruct((count, features + LANES), BF),
            *[jax.ShapeDtypeStruct((2 * hid, count), BF)] * n,
            jax.ShapeDtypeStruct((n, hid, count), BF),
        ],
        in_specs=[pl.BlockSpec(memory_space=pltpu.SMEM)] + [pl.BlockSpec(memory_space=pl.ANY)] * 4,
        out_specs=[vmem()] * (n + 2),
        scratch_shapes=[
            pltpu.VMEM((n * 2 * hid, features), BF),
            pltpu.VMEM((n, hid, features), BF),
            pltpu.VMEM((count, width), BF),
            pltpu.VMEM((n * 2 * hid, count), BF),
            pltpu.SemaphoreType.DMA((3 + 2 * n,)),
        ],
        compiler_params=pltpu.CompilerParams(vmem_limit_bytes=56 * MIB),
        cost_estimate=pl.CostEstimate(
            flops=2 * count * features * hid * n * 5,
            bytes_accessed=2 * features * hid * 12 + 6 * count * features,
            transcendentals=count * hid * n,
        ),
        name="rows",
    )(zs, *chunks, weights)


def down_kernel(s_ref, a_ref, b_ref, c_ref, own_ref, go_ref, come_ref, right_ref, left_ref, rows):
    quarter = a_ref.shape[0]
    rows[0:quarter, :] = a_ref[...]
    rows[quarter : 3 * quarter, :] = b_ref[...]
    rows[3 * quarter :, :] = c_ref[...]
    grads = rows[...]
    half = right_ref.shape[0]
    own_ref[...] = dot(s_ref[0], grads, 1, 0)
    left = dot(s_ref[1], grads, 1, 0).astype(BF)
    right = dot(s_ref[2], grads, 1, 0).astype(BF)
    two = dot(s_ref[3], grads, 1, 0).astype(BF)
    go_ref[:half, :] = two[:half]
    go_ref[half:, :] = right[half:]
    come_ref[:half, :] = left[:half]
    come_ref[half:, :] = two[half:]
    right_ref[...] = right[:half]
    left_ref[...] = left[half:]


def down_call(scaled, chunks, features):
    tile = 512
    n, hid, count = scaled.shape
    first = features // tile
    tiled = [pl.BlockSpec((c.shape[0], tile), lambda j: (0, first + j)) for c in chunks]
    return pl.pallas_call(
        down_kernel,
        grid=(features // tile,),
        out_shape=[jax.ShapeDtypeStruct((hid, features), F32)]
        + [jax.ShapeDtypeStruct((hid, features), BF)] * 2
        + [jax.ShapeDtypeStruct((hid // 2, features), BF)] * 2,
        in_specs=[pl.BlockSpec(scaled.shape, lambda j: (0, 0, 0))] + tiled,
        out_specs=[pl.BlockSpec((hid, tile), lambda j: (0, j))] * 3
        + [pl.BlockSpec((hid // 2, tile), lambda j: (0, j))] * 2,
        scratch_shapes=[pltpu.VMEM((count, tile), BF)],
        compiler_params=pltpu.CompilerParams(vmem_limit_bytes=24 * MIB),
        cost_estimate=pl.CostEstimate(
            flops=2 * n * count * features * hid,
            bytes_accessed=2 * features * (count + 5 * hid),
            transcendentals=0,
        ),
        name="down_parts",
    )(scaled, *chunks)


def weights_kernel(zs_ref, *refs):
    d_refs, x_refs, (gate_ref, up_ref) = refs[:4], refs[4:8], refs[8:]
    hid = gate_ref.shape[0]
    total = sum(dot(d[...], x[0], 1, 0) for d, x in zip(d_refs, x_refs)).astype(BF)
    gate_ref[...] = total[:hid]
    up_ref[...] = total[hid:]


def weights_call(zs, ds, xs):
    tile = 512
    n, count, features = xs.shape
    hid = ds[0].shape[0] // 2
    whole = [pl.BlockSpec(d.shape, lambda j, zs: (0, 0)) for d in ds]
    tiled = [
        pl.BlockSpec((1, count, tile), lambda j, zs, at=at: ((zs[2] + at) % 4, 0, j))
        for at in (0, 3, 1, 2)
    ]
    return pl.pallas_call(
        weights_kernel,
        grid_spec=pltpu.PrefetchScalarGridSpec(
            num_scalar_prefetch=1,
            grid=(features // tile,),
            in_specs=whole + tiled,
            out_specs=[pl.BlockSpec((hid, tile), lambda j, zs: (0, j))] * 2,
        ),
        out_shape=[jax.ShapeDtypeStruct((hid, features), BF)] * 2,
        compiler_params=pltpu.CompilerParams(vmem_limit_bytes=24 * MIB),
        cost_estimate=pl.CostEstimate(
            flops=4 * n * count * features * hid,
            bytes_accessed=2 * features * (n * count + 2 * hid),
            transcendentals=0,
        ),
        name="weight_grads",
    )(zs, *ds, *[xs] * n)


def home_kernel(code_ref, home_ref, grad_ref, score_ref):
    top, rows = code_ref.shape
    places = home_ref.shape[0]
    features = grad_ref.shape[1]
    wanted = (iota((places, rows), 0) + 1).astype(F32)
    hits = [jnp.where(wanted == code_ref[k : k + 1, :], 1.0, 0.0) for k in range(top)]
    score = home_ref[:, features : features + 1].astype(F32)
    score_ref[...] = jnp.concatenate(
        [jnp.sum(hit * score, axis=0, keepdims=True) for hit in hits], axis=0
    ).astype(BF)
    pick = sum(hits).astype(BF)
    grad_ref[...] = dot(pick, home_ref[:, :features], 0, 0).astype(BF)


def home_call(code, home, features):
    return pl.pallas_call(
        home_kernel,
        out_shape=[
            jax.ShapeDtypeStruct((code.shape[1], features), BF),
            jax.ShapeDtypeStruct(code.shape, BF),
        ],
        in_specs=[vmem()] * 2,
        out_specs=[vmem()] * 2,
        name="home",
    )(code, home)


def local(tokens, out_grad, expert_ids, keep_flags, route_weights, gate_w, up_w, down_w):
    nz, n = lax.axis_size(Z), lax.axis_size("x")
    step, features = tokens.shape
    zs = jnp.stack([lax.axis_index(a) for a in ("zh", ("zq", "zr"), "x")]).astype(jnp.int32)
    half = gate_w.shape[1] // 2

    joined = jnp.concatenate([gate_w[0], up_w[0], down_w[0]], axis=0)
    weights = lax.all_gather(joined, "x", axis=0)
    own, code = payload_call(tokens, out_grad, expert_ids.T, keep_flags.T, route_weights.T)

    chunk = lax.all_gather(own, FAR, axis=0, tiled=True)
    left, right = shift(chunk, 1, Z, nz), shift(chunk, -1, Z, nz)

    def exchange(packed):
        rows, width = packed.shape
        return lax.all_to_all(
            packed.reshape(8, rows // 8, width), YC, split_axis=0, concat_axis=0, tiled=True
        ).reshape(rows, width)

    rows_a = exchange(pack_call(zs, [chunk], step))
    rest_a = shift(right[: 2 * step], -1, Z, nz)
    rest_b = shift(left[2 * step :], 1, Z, nz)
    packed_b = pack_call(zs, [left, right], step)
    rest_a, rest_b, _ = lax.optimization_barrier((rest_a, rest_b, packed_b))
    packed_b, rows_a = lax.optimization_barrier((packed_b, rows_a))
    rows_b = exchange(packed_b)
    packed_c = pack_call(zs, [rest_a, rest_b], step)
    packed_c, rows_b = lax.optimization_barrier((packed_c, rows_b))
    rows_c = exchange(packed_c)

    chunks = [rows_a, rows_b, rows_c]
    x = lax.all_gather(jnp.concatenate([c[:, :features] for c in chunks], axis=0), "x", axis=0)

    back, d_own, d_left, d_right, d_two, scaled = rows_call(zs, chunks, weights)
    home = lax.all_to_all(
        back.reshape(-1, CAPACITY, back.shape[1]), PLACE, split_axis=0, concat_axis=0, tiled=True
    ).reshape(back.shape)
    ds = [d_own, shift(d_right, 1, "x", n), shift(d_left, -1, "x", n), shift(d_two, 2, "x", n)]
    grad_gate, grad_up = weights_call(zs, ds, x)

    p_own, p_go, p_come, p_right, p_left = down_call(scaled, chunks, features)
    from_left, from_right = shift(p_go, 1, "x", n), shift(p_come, -1, "x", n)
    p_right = (p_right.astype(F32) + from_left[:half].astype(F32)).astype(BF)
    p_left = (p_left.astype(F32) + from_right[half:].astype(F32)).astype(BF)
    left_top, right_low = shift(p_right, 1, "x", n), shift(p_left, -1, "x", n)
    grad_down = jnp.concatenate(
        [
            p_own[:half] + left_top.astype(F32) + from_right[:half].astype(F32),
            p_own[half:] + from_left[half:].astype(F32) + right_low.astype(F32),
        ],
        axis=0,
    ).astype(BF)

    token_grad, slot_score = home_call(code, home, features)
    return (token_grad, slot_score.T, grad_gate[None], grad_up[None], grad_down[None])


def solution(mesh):
    fine = Mesh(mesh.devices.reshape(2, 4, 2, 2, 4, 4), (*PLACE, "x"))
    by_row = P((*PLACE, "x"), None)
    by_expert = P(PLACE, "x", None)
    return jax.shard_map(
        local,
        mesh=fine,
        in_specs=(by_row,) * 5 + (by_expert,) * 3,
        out_specs=(by_row,) * 2 + (by_expert,) * 3,
        check_vma=False,
    )
```

```python
import jax
import jax.numpy as jnp
from jax import lax
from jax.experimental import pallas as pl
from jax.experimental.pallas import tpu as pltpu
from jax.sharding import Mesh, PartitionSpec as P

BF = jnp.bfloat16
F32 = jnp.float32
LANES = 128
CAPACITY = 2
MIB = 1024 * 1024
FAR = ("zh", "zq")
Z = ("zh", "zq", "zr")
YC = ("y", "c")
PLACE = ("zh", "y", "c", "zq", "zr")


def dot(a, b, da, db):
    return lax.dot_general(a, b, (((da,), (db,)), ((), ())), preferred_element_type=F32)


def iota(shape, axis):
    return lax.broadcasted_iota(jnp.int32, shape, axis)


def shift(block, step, axes, n):
    return lax.ppermute(block, axes, [(i, (i + step) % n) for i in range(n)])


def vmem():
    return pl.BlockSpec(memory_space=pltpu.VMEM)


def payload_kernel(tok_ref, grad_ref, ids_ref, keep_ref, weight_ref, out_ref, code_ref):
    features = tok_ref.shape[1]
    top, rows = ids_ref.shape
    experts = LANES
    ids, kept = ids_ref[...], keep_ref[...] > 0
    names = iota((experts, rows), 0)
    named = [names == ids[k : k + 1, :] for k in range(top)]
    tally = sum(jnp.where(named[k] & kept[k : k + 1, :], 1.0, 0.0) for k in range(top))
    before = (iota((rows, rows), 0) < iota((rows, rows), 1)).astype(BF)
    earlier = dot(tally.astype(BF), before, 1, 0)
    position = jnp.concatenate(
        [jnp.sum(jnp.where(named[k], earlier, 0.0), axis=0, keepdims=True) for k in range(top)],
        axis=0,
    )
    code = jnp.where(kept, ids.astype(F32) * CAPACITY + position + 1.0, 0.0)
    code_ref[...] = code
    spread = (iota((rows, LANES), 0) == iota((rows, LANES), 1)).astype(BF)
    both = jnp.concatenate([code.astype(BF), weight_ref[...]], axis=0)
    out_ref[:, :features] = tok_ref[...]
    out_ref[:, features : 2 * features] = grad_ref[...]
    out_ref[:, 2 * features :] = dot(both, spread, 1, 0).astype(BF)


def payload_call(tokens, out_grad, ids, keep, weights):
    rows, features = tokens.shape
    return pl.pallas_call(
        payload_kernel,
        out_shape=[
            jax.ShapeDtypeStruct((rows, 2 * features + LANES), BF),
            jax.ShapeDtypeStruct(ids.shape, F32),
        ],
        in_specs=[vmem()] * 5,
        out_specs=[vmem()] * 2,
        name="payload",
    )(tokens, out_grad, ids, keep, weights)


def pack_kernel(step, zs_ref, *refs):
    blocks, out_ref = refs[:-1], refs[-1]
    count = sum(b.shape[0] for b in blocks)
    zn = count // step
    rows, width = out_ref.shape
    features = (width - LANES) // 2
    half = step // 2
    codes = jnp.zeros((half, count), F32)
    weights = jnp.zeros((half, count), F32)
    at = 0
    for block in blocks:
        for first in range(0, block.shape[0], step):
            place = (iota((LANES, count), 0) + at == iota((LANES, count), 1)) & (
                iota((LANES, count), 0) < step
            )
            both = dot(
                block[first : first + step, 2 * features :], place.astype(BF), 1, 0
            )
            codes = codes + both[:half]
            weights = weights + both[half:]
            at += step
    zh, zl = zs_ref[0], zs_ref[1]
    row, col = iota((rows, count), 0), iota((rows, count), 1)
    dest = row // (zn * CAPACITY)
    wanted = ((zh * 64 + dest * 8 + zl) * CAPACITY + row % CAPACITY + 1).astype(F32)
    wanted = jnp.where((row // CAPACITY) % zn == col // step, wanted, -1.0)
    pick = jnp.zeros((rows, count), F32)
    coef = jnp.zeros((rows, count), F32)
    for k in range(half):
        hit = wanted == codes[k : k + 1, :]
        pick = pick + jnp.where(hit, 1.0, 0.0)
        coef = coef + jnp.where(hit, weights[k : k + 1, :], 0.0)
    pick = pick.astype(BF)
    tile = 1024
    for j in range(0, 2 * features, tile):
        total, at = None, 0
        for block in blocks:
            size = block.shape[0]
            part = dot(pick[:, at : at + size], block[:, j : j + tile], 1, 0)
            total = part if total is None else total + part
            at += size
        out_ref[:, j : j + tile] = total.astype(BF)
    out_ref[:, 2 * features :] = jnp.broadcast_to(
        jnp.sum(coef, axis=1, keepdims=True), (rows, LANES)
    ).astype(BF)


def pack_call(zs, blocks, step):
    count, width = sum(b.shape[0] for b in blocks), blocks[0].shape[1]
    rows = 8 * (count // step) * CAPACITY

    def body(*refs):
        pack_kernel(step, *refs)

    return pl.pallas_call(
        body,
        out_shape=jax.ShapeDtypeStruct((rows, width), BF),
        in_specs=[pl.BlockSpec(memory_space=pltpu.SMEM)] + [vmem()] * len(blocks),
        out_specs=vmem(),
        name="pack",
    )(zs, *blocks)


def homes(z, rows):
    row, place = iota((rows, rows), 0), iota((rows, rows), 1)
    quarter = rows // 4
    second, last = row >= 2 * quarter, row >= 3 * quarter
    inside = jnp.where(last, row - 3 * quarter, jnp.where(second, row - 2 * quarter, row))
    zn = jnp.where(second, 4, 8)
    source = inside // (zn * CAPACITY)
    zi = (inside // CAPACITY) % zn
    turn = jnp.where(last, 2, jnp.where(second, 0, jnp.where(zi < 4, 3, 1)))
    zed = 4 * (zi % 4) + (z + turn) % 4
    home = ((zed // 8) * 64 + source * 8 + zed % 8) * CAPACITY + inside % CAPACITY
    return (home == place).astype(BF)


def rows_kernel(zs_ref, b_ref, a_ref, c_ref, w_ref, p_ref, *refs):
    d_refs, s_ref, (gu, dn, rows, d_all, sems) = refs[:4], refs[4], refs[5:]
    hid = dn.shape[1]
    count, width = rows.shape
    features = (width - LANES) // 2
    quarter = count // 4
    me = zs_ref[2]
    places = [(me + offset) % 4 for offset in (0, 3, 1, 2)]
    pairs = [
        (b_ref, rows.at[pl.ds(0, 2 * quarter)]),
        (a_ref, rows.at[pl.ds(2 * quarter, quarter)]),
        (c_ref, rows.at[pl.ds(3 * quarter, quarter)]),
    ]
    for q, place in enumerate(places):
        pairs.append((w_ref.at[place, pl.ds(0, 2 * hid)], gu.at[pl.ds(q * 2 * hid, 2 * hid)]))
        pairs.append((w_ref.at[place, pl.ds(2 * hid, hid)], dn.at[q]))
    copies = [pltpu.make_async_copy(s, t, sems.at[i]) for i, (s, t) in enumerate(pairs)]
    for copy in copies:
        copy.start()
    for copy in copies[:3]:
        copy.wait()
    home = homes(zs_ref[0] * 8 + zs_ref[1], count)
    coef = rows[:, 2 * features :].astype(F32).T[0:1, :]
    score = None
    for q in range(4):
        copies[3 + 2 * q].wait()
        copies[4 + 2 * q].wait()
        first = q * 2 * hid
        pre = dot(gu[first : first + 2 * hid, :], rows[:, :features], 1, 1)
        back = dot(dn[q], rows[:, features : 2 * features], 1, 1)
        gate_pre, up_pre = pre[:hid], pre[hid:]
        sigma = jax.nn.sigmoid(gate_pre)
        active = gate_pre * sigma
        hidden = active * up_pre
        part = jnp.sum(hidden.astype(BF).astype(F32) * back, axis=0, keepdims=True)
        score = part if score is None else score + part
        d_hidden = coef * back
        d_gate = d_hidden * up_pre * sigma * (1.0 + gate_pre * (1.0 - sigma))
        d_all[first : first + hid, :] = d_gate.astype(BF)
        d_all[first + hid : first + 2 * hid, :] = (d_hidden * active).astype(BF)
        d_refs[q][...] = d_all[first : first + 2 * hid, :]
        s_ref[q] = (coef * hidden).astype(BF)
    moved = dot(d_all[...], home, 1, 0).astype(BF)
    tile = 512
    for j in range(0, features, tile):
        p_ref[:, j : j + tile] = dot(moved, gu[:, j : j + tile], 0, 0).astype(BF)
    score = dot(jnp.broadcast_to(score, (LANES, count)).astype(BF), home, 1, 0)
    p_ref[:, features:] = score.T.astype(BF)


def rows_call(zs, chunks, weights):
    count = sum(c.shape[0] for c in chunks)
    width = chunks[0].shape[1]
    n, hid, features = weights.shape[0], weights.shape[1] // 3, weights.shape[2]
    return pl.pallas_call(
        rows_kernel,
        out_shape=[
            jax.ShapeDtypeStruct((count, features + LANES), BF),
            *[jax.ShapeDtypeStruct((2 * hid, count), BF)] * n,
            jax.ShapeDtypeStruct((n, hid, count), BF),
        ],
        in_specs=[pl.BlockSpec(memory_space=pltpu.SMEM)] + [pl.BlockSpec(memory_space=pl.ANY)] * 4,
        out_specs=[vmem()] * (n + 2),
        scratch_shapes=[
            pltpu.VMEM((n * 2 * hid, features), BF),
            pltpu.VMEM((n, hid, features), BF),
            pltpu.VMEM((count, width), BF),
            pltpu.VMEM((n * 2 * hid, count), BF),
            pltpu.SemaphoreType.DMA((3 + 2 * n,)),
        ],
        compiler_params=pltpu.CompilerParams(vmem_limit_bytes=56 * MIB),
        cost_estimate=pl.CostEstimate(
            flops=2 * count * features * hid * n * 5,
            bytes_accessed=2 * features * hid * 12 + 6 * count * features,
            transcendentals=count * hid * n,
        ),
        name="rows",
    )(zs, *chunks, weights)


def down_kernel(s_ref, b_ref, a_ref, c_ref, own_ref, go_ref, come_ref, right_ref, left_ref, rows):
    quarter = a_ref.shape[0]
    rows[0 : 2 * quarter, :] = b_ref[...]
    rows[2 * quarter : 3 * quarter, :] = a_ref[...]
    rows[3 * quarter :, :] = c_ref[...]
    grads = rows[...]
    half = right_ref.shape[0]
    own_ref[...] = dot(s_ref[0], grads, 1, 0)
    left = dot(s_ref[1], grads, 1, 0).astype(BF)
    right = dot(s_ref[2], grads, 1, 0).astype(BF)
    two = dot(s_ref[3], grads, 1, 0).astype(BF)
    go_ref[:half, :] = two[:half]
    go_ref[half:, :] = right[half:]
    come_ref[:half, :] = left[:half]
    come_ref[half:, :] = two[half:]
    right_ref[...] = right[:half]
    left_ref[...] = left[half:]


def down_call(scaled, chunks, features):
    tile = 512
    n, hid, count = scaled.shape
    first = features // tile
    tiled = [pl.BlockSpec((c.shape[0], tile), lambda j: (0, first + j)) for c in chunks]
    return pl.pallas_call(
        down_kernel,
        grid=(features // tile,),
        out_shape=[jax.ShapeDtypeStruct((hid, features), F32)]
        + [jax.ShapeDtypeStruct((hid, features), BF)] * 2
        + [jax.ShapeDtypeStruct((hid // 2, features), BF)] * 2,
        in_specs=[pl.BlockSpec(scaled.shape, lambda j: (0, 0, 0))] + tiled,
        out_specs=[pl.BlockSpec((hid, tile), lambda j: (0, j))] * 3
        + [pl.BlockSpec((hid // 2, tile), lambda j: (0, j))] * 2,
        scratch_shapes=[pltpu.VMEM((count, tile), BF)],
        compiler_params=pltpu.CompilerParams(vmem_limit_bytes=24 * MIB),
        cost_estimate=pl.CostEstimate(
            flops=2 * n * count * features * hid,
            bytes_accessed=2 * features * (count + 5 * hid),
            transcendentals=0,
        ),
        name="down_parts",
    )(scaled, *chunks)


def weights_kernel(zs_ref, *refs):
    d_refs, b_refs, ac_refs, (gate_ref, up_ref, two) = refs[:4], refs[4:9], refs[9:13], refs[13:]
    hid = gate_ref.shape[0]
    half, quarter = two.shape[0], two.shape[0] // 2
    two[:quarter, :] = b_refs[3][...]
    two[quarter:, :] = b_refs[4][...]
    total = dot(d_refs[3][:, :half], two[...], 1, 0)
    for d, x in zip(d_refs[:3], b_refs[:3]):
        total = total + dot(d[:, :half], x[...], 1, 0)
    for d, x in zip(d_refs, ac_refs):
        total = total + dot(d[:, half:], x[0], 1, 0)
    total = total.astype(BF)
    gate_ref[...] = total[:hid]
    up_ref[...] = total[hid:]


def weights_call(zs, ds, x_b, x_ac):
    tile = 512
    n, count, features = x_ac.shape
    hid = ds[0].shape[0] // 2
    whole = [pl.BlockSpec(d.shape, lambda j, zs: (0, 0)) for d in ds]
    near = [pl.BlockSpec((x.shape[0], tile), lambda j, zs: (0, j)) for x in x_b]
    tiled = [
        pl.BlockSpec((1, count, tile), lambda j, zs, at=at: ((zs[2] + at) % 4, 0, j))
        for at in (0, 3, 1, 2)
    ]
    return pl.pallas_call(
        weights_kernel,
        grid_spec=pltpu.PrefetchScalarGridSpec(
            num_scalar_prefetch=1,
            grid=(features // tile,),
            in_specs=whole + near + tiled,
            out_specs=[pl.BlockSpec((hid, tile), lambda j, zs: (0, j))] * 2,
            scratch_shapes=[pltpu.VMEM((count, tile), BF)],
        ),
        out_shape=[jax.ShapeDtypeStruct((hid, features), BF)] * 2,
        compiler_params=pltpu.CompilerParams(vmem_limit_bytes=24 * MIB),
        cost_estimate=pl.CostEstimate(
            flops=8 * n * count * features * hid,
            bytes_accessed=2 * features * (2 * n * count + 2 * hid),
            transcendentals=0,
        ),
        name="weight_grads",
    )(zs, *ds, *x_b, *[x_ac] * n)


def home_kernel(code_ref, home_ref, grad_ref, score_ref):
    top, rows = code_ref.shape
    places = home_ref.shape[0]
    features = grad_ref.shape[1]
    wanted = (iota((places, rows), 0) + 1).astype(F32)
    hits = [jnp.where(wanted == code_ref[k : k + 1, :], 1.0, 0.0) for k in range(top)]
    score = home_ref[:, features : features + 1].astype(F32)
    score_ref[...] = jnp.concatenate(
        [jnp.sum(hit * score, axis=0, keepdims=True) for hit in hits], axis=0
    ).astype(BF)
    pick = sum(hits).astype(BF)
    grad_ref[...] = dot(pick, home_ref[:, :features], 0, 0).astype(BF)


def home_call(code, home, features):
    return pl.pallas_call(
        home_kernel,
        out_shape=[
            jax.ShapeDtypeStruct((code.shape[1], features), BF),
            jax.ShapeDtypeStruct(code.shape, BF),
        ],
        in_specs=[vmem()] * 2,
        out_specs=[vmem()] * 2,
        name="home",
    )(code, home)


def local(tokens, out_grad, expert_ids, keep_flags, route_weights, gate_w, up_w, down_w):
    nz, n = lax.axis_size(Z), lax.axis_size("x")
    step, features = tokens.shape
    zs = jnp.stack([lax.axis_index(a) for a in ("zh", ("zq", "zr"), "x")]).astype(jnp.int32)
    half = gate_w.shape[1] // 2

    joined = jnp.concatenate([gate_w[0], up_w[0], down_w[0]], axis=0)
    weights = lax.all_gather(joined, "x", axis=0)
    own, code = payload_call(tokens, out_grad, expert_ids.T, keep_flags.T, route_weights.T)

    chunk = lax.all_gather(own, FAR, axis=0, tiled=True)
    left, right = shift(chunk, 1, Z, nz), shift(chunk, -1, Z, nz)

    def exchange(packed):
        rows, width = packed.shape
        return lax.all_to_all(
            packed.reshape(8, rows // 8, width), YC, split_axis=0, concat_axis=0, tiled=True
        ).reshape(rows, width)

    rows_a = exchange(pack_call(zs, [chunk], step))
    packed_b = pack_call(zs, [left, right], step)
    rest_a = shift(right[: 2 * step], -1, Z, nz)
    rest_b = shift(left[2 * step :], 1, Z, nz)
    rest_a, rest_b, _ = lax.optimization_barrier((rest_a, rest_b, packed_b))
    packed_b, rows_a = lax.optimization_barrier((packed_b, rows_a))
    rows_b = exchange(packed_b)
    packed_c = pack_call(zs, [rest_a, rest_b], step)
    packed_c, rows_b = lax.optimization_barrier((packed_c, rows_b))
    x_b = rows_b[:, :features]
    mid = x_b.shape[0] // 2
    x_left, x_right = shift(x_b, 1, "x", n), shift(x_b, -1, "x", n)
    rows_c = exchange(packed_c)
    x_ac = jnp.concatenate([rows_a[:, :features], rows_c[:, :features]], axis=0)
    x_ac, rows_c, x_left, x_right = lax.optimization_barrier((x_ac, rows_c, x_left, x_right))
    x_ac = lax.all_gather(x_ac, "x", axis=0)
    x_far = [shift(x_right[:mid], -1, "x", n), shift(x_left[mid:], 1, "x", n)]

    chunks = [rows_b, rows_a, rows_c]
    back, d_own, d_left, d_right, d_two, scaled = rows_call(zs, chunks, weights)
    home = lax.all_to_all(
        back.reshape(-1, CAPACITY, back.shape[1]), PLACE, split_axis=0, concat_axis=0, tiled=True
    ).reshape(back.shape)
    ds = [d_own, shift(d_right, 1, "x", n), shift(d_left, -1, "x", n), shift(d_two, 2, "x", n)]
    p_own, p_go, p_come, p_right, p_left = down_call(scaled, chunks, features)
    from_left, from_right = shift(p_go, 1, "x", n), shift(p_come, -1, "x", n)
    from_left, from_right, *ds = lax.optimization_barrier((from_left, from_right, *ds))
    p_right = (p_right.astype(F32) + from_left[:half].astype(F32)).astype(BF)
    p_left = (p_left.astype(F32) + from_right[half:].astype(F32)).astype(BF)
    left_top, right_low = shift(p_right, 1, "x", n), shift(p_left, -1, "x", n)
    grad_down = jnp.concatenate(
        [
            p_own[:half] + left_top.astype(F32) + from_right[:half].astype(F32),
            p_own[half:] + from_left[half:].astype(F32) + right_low.astype(F32),
        ],
        axis=0,
    ).astype(BF)

    grad_gate, grad_up = weights_call(zs, ds, [x_b, x_left, x_right, *x_far], x_ac)

    token_grad, slot_score = home_call(code, home, features)
    return (token_grad, slot_score.T, grad_gate[None], grad_up[None], grad_down[None])


def solution(mesh):
    fine = Mesh(mesh.devices.reshape(2, 4, 2, 2, 4, 4), (*PLACE, "x"))
    by_row = P((*PLACE, "x"), None)
    by_expert = P(PLACE, "x", None)
    return jax.shard_map(
        local,
        mesh=fine,
        in_specs=(by_row,) * 5 + (by_expert,) * 3,
        out_specs=(by_row,) * 2 + (by_expert,) * 3,
        check_vma=False,
    )
```

```python
import jax
import jax.numpy as jnp
from jax import lax
from jax.experimental import pallas as pl
from jax.experimental.pallas import tpu as pltpu
from jax.sharding import Mesh, PartitionSpec as P

BF = jnp.bfloat16
F32 = jnp.float32
LANES = 128
CAPACITY = 2
MIB = 1024 * 1024
FAR = ("zh", "zq")
Z = ("zh", "zq", "zr")
YC = ("y", "c")
PLACE = ("zh", "y", "c", "zq", "zr")


def dot(a, b, da, db):
    return lax.dot_general(a, b, (((da,), (db,)), ((), ())), preferred_element_type=F32)


def iota(shape, axis):
    return lax.broadcasted_iota(jnp.int32, shape, axis)


def shift(block, step, axes, n):
    return lax.ppermute(block, axes, [(i, (i + step) % n) for i in range(n)])


def vmem():
    return pl.BlockSpec(memory_space=pltpu.VMEM)


def payload_kernel(tok_ref, grad_ref, ids_ref, keep_ref, weight_ref, out_ref, code_ref):
    features = tok_ref.shape[1]
    top, rows = ids_ref.shape
    experts = LANES
    ids, kept = ids_ref[...], keep_ref[...] > 0
    names = iota((experts, rows), 0)
    named = [names == ids[k : k + 1, :] for k in range(top)]
    tally = sum(jnp.where(named[k] & kept[k : k + 1, :], 1.0, 0.0) for k in range(top))
    before = (iota((rows, rows), 0) < iota((rows, rows), 1)).astype(BF)
    earlier = dot(tally.astype(BF), before, 1, 0)
    position = jnp.concatenate(
        [jnp.sum(jnp.where(named[k], earlier, 0.0), axis=0, keepdims=True) for k in range(top)],
        axis=0,
    )
    code = jnp.where(kept, ids.astype(F32) * CAPACITY + position + 1.0, 0.0)
    code_ref[...] = code
    spread = (iota((rows, LANES), 0) == iota((rows, LANES), 1)).astype(BF)
    both = jnp.concatenate([code.astype(BF), weight_ref[...]], axis=0)
    out_ref[:, :features] = tok_ref[...]
    out_ref[:, features : 2 * features] = grad_ref[...]
    out_ref[:, 2 * features :] = dot(both, spread, 1, 0).astype(BF)


def payload_call(tokens, out_grad, ids, keep, weights):
    rows, features = tokens.shape
    return pl.pallas_call(
        payload_kernel,
        out_shape=[
            jax.ShapeDtypeStruct((rows, 2 * features + LANES), BF),
            jax.ShapeDtypeStruct(ids.shape, F32),
        ],
        in_specs=[vmem()] * 5,
        out_specs=[vmem()] * 2,
        name="payload",
    )(tokens, out_grad, ids, keep, weights)


def pack_kernel(step, zs_ref, *refs):
    blocks, out_ref = refs[:-1], refs[-1]
    count = sum(b.shape[0] for b in blocks)
    zn = count // step
    rows, width = out_ref.shape
    features = (width - LANES) // 2
    half = step // 2
    codes = jnp.zeros((half, count), F32)
    weights = jnp.zeros((half, count), F32)
    at = 0
    for block in blocks:
        for first in range(0, block.shape[0], step):
            place = (iota((LANES, count), 0) + at == iota((LANES, count), 1)) & (
                iota((LANES, count), 0) < step
            )
            both = dot(
                block[first : first + step, 2 * features :], place.astype(BF), 1, 0
            )
            codes = codes + both[:half]
            weights = weights + both[half:]
            at += step
    zh, zl = zs_ref[0], zs_ref[1]
    row, col = iota((rows, count), 0), iota((rows, count), 1)
    dest = row // (zn * CAPACITY)
    wanted = ((zh * 64 + dest * 8 + zl) * CAPACITY + row % CAPACITY + 1).astype(F32)
    wanted = jnp.where((row // CAPACITY) % zn == col // step, wanted, -1.0)
    pick = jnp.zeros((rows, count), F32)
    coef = jnp.zeros((rows, count), F32)
    for k in range(half):
        hit = wanted == codes[k : k + 1, :]
        pick = pick + jnp.where(hit, 1.0, 0.0)
        coef = coef + jnp.where(hit, weights[k : k + 1, :], 0.0)
    pick = pick.astype(BF)
    tile = 1024
    for j in range(0, 2 * features, tile):
        total, at = None, 0
        for block in blocks:
            size = block.shape[0]
            part = dot(pick[:, at : at + size], block[:, j : j + tile], 1, 0)
            total = part if total is None else total + part
            at += size
        out_ref[:, j : j + tile] = total.astype(BF)
    out_ref[:, 2 * features :] = jnp.broadcast_to(
        jnp.sum(coef, axis=1, keepdims=True), (rows, LANES)
    ).astype(BF)


def pack_call(zs, blocks, step):
    count, width = sum(b.shape[0] for b in blocks), blocks[0].shape[1]
    rows = 8 * (count // step) * CAPACITY

    def body(*refs):
        pack_kernel(step, *refs)

    return pl.pallas_call(
        body,
        out_shape=jax.ShapeDtypeStruct((rows, width), BF),
        in_specs=[pl.BlockSpec(memory_space=pltpu.SMEM)] + [vmem()] * len(blocks),
        out_specs=vmem(),
        name="pack",
    )(zs, *blocks)


def homes(z, rows):
    row, place = iota((rows, rows), 0), iota((rows, rows), 1)
    quarter = rows // 4
    first, last = row < quarter, row >= 3 * quarter
    inside = jnp.where(first, row, jnp.where(last, row - 3 * quarter, row - quarter))
    zn = jnp.where(first | last, 4, 8)
    source = inside // (zn * CAPACITY)
    zi = (inside // CAPACITY) % zn
    turn = jnp.where(first, 0, jnp.where(last, 2, jnp.where(zi < 4, 3, 1)))
    zed = 4 * (zi % 4) + (z + turn) % 4
    home = ((zed // 8) * 64 + source * 8 + zed % 8) * CAPACITY + inside % CAPACITY
    return (home == place).astype(BF)


def rows_kernel(zs_ref, *refs):
    (a_ref, b_ref, c_ref, *w_refs), p_ref, refs = refs[:8], refs[8], refs[9:]
    d_refs, s_ref, (gu, dn, rows, d_all, sems) = refs[:4], refs[4], refs[5:]
    hid = dn.shape[1]
    count, width = rows.shape
    features = (width - LANES) // 2
    quarter = count // 4
    pairs = [
        (a_ref, rows.at[pl.ds(0, quarter)]),
        (b_ref, rows.at[pl.ds(quarter, 2 * quarter)]),
        (c_ref, rows.at[pl.ds(3 * quarter, quarter)]),
    ]
    for q in range(3):
        pairs.append((w_refs[q].at[pl.ds(0, 2 * hid)], gu.at[pl.ds(q * 2 * hid, 2 * hid)]))
        pairs.append((w_refs[q].at[pl.ds(2 * hid, hid)], dn.at[q]))
    top, first = w_refs[3].shape[0], 6 * hid
    pairs.append((w_refs[3], gu.at[pl.ds(first, top)]))
    pairs.append((w_refs[4].at[pl.ds(0, 2 * hid - top)], gu.at[pl.ds(first + top, 2 * hid - top)]))
    pairs.append((w_refs[4].at[pl.ds(2 * hid - top, hid)], dn.at[3]))
    copies = [pltpu.make_async_copy(s, t, sems.at[i]) for i, (s, t) in enumerate(pairs)]
    for copy in copies:
        copy.start()
    for copy in copies[:3]:
        copy.wait()
    home = homes(zs_ref[0] * 8 + zs_ref[1], count)
    coef = rows[:, 2 * features :].astype(F32).T[0:1, :]
    score = None
    for q in range(4):
        for copy in copies[3 + 2 * q : 5 + 2 * q + q // 3]:
            copy.wait()
        first = q * 2 * hid
        pre = dot(gu[first : first + 2 * hid, :], rows[:, :features], 1, 1)
        back = dot(dn[q], rows[:, features : 2 * features], 1, 1)
        gate_pre, up_pre = pre[:hid], pre[hid:]
        sigma = jax.nn.sigmoid(gate_pre)
        active = gate_pre * sigma
        hidden = active * up_pre
        part = jnp.sum(hidden.astype(BF).astype(F32) * back, axis=0, keepdims=True)
        score = part if score is None else score + part
        d_hidden = coef * back
        d_gate = d_hidden * up_pre * sigma * (1.0 + gate_pre * (1.0 - sigma))
        d_all[first : first + hid, :] = d_gate.astype(BF)
        d_all[first + hid : first + 2 * hid, :] = (d_hidden * active).astype(BF)
        d_refs[q][...] = d_all[first : first + 2 * hid, :]
        s_ref[q] = (coef * hidden).astype(BF)
    moved = dot(d_all[...], home, 1, 0).astype(BF)
    tile = 512
    for j in range(0, features, tile):
        p_ref[:, j : j + tile] = dot(moved, gu[:, j : j + tile], 0, 0).astype(BF)
    score = dot(jnp.broadcast_to(score, (LANES, count)).astype(BF), home, 1, 0)
    p_ref[:, features:] = score.T.astype(BF)


def rows_call(zs, chunks, weights):
    count = sum(c.shape[0] for c in chunks)
    width = chunks[0].shape[1]
    n, hid, features = 4, weights[0].shape[0] // 3, weights[0].shape[1]
    return pl.pallas_call(
        rows_kernel,
        out_shape=[
            jax.ShapeDtypeStruct((count, features + LANES), BF),
            *[jax.ShapeDtypeStruct((2 * hid, count), BF)] * n,
            jax.ShapeDtypeStruct((n, hid, count), BF),
        ],
        in_specs=[pl.BlockSpec(memory_space=pltpu.SMEM)] + [pl.BlockSpec(memory_space=pl.ANY)] * 8,
        out_specs=[vmem()] * (n + 2),
        scratch_shapes=[
            pltpu.VMEM((n * 2 * hid, features), BF),
            pltpu.VMEM((n, hid, features), BF),
            pltpu.VMEM((count, width), BF),
            pltpu.VMEM((n * 2 * hid, count), BF),
            pltpu.SemaphoreType.DMA((4 + 2 * n,)),
        ],
        compiler_params=pltpu.CompilerParams(vmem_limit_bytes=56 * MIB),
        cost_estimate=pl.CostEstimate(
            flops=2 * count * features * hid * n * 5,
            bytes_accessed=2 * features * hid * 12 + 6 * count * features,
            transcendentals=count * hid * n,
        ),
        name="rows",
    )(zs, *chunks, *weights)


def down_kernel(s_ref, a_ref, b_ref, c_ref, own_ref, go_ref, come_ref, right_ref, left_ref, rows):
    quarter = a_ref.shape[0]
    rows[0:quarter, :] = a_ref[...]
    rows[quarter : 3 * quarter, :] = b_ref[...]
    rows[3 * quarter :, :] = c_ref[...]
    grads = rows[...]
    half = right_ref.shape[0]
    own_ref[...] = dot(s_ref[0], grads, 1, 0)
    left = dot(s_ref[1], grads, 1, 0).astype(BF)
    right = dot(s_ref[2], grads, 1, 0).astype(BF)
    two = dot(s_ref[3], grads, 1, 0).astype(BF)
    go_ref[:half, :] = two[:half]
    go_ref[half:, :] = right[half:]
    come_ref[:half, :] = left[:half]
    come_ref[half:, :] = two[half:]
    right_ref[...] = right[:half]
    left_ref[...] = left[half:]


def down_call(scaled, chunks, features):
    tile = 512
    n, hid, count = scaled.shape
    first = features // tile
    tiled = [pl.BlockSpec((c.shape[0], tile), lambda j: (0, first + j)) for c in chunks]
    return pl.pallas_call(
        down_kernel,
        grid=(features // tile,),
        out_shape=[jax.ShapeDtypeStruct((hid, features), F32)]
        + [jax.ShapeDtypeStruct((hid, features), BF)] * 2
        + [jax.ShapeDtypeStruct((hid // 2, features), BF)] * 2,
        in_specs=[pl.BlockSpec(scaled.shape, lambda j: (0, 0, 0))] + tiled,
        out_specs=[pl.BlockSpec((hid, tile), lambda j: (0, j))] * 3
        + [pl.BlockSpec((hid // 2, tile), lambda j: (0, j))] * 2,
        scratch_shapes=[pltpu.VMEM((count, tile), BF)],
        compiler_params=pltpu.CompilerParams(vmem_limit_bytes=24 * MIB),
        cost_estimate=pl.CostEstimate(
            flops=2 * n * count * features * hid,
            bytes_accessed=2 * features * (count + 5 * hid),
            transcendentals=0,
        ),
        name="down_parts",
    )(scaled, *chunks)


def weights_kernel(*refs):
    d_refs, x_refs, (gate_ref, up_ref, rows) = refs[:4], refs[4:11], refs[11:]
    own, left, right, more_left, more_right, last, two = x_refs
    hid = gate_ref.shape[0]
    most, mid = own.shape[0], own.shape[0] // 2
    for q, (first, end) in enumerate(((own, last), (left, more_left), (right, more_right))):
        rows[q, :most, :] = first[...]
        rows[q, most:, :] = end[end.shape[0] - two.shape[0] :, :]
    rows[3, :mid, :] = more_right[:mid, :]
    rows[3, mid:most, :] = more_left[:mid, :]
    rows[3, most:, :] = two[...]
    total = sum(dot(d[...], rows[q], 1, 0) for q, d in enumerate(d_refs)).astype(BF)
    gate_ref[...] = total[:hid]
    up_ref[...] = total[hid:]


def weights_call(ds, xs):
    tile = 512
    hid, count, features = ds[0].shape[0] // 2, ds[0].shape[1], xs[0].shape[1]
    whole = [pl.BlockSpec(d.shape, lambda j: (0, 0)) for d in ds]
    tiled = [pl.BlockSpec((x.shape[0], tile), lambda j: (0, j)) for x in xs]
    return pl.pallas_call(
        weights_kernel,
        grid=(features // tile,),
        out_shape=[jax.ShapeDtypeStruct((hid, features), BF)] * 2,
        in_specs=whole + tiled,
        out_specs=[pl.BlockSpec((hid, tile), lambda j: (0, j))] * 2,
        scratch_shapes=[pltpu.VMEM((len(ds), count, tile), BF)],
        compiler_params=pltpu.CompilerParams(vmem_limit_bytes=24 * MIB),
        cost_estimate=pl.CostEstimate(
            flops=4 * len(ds) * count * features * hid,
            bytes_accessed=2 * features * (len(ds) * count + 2 * hid),
            transcendentals=0,
        ),
        name="weight_grads",
    )(*ds, *xs)


def home_kernel(code_ref, home_ref, grad_ref, score_ref):
    top, rows = code_ref.shape
    places = home_ref.shape[0]
    features = grad_ref.shape[1]
    wanted = (iota((places, rows), 0) + 1).astype(F32)
    hits = [jnp.where(wanted == code_ref[k : k + 1, :], 1.0, 0.0) for k in range(top)]
    score = home_ref[:, features : features + 1].astype(F32)
    score_ref[...] = jnp.concatenate(
        [jnp.sum(hit * score, axis=0, keepdims=True) for hit in hits], axis=0
    ).astype(BF)
    pick = sum(hits).astype(BF)
    grad_ref[...] = dot(pick, home_ref[:, :features], 0, 0).astype(BF)


def home_call(code, home, features):
    return pl.pallas_call(
        home_kernel,
        out_shape=[
            jax.ShapeDtypeStruct((code.shape[1], features), BF),
            jax.ShapeDtypeStruct(code.shape, BF),
        ],
        in_specs=[vmem()] * 2,
        out_specs=[vmem()] * 2,
        name="home",
    )(code, home)


def local(tokens, out_grad, expert_ids, keep_flags, route_weights, gate_w, up_w, down_w):
    nz, n = lax.axis_size(Z), lax.axis_size("x")
    step, features = tokens.shape
    zs = jnp.stack([lax.axis_index(a) for a in ("zh", ("zq", "zr"), "x")]).astype(jnp.int32)
    half = gate_w.shape[1] // 2

    joined = jnp.concatenate([gate_w[0], up_w[0], down_w[0]], axis=0)
    part = joined.shape[0] // 2
    w_left, w_right = shift(joined, 1, "x", n), shift(joined, -1, "x", n)
    own, code = payload_call(tokens, out_grad, expert_ids.T, keep_flags.T, route_weights.T)

    chunk = lax.all_gather(own, FAR, axis=0, tiled=True)
    left, right = shift(chunk, 1, Z, nz), shift(chunk, -1, Z, nz)

    def exchange(packed):
        rows, width = packed.shape
        return lax.all_to_all(
            packed.reshape(8, rows // 8, width), YC, split_axis=0, concat_axis=0, tiled=True
        ).reshape(rows, width)

    rows_a = exchange(pack_call(zs, [chunk], step))
    packed_b = pack_call(zs, [left, right], step)
    packed_b, w_left, w_right = lax.optimization_barrier((packed_b, w_left, w_right))
    w_a, w_b = shift(w_right[:part], -1, "x", n), shift(w_left[part:], 1, "x", n)
    rest_a = shift(right[: 2 * step], -1, Z, nz)
    rest_b = shift(left[2 * step :], 1, Z, nz)
    rest_a, rest_b, _ = lax.optimization_barrier((rest_a, rest_b, packed_b))
    packed_b, rows_a = lax.optimization_barrier((packed_b, rows_a))
    rows_b = exchange(packed_b)
    packed_c = pack_call(zs, [rest_a, rest_b], step)
    packed_c, rows_b = lax.optimization_barrier((packed_c, rows_b))
    rows_c = exchange(packed_c)

    chunks = [rows_a, rows_b, rows_c]
    back, d_own, d_left, d_right, d_two, scaled = rows_call(
        zs, chunks, [joined, w_left, w_right, w_a, w_b]
    )
    x_ab = jnp.concatenate([rows_a[:, :features], rows_b[:, :features]], axis=0)
    x_left, x_right = shift(x_ab, 1, "x", n), shift(x_ab, -1, "x", n)
    back, x_left, x_right = lax.optimization_barrier((back, x_left, x_right))
    home = lax.all_to_all(
        back.reshape(-1, CAPACITY, back.shape[1]), PLACE, split_axis=0, concat_axis=0, tiled=True
    ).reshape(back.shape)
    mid = x_ab.shape[0] // 2
    x_c = rows_c[:, :features]
    x_two = shift(x_c, 2, "x", n)
    more_left = shift(jnp.concatenate([x_left[mid:], x_c], axis=0), 1, "x", n)
    more_right = shift(jnp.concatenate([x_right[:mid], x_c], axis=0), -1, "x", n)
    ds = [d_own, shift(d_right, 1, "x", n), shift(d_left, -1, "x", n), shift(d_two, 2, "x", n)]

    p_own, p_go, p_come, p_right, p_left = down_call(scaled, chunks, features)
    from_left, from_right = shift(p_go, 1, "x", n), shift(p_come, -1, "x", n)
    p_right = (p_right.astype(F32) + from_left[:half].astype(F32)).astype(BF)
    p_left = (p_left.astype(F32) + from_right[half:].astype(F32)).astype(BF)
    left_top, right_low = shift(p_right, 1, "x", n), shift(p_left, -1, "x", n)
    grad_down = jnp.concatenate(
        [
            p_own[:half] + left_top.astype(F32) + from_right[:half].astype(F32),
            p_own[half:] + from_left[half:].astype(F32) + right_low.astype(F32),
        ],
        axis=0,
    ).astype(BF)

    grad_gate, grad_up = weights_call(
        ds, [x_ab, x_left, x_right, more_left, more_right, x_c, x_two]
    )

    token_grad, slot_score = home_call(code, home, features)
    return (token_grad, slot_score.T, grad_gate[None], grad_up[None], grad_down[None])


def solution(mesh):
    fine = Mesh(mesh.devices.reshape(2, 4, 2, 2, 4, 4), (*PLACE, "x"))
    by_row = P((*PLACE, "x"), None)
    by_expert = P(PLACE, "x", None)
    return jax.shard_map(
        local,
        mesh=fine,
        in_specs=(by_row,) * 5 + (by_expert,) * 3,
        out_specs=(by_row,) * 2 + (by_expert,) * 3,
        check_vma=False,
    )
```

```python
import jax
import jax.numpy as jnp
from jax import lax
from jax.experimental import pallas as pl
from jax.experimental.pallas import tpu as pltpu
from jax.sharding import Mesh, PartitionSpec as P

BF = jnp.bfloat16
F32 = jnp.float32
LANES = 128
CAPACITY = 2
MIB = 1024 * 1024
FAR = ("zh", "zq")
Z = ("zh", "zq", "zr")
YC = ("y", "c")
PLACE = ("zh", "y", "c", "zq", "zr")


def dot(a, b, da, db):
    return lax.dot_general(a, b, (((da,), (db,)), ((), ())), preferred_element_type=F32)


def iota(shape, axis):
    return lax.broadcasted_iota(jnp.int32, shape, axis)


def shift(block, step, axes, n):
    return lax.ppermute(block, axes, [(i, (i + step) % n) for i in range(n)])


def vmem():
    return pl.BlockSpec(memory_space=pltpu.VMEM)


def payload_kernel(tok_ref, grad_ref, ids_ref, keep_ref, weight_ref, out_ref, code_ref):
    features = tok_ref.shape[1]
    top, rows = ids_ref.shape
    experts = LANES
    ids, kept = ids_ref[...], keep_ref[...] > 0
    names = iota((experts, rows), 0)
    named = [names == ids[k : k + 1, :] for k in range(top)]
    tally = sum(jnp.where(named[k] & kept[k : k + 1, :], 1.0, 0.0) for k in range(top))
    before = (iota((rows, rows), 0) < iota((rows, rows), 1)).astype(BF)
    earlier = dot(tally.astype(BF), before, 1, 0)
    position = jnp.concatenate(
        [jnp.sum(jnp.where(named[k], earlier, 0.0), axis=0, keepdims=True) for k in range(top)],
        axis=0,
    )
    code = jnp.where(kept, ids.astype(F32) * CAPACITY + position + 1.0, 0.0)
    code_ref[...] = code
    spread = (iota((rows, LANES), 0) == iota((rows, LANES), 1)).astype(BF)
    both = jnp.concatenate([code.astype(BF), weight_ref[...]], axis=0)
    out_ref[:, :features] = tok_ref[...]
    out_ref[:, features : 2 * features] = grad_ref[...]
    out_ref[:, 2 * features :] = dot(both, spread, 1, 0).astype(BF)


def payload_call(tokens, out_grad, ids, keep, weights):
    rows, features = tokens.shape
    return pl.pallas_call(
        payload_kernel,
        out_shape=[
            jax.ShapeDtypeStruct((rows, 2 * features + LANES), BF),
            jax.ShapeDtypeStruct(ids.shape, F32),
        ],
        in_specs=[vmem()] * 5,
        out_specs=[vmem()] * 2,
        name="payload",
    )(tokens, out_grad, ids, keep, weights)


def pack_kernel(step, zs_ref, *refs):
    blocks, out_ref = refs[:-1], refs[-1]
    count = sum(b.shape[0] for b in blocks)
    zn = count // step
    rows, width = out_ref.shape
    features = (width - LANES) // 2
    half = step // 2
    codes = jnp.zeros((half, count), F32)
    weights = jnp.zeros((half, count), F32)
    at = 0
    for block in blocks:
        for first in range(0, block.shape[0], step):
            place = (iota((LANES, count), 0) + at == iota((LANES, count), 1)) & (
                iota((LANES, count), 0) < step
            )
            both = dot(
                block[first : first + step, 2 * features :], place.astype(BF), 1, 0
            )
            codes = codes + both[:half]
            weights = weights + both[half:]
            at += step
    zh, zl = zs_ref[0], zs_ref[1]
    row, col = iota((rows, count), 0), iota((rows, count), 1)
    dest = row // (zn * CAPACITY)
    wanted = ((zh * 64 + dest * 8 + zl) * CAPACITY + row % CAPACITY + 1).astype(F32)
    wanted = jnp.where((row // CAPACITY) % zn == col // step, wanted, -1.0)
    pick = jnp.zeros((rows, count), F32)
    coef = jnp.zeros((rows, count), F32)
    for k in range(half):
        hit = wanted == codes[k : k + 1, :]
        pick = pick + jnp.where(hit, 1.0, 0.0)
        coef = coef + jnp.where(hit, weights[k : k + 1, :], 0.0)
    pick = pick.astype(BF)
    tile = 1024
    for j in range(0, 2 * features, tile):
        total, at = None, 0
        for block in blocks:
            size = block.shape[0]
            part = dot(pick[:, at : at + size], block[:, j : j + tile], 1, 0)
            total = part if total is None else total + part
            at += size
        out_ref[:, j : j + tile] = total.astype(BF)
    out_ref[:, 2 * features :] = jnp.broadcast_to(
        jnp.sum(coef, axis=1, keepdims=True), (rows, LANES)
    ).astype(BF)


def pack_call(zs, blocks, step):
    count, width = sum(b.shape[0] for b in blocks), blocks[0].shape[1]
    rows = 8 * (count // step) * CAPACITY

    def body(*refs):
        pack_kernel(step, *refs)

    return pl.pallas_call(
        body,
        out_shape=jax.ShapeDtypeStruct((rows, width), BF),
        in_specs=[pl.BlockSpec(memory_space=pltpu.SMEM)] + [vmem()] * len(blocks),
        out_specs=vmem(),
        name="pack",
    )(zs, *blocks)


def homes(z, rows):
    row, place = iota((rows, rows), 0), iota((rows, rows), 1)
    quarter = rows // 4
    first, last = row < quarter, row >= 3 * quarter
    inside = jnp.where(first, row, jnp.where(last, row - 3 * quarter, row - quarter))
    zn = jnp.where(first | last, 4, 8)
    source = inside // (zn * CAPACITY)
    zi = (inside // CAPACITY) % zn
    turn = jnp.where(first, 0, jnp.where(last, 2, jnp.where(zi < 4, 3, 1)))
    zed = 4 * (zi % 4) + (z + turn) % 4
    home = ((zed // 8) * 64 + source * 8 + zed % 8) * CAPACITY + inside % CAPACITY
    return (home == place).astype(BF)


def rows_kernel(zs_ref, *refs):
    (a_ref, b_ref, c_ref, *w_refs), p_ref, refs = refs[:8], refs[8], refs[9:]
    d_refs, s_ref, (gu, dn, rows, d_all, sems) = refs[:4], refs[4], refs[5:]
    hid = dn.shape[1]
    count, width = rows.shape
    features = (width - LANES) // 2
    quarter = count // 4
    pairs = [
        (a_ref, rows.at[pl.ds(0, quarter)]),
        (b_ref, rows.at[pl.ds(quarter, 2 * quarter)]),
        (c_ref, rows.at[pl.ds(3 * quarter, quarter)]),
    ]
    for q in range(3):
        pairs.append((w_refs[q].at[pl.ds(0, 2 * hid)], gu.at[pl.ds(q * 2 * hid, 2 * hid)]))
        pairs.append((w_refs[q].at[pl.ds(2 * hid, hid)], dn.at[q]))
    top, first = w_refs[3].shape[0], 6 * hid
    pairs.append((w_refs[3], gu.at[pl.ds(first, top)]))
    pairs.append((w_refs[4].at[pl.ds(0, 2 * hid - top)], gu.at[pl.ds(first + top, 2 * hid - top)]))
    pairs.append((w_refs[4].at[pl.ds(2 * hid - top, hid)], dn.at[3]))
    copies = [pltpu.make_async_copy(s, t, sems.at[i]) for i, (s, t) in enumerate(pairs)]
    for copy in copies:
        copy.start()
    for copy in copies[:3]:
        copy.wait()
    home = homes(zs_ref[0] * 8 + zs_ref[1], count)
    coef = rows[:, 2 * features :].astype(F32).T[0:1, :]
    score = None
    for q in range(4):
        for copy in copies[3 + 2 * q : 5 + 2 * q + q // 3]:
            copy.wait()
        first = q * 2 * hid
        pre = dot(gu[first : first + 2 * hid, :], rows[:, :features], 1, 1)
        back = dot(dn[q], rows[:, features : 2 * features], 1, 1)
        gate_pre, up_pre = pre[:hid], pre[hid:]
        sigma = jax.nn.sigmoid(gate_pre)
        active = gate_pre * sigma
        hidden = active * up_pre
        part = jnp.sum(hidden.astype(BF).astype(F32) * back, axis=0, keepdims=True)
        score = part if score is None else score + part
        d_hidden = coef * back
        d_gate = d_hidden * up_pre * sigma * (1.0 + gate_pre * (1.0 - sigma))
        d_all[first : first + hid, :] = d_gate.astype(BF)
        d_all[first + hid : first + 2 * hid, :] = (d_hidden * active).astype(BF)
        if q == 0:
            d_refs[0][...] = d_all[: 2 * hid, :]
        else:
            size = d_refs[q].shape[0]
            for j in range(features // count):
                d_refs[q][:, j * count : (j + 1) * count] = d_all[
                    first + j * size : first + (j + 1) * size, :
                ]
        s_ref[q] = (coef * hidden).astype(BF)
    moved = dot(d_all[...], home, 1, 0).astype(BF)
    tile = 512
    for j in range(0, features, tile):
        p_ref[:, j : j + tile] = dot(moved, gu[:, j : j + tile], 0, 0).astype(BF)
    score = dot(jnp.broadcast_to(score, (LANES, count)).astype(BF), home, 1, 0)
    p_ref[:, features:] = score.T.astype(BF)


def rows_call(zs, chunks, weights):
    count = sum(c.shape[0] for c in chunks)
    width = chunks[0].shape[1]
    n, hid, features = 4, weights[0].shape[0] // 3, weights[0].shape[1]
    return pl.pallas_call(
        rows_kernel,
        out_shape=[
            jax.ShapeDtypeStruct((count, features + LANES), BF),
            jax.ShapeDtypeStruct((2 * hid, count), BF),
            *[jax.ShapeDtypeStruct((2 * hid * count // features, features), BF)] * (n - 1),
            jax.ShapeDtypeStruct((n, hid, count), BF),
        ],
        in_specs=[pl.BlockSpec(memory_space=pltpu.SMEM)] + [pl.BlockSpec(memory_space=pl.ANY)] * 8,
        out_specs=[vmem()] * (n + 2),
        scratch_shapes=[
            pltpu.VMEM((n * 2 * hid, features), BF),
            pltpu.VMEM((n, hid, features), BF),
            pltpu.VMEM((count, width), BF),
            pltpu.VMEM((n * 2 * hid, count), BF),
            pltpu.SemaphoreType.DMA((4 + 2 * n,)),
        ],
        compiler_params=pltpu.CompilerParams(vmem_limit_bytes=56 * MIB),
        cost_estimate=pl.CostEstimate(
            flops=2 * count * features * hid * n * 5,
            bytes_accessed=2 * features * hid * 12 + 6 * count * features,
            transcendentals=count * hid * n,
        ),
        name="rows",
    )(zs, *chunks, *weights)


def down_kernel(
    s_ref, a_ref, b_ref, c_ref, dl_ref, dr_ref, own_ref, go_ref, come_ref, right_ref, left_ref, rows
):
    quarter = a_ref.shape[0]
    rows[0:quarter, :] = a_ref[...]
    rows[quarter : 3 * quarter, :] = b_ref[...]
    rows[3 * quarter :, :] = c_ref[...]
    grads = rows[...]
    half = right_ref.shape[0]
    own_ref[...] = dot(s_ref[0], grads, 1, 0)
    left = dot(s_ref[1], grads, 1, 0).astype(BF)
    right = dot(s_ref[2], grads, 1, 0).astype(BF)
    two = dot(s_ref[3], grads, 1, 0).astype(BF)
    go_ref[:half, :] = two[:half]
    go_ref[half : 2 * half, :] = right[half:]
    go_ref[2 * half :, :] = dr_ref[...]
    come_ref[:half, :] = left[:half]
    come_ref[half : 2 * half, :] = two[half:]
    come_ref[2 * half :, :] = dl_ref[...]
    right_ref[...] = right[:half]
    left_ref[...] = left[half:]


def down_call(scaled, chunks, d_left, d_right, features):
    tile = 512
    n, hid, count = scaled.shape
    first = features // tile
    tiled = [pl.BlockSpec((c.shape[0], tile), lambda j: (0, first + j)) for c in chunks]
    extra = d_left.shape[0]
    tiled += [pl.BlockSpec((extra, tile), lambda j: (0, j))] * 2
    return pl.pallas_call(
        down_kernel,
        grid=(features // tile,),
        out_shape=[jax.ShapeDtypeStruct((hid, features), F32)]
        + [jax.ShapeDtypeStruct((hid + extra, features), BF)] * 2
        + [jax.ShapeDtypeStruct((hid // 2, features), BF)] * 2,
        in_specs=[pl.BlockSpec(scaled.shape, lambda j: (0, 0, 0))] + tiled,
        out_specs=[pl.BlockSpec((hid, tile), lambda j: (0, j))]
        + [pl.BlockSpec((hid + extra, tile), lambda j: (0, j))] * 2
        + [pl.BlockSpec((hid // 2, tile), lambda j: (0, j))] * 2,
        scratch_shapes=[pltpu.VMEM((count, tile), BF)],
        compiler_params=pltpu.CompilerParams(vmem_limit_bytes=24 * MIB),
        cost_estimate=pl.CostEstimate(
            flops=2 * n * count * features * hid,
            bytes_accessed=2 * features * (count + 5 * hid),
            transcendentals=0,
        ),
        name="down_parts",
    )(scaled, *chunks, d_left, d_right)


def weights_kernel(*refs):
    d_refs, x_refs, (gate_ref, up_ref, factors, rows) = refs[:4], refs[4:11], refs[11:]
    own, left, right, more_left, more_right, last, two = x_refs
    hid = gate_ref.shape[0]
    most, mid = own.shape[0], own.shape[0] // 2
    count = rows.shape[1]

    @pl.when(pl.program_id(0) == 0)
    def _():
        factors[0] = d_refs[0][...]
        for q in range(1, 4):
            size = d_refs[q].shape[0]
            for j in range(d_refs[q].shape[1] // count):
                factors[q, j * size : (j + 1) * size, :] = d_refs[q][:, j * count : (j + 1) * count]

    for q, (first, end) in enumerate(((own, last), (left, more_left), (right, more_right))):
        rows[q, :most, :] = first[...]
        rows[q, most:, :] = end[end.shape[0] - last.shape[0] :, :]
    rows[3, :mid, :] = more_right[:mid, :]
    rows[3, mid:most, :] = more_left[:mid, :]
    rows[3, most:, :] = two[two.shape[0] - last.shape[0] :, :]
    total = sum(dot(factors[q], rows[q], 1, 0) for q in range(4)).astype(BF)
    gate_ref[...] = total[:hid]
    up_ref[...] = total[hid:]


def weights_call(d_own, from_left, from_right, from_two, xs):
    tile = 512
    n, (both, count), features = 4, d_own.shape, xs[0].shape[1]
    hid, size = both // 2, both * count // features
    last = from_left.shape[0] // size - 1
    packed = [
        pl.BlockSpec((size, features), lambda j, at=at: (at, 0)) for at in (last, last, 0)
    ]
    tiled = [pl.BlockSpec((x.shape[0], tile), lambda j: (0, j)) for x in [*xs, from_two]]
    return pl.pallas_call(
        weights_kernel,
        grid=(features // tile,),
        out_shape=[jax.ShapeDtypeStruct((hid, features), BF)] * 2,
        in_specs=[pl.BlockSpec(d_own.shape, lambda j: (0, 0)), *packed, *tiled],
        out_specs=[pl.BlockSpec((hid, tile), lambda j: (0, j))] * 2,
        scratch_shapes=[pltpu.VMEM((n, both, count), BF), pltpu.VMEM((n, count, tile), BF)],
        compiler_params=pltpu.CompilerParams(vmem_limit_bytes=24 * MIB),
        cost_estimate=pl.CostEstimate(
            flops=4 * n * count * features * hid,
            bytes_accessed=2 * features * (n * count + 2 * hid),
            transcendentals=0,
        ),
        name="weight_grads",
    )(d_own, from_left, from_right, from_two, *xs, from_two)


def home_kernel(code_ref, home_ref, grad_ref, score_ref):
    top, rows = code_ref.shape
    places = home_ref.shape[0]
    features = grad_ref.shape[1]
    wanted = (iota((places, rows), 0) + 1).astype(F32)
    hits = [jnp.where(wanted == code_ref[k : k + 1, :], 1.0, 0.0) for k in range(top)]
    score = home_ref[:, features : features + 1].astype(F32)
    score_ref[...] = jnp.concatenate(
        [jnp.sum(hit * score, axis=0, keepdims=True) for hit in hits], axis=0
    ).astype(BF)
    pick = sum(hits).astype(BF)
    grad_ref[...] = dot(pick, home_ref[:, :features], 0, 0).astype(BF)


def home_call(code, home, features):
    return pl.pallas_call(
        home_kernel,
        out_shape=[
            jax.ShapeDtypeStruct((code.shape[1], features), BF),
            jax.ShapeDtypeStruct(code.shape, BF),
        ],
        in_specs=[vmem()] * 2,
        out_specs=[vmem()] * 2,
        name="home",
    )(code, home)


def local(tokens, out_grad, expert_ids, keep_flags, route_weights, gate_w, up_w, down_w):
    nz, n = lax.axis_size(Z), lax.axis_size("x")
    step, features = tokens.shape
    zs = jnp.stack([lax.axis_index(a) for a in ("zh", ("zq", "zr"), "x")]).astype(jnp.int32)
    half = gate_w.shape[1] // 2

    joined = jnp.concatenate([gate_w[0], up_w[0], down_w[0]], axis=0)
    part = joined.shape[0] // 2
    w_left, w_right = shift(joined, 1, "x", n), shift(joined, -1, "x", n)
    own, code = payload_call(tokens, out_grad, expert_ids.T, keep_flags.T, route_weights.T)

    chunk = lax.all_gather(own, FAR, axis=0, tiled=True)
    left, right = shift(chunk, 1, Z, nz), shift(chunk, -1, Z, nz)

    def exchange(packed):
        rows, width = packed.shape
        return lax.all_to_all(
            packed.reshape(8, rows // 8, width), YC, split_axis=0, concat_axis=0, tiled=True
        ).reshape(rows, width)

    rows_a = exchange(pack_call(zs, [chunk], step))
    packed_b = pack_call(zs, [left, right], step)
    packed_b, w_left, w_right = lax.optimization_barrier((packed_b, w_left, w_right))
    w_a, w_b = shift(w_right[:part], -1, "x", n), shift(w_left[part:], 1, "x", n)
    rest_a = shift(right[: 2 * step], -1, Z, nz)
    rest_b = shift(left[2 * step :], 1, Z, nz)
    rest_a, rest_b, _ = lax.optimization_barrier((rest_a, rest_b, packed_b))
    packed_b, rows_a = lax.optimization_barrier((packed_b, rows_a))
    rows_b = exchange(packed_b)
    packed_c = pack_call(zs, [rest_a, rest_b], step)
    packed_c, rows_b = lax.optimization_barrier((packed_c, rows_b))
    rows_c = exchange(packed_c)

    chunks = [rows_a, rows_b, rows_c]
    back, d_own, d_left, d_right, d_two, scaled = rows_call(
        zs, chunks, [joined, w_left, w_right, w_a, w_b]
    )
    x_ab = jnp.concatenate([rows_a[:, :features], rows_b[:, :features]], axis=0)
    x_left, x_right = shift(x_ab, 1, "x", n), shift(x_ab, -1, "x", n)
    back, x_left, x_right = lax.optimization_barrier((back, x_left, x_right))
    home = lax.all_to_all(
        back.reshape(-1, CAPACITY, back.shape[1]), PLACE, split_axis=0, concat_axis=0, tiled=True
    ).reshape(back.shape)
    mid = x_ab.shape[0] // 2
    x_c = rows_c[:, :features]
    from_two = shift(jnp.concatenate([d_two, x_c], axis=0), 2, "x", n)
    more_left = shift(jnp.concatenate([x_left[mid:], x_c], axis=0), 1, "x", n)
    more_right = shift(jnp.concatenate([x_right[:mid], x_c], axis=0), -1, "x", n)

    p_own, p_go, p_come, p_right, p_left = down_call(scaled, chunks, d_left, d_right, features)
    from_left, from_right = shift(p_go, 1, "x", n), shift(p_come, -1, "x", n)
    p_right = (p_right.astype(F32) + from_left[:half].astype(F32)).astype(BF)
    p_left = (p_left.astype(F32) + from_right[half : 2 * half].astype(F32)).astype(BF)
    left_top, right_low = shift(p_right, 1, "x", n), shift(p_left, -1, "x", n)
    grad_down = jnp.concatenate(
        [
            p_own[:half] + left_top.astype(F32) + from_right[:half].astype(F32),
            p_own[half:] + from_left[half : 2 * half].astype(F32) + right_low.astype(F32),
        ],
        axis=0,
    ).astype(BF)
    grad_gate, grad_up = weights_call(
        d_own, from_left, from_right, from_two, [x_ab, x_left, x_right, more_left, more_right, x_c]
    )

    token_grad, slot_score = home_call(code, home, features)
    return (token_grad, slot_score.T, grad_gate[None], grad_up[None], grad_down[None])


def solution(mesh):
    fine = Mesh(mesh.devices.reshape(2, 4, 2, 2, 4, 4), (*PLACE, "x"))
    by_row = P((*PLACE, "x"), None)
    by_expert = P(PLACE, "x", None)
    return jax.shard_map(
        local,
        mesh=fine,
        in_specs=(by_row,) * 5 + (by_expert,) * 3,
        out_specs=(by_row,) * 2 + (by_expert,) * 3,
        check_vma=False,
    )
```

```python
import jax
import jax.numpy as jnp
from jax import lax
from jax.experimental import pallas as pl
from jax.experimental.pallas import tpu as pltpu
from jax.sharding import Mesh, PartitionSpec as P

BF = jnp.bfloat16
F32 = jnp.float32
LANES = 128
CAPACITY = 2
MIB = 1024 * 1024
FAR = ("zh", "zq")
Z = ("zh", "zq", "zr")
YC = ("y", "c")
PLACE = ("zh", "y", "c", "zq", "zr")


def dot(a, b, da, db):
    return lax.dot_general(a, b, (((da,), (db,)), ((), ())), preferred_element_type=F32)


def iota(shape, axis):
    return lax.broadcasted_iota(jnp.int32, shape, axis)


def shift(block, step, axes, n):
    return lax.ppermute(block, axes, [(i, (i + step) % n) for i in range(n)])


def vmem():
    return pl.BlockSpec(memory_space=pltpu.VMEM)


def payload_kernel(tok_ref, grad_ref, ids_ref, keep_ref, weight_ref, out_ref, code_ref):
    features = tok_ref.shape[1]
    top, rows = ids_ref.shape
    experts = LANES
    ids, kept = ids_ref[...], keep_ref[...] > 0
    names = iota((experts, rows), 0)
    named = [names == ids[k : k + 1, :] for k in range(top)]
    tally = sum(jnp.where(named[k] & kept[k : k + 1, :], 1.0, 0.0) for k in range(top))
    before = (iota((rows, rows), 0) < iota((rows, rows), 1)).astype(BF)
    earlier = dot(tally.astype(BF), before, 1, 0)
    position = jnp.concatenate(
        [jnp.sum(jnp.where(named[k], earlier, 0.0), axis=0, keepdims=True) for k in range(top)],
        axis=0,
    )
    code = jnp.where(kept, ids.astype(F32) * CAPACITY + position + 1.0, 0.0)
    code_ref[...] = code
    spread = (iota((rows, LANES), 0) == iota((rows, LANES), 1)).astype(BF)
    both = jnp.concatenate([code.astype(BF), weight_ref[...]], axis=0)
    out_ref[:, :features] = tok_ref[...]
    out_ref[:, features : 2 * features] = grad_ref[...]
    out_ref[:, 2 * features :] = dot(both, spread, 1, 0).astype(BF)


def payload_call(tokens, out_grad, ids, keep, weights):
    rows, features = tokens.shape
    return pl.pallas_call(
        payload_kernel,
        out_shape=[
            jax.ShapeDtypeStruct((rows, 2 * features + LANES), BF),
            jax.ShapeDtypeStruct(ids.shape, F32),
        ],
        in_specs=[vmem()] * 5,
        out_specs=[vmem()] * 2,
        name="payload",
    )(tokens, out_grad, ids, keep, weights)


def pack_kernel(step, zs_ref, *refs):
    blocks, out_ref = refs[:-1], refs[-1]
    count = sum(b.shape[0] for b in blocks)
    zn = count // step
    rows, width = out_ref.shape
    features = (width - LANES) // 2
    half = step // 2
    codes = jnp.zeros((half, count), F32)
    weights = jnp.zeros((half, count), F32)
    at = 0
    for block in blocks:
        for first in range(0, block.shape[0], step):
            place = (iota((LANES, count), 0) + at == iota((LANES, count), 1)) & (
                iota((LANES, count), 0) < step
            )
            both = dot(
                block[first : first + step, 2 * features :], place.astype(BF), 1, 0
            )
            codes = codes + both[:half]
            weights = weights + both[half:]
            at += step
    zh, zl = zs_ref[0], zs_ref[1]
    row, col = iota((rows, count), 0), iota((rows, count), 1)
    dest = row // (zn * CAPACITY)
    wanted = ((zh * 64 + dest * 8 + zl) * CAPACITY + row % CAPACITY + 1).astype(F32)
    wanted = jnp.where((row // CAPACITY) % zn == col // step, wanted, -1.0)
    pick = jnp.zeros((rows, count), F32)
    coef = jnp.zeros((rows, count), F32)
    for k in range(half):
        hit = wanted == codes[k : k + 1, :]
        pick = pick + jnp.where(hit, 1.0, 0.0)
        coef = coef + jnp.where(hit, weights[k : k + 1, :], 0.0)
    pick = pick.astype(BF)
    tile = 1024
    for j in range(0, 2 * features, tile):
        total, at = None, 0
        for block in blocks:
            size = block.shape[0]
            part = dot(pick[:, at : at + size], block[:, j : j + tile], 1, 0)
            total = part if total is None else total + part
            at += size
        out_ref[:, j : j + tile] = total.astype(BF)
    out_ref[:, 2 * features :] = jnp.broadcast_to(
        jnp.sum(coef, axis=1, keepdims=True), (rows, LANES)
    ).astype(BF)


def pack_call(zs, blocks, step):
    count, width = sum(b.shape[0] for b in blocks), blocks[0].shape[1]
    rows = 8 * (count // step) * CAPACITY

    def body(*refs):
        pack_kernel(step, *refs)

    return pl.pallas_call(
        body,
        out_shape=jax.ShapeDtypeStruct((rows, width), BF),
        in_specs=[pl.BlockSpec(memory_space=pltpu.SMEM)] + [vmem()] * len(blocks),
        out_specs=vmem(),
        name="pack",
    )(zs, *blocks)


def homes(z, rows):
    row, place = iota((rows, rows), 0), iota((rows, rows), 1)
    quarter = rows // 4
    first, last = row < quarter, row >= 3 * quarter
    inside = jnp.where(first, row, jnp.where(last, row - 3 * quarter, row - quarter))
    zn = jnp.where(first | last, 4, 8)
    source = inside // (zn * CAPACITY)
    zi = (inside // CAPACITY) % zn
    turn = jnp.where(first, 0, jnp.where(last, 2, jnp.where(zi < 4, 3, 1)))
    zed = 4 * (zi % 4) + (z + turn) % 4
    home = ((zed // 8) * 64 + source * 8 + zed % 8) * CAPACITY + inside % CAPACITY
    return (home == place).astype(BF)


def rows_kernel(zs_ref, *refs):
    (a_ref, b_ref, c_ref, *w_refs), p_ref, refs = refs[:8], refs[8], refs[9:]
    d_refs, s_ref, (gu, dn, rows, d_all, sems) = refs[:4], refs[4], refs[5:]
    hid = dn.shape[1]
    count, width = rows.shape
    features = (width - LANES) // 2
    quarter = count // 4
    pairs = [
        (a_ref, rows.at[pl.ds(0, quarter)]),
        (b_ref, rows.at[pl.ds(quarter, 2 * quarter)]),
        (c_ref, rows.at[pl.ds(3 * quarter, quarter)]),
    ]
    for q in range(3):
        pairs.append((w_refs[q].at[pl.ds(0, 2 * hid)], gu.at[pl.ds(q * 2 * hid, 2 * hid)]))
        pairs.append((w_refs[q].at[pl.ds(2 * hid, hid)], dn.at[q]))
    top, first = w_refs[3].shape[0], 6 * hid
    pairs.append((w_refs[3], gu.at[pl.ds(first, top)]))
    pairs.append((w_refs[4].at[pl.ds(0, 2 * hid - top)], gu.at[pl.ds(first + top, 2 * hid - top)]))
    pairs.append((w_refs[4].at[pl.ds(2 * hid - top, hid)], dn.at[3]))
    copies = [pltpu.make_async_copy(s, t, sems.at[i]) for i, (s, t) in enumerate(pairs)]
    for copy in copies:
        copy.start()
    for copy in copies[:3]:
        copy.wait()
    home = homes(zs_ref[0] * 8 + zs_ref[1], count)
    coef = rows[:, 2 * features :].astype(F32).T[0:1, :]
    score = None
    for q in range(4):
        for copy in copies[3 + 2 * q : 5 + 2 * q + q // 3]:
            copy.wait()
        first = q * 2 * hid
        pre = dot(gu[first : first + 2 * hid, :], rows[:, :features], 1, 1)
        back = dot(dn[q], rows[:, features : 2 * features], 1, 1)
        gate_pre, up_pre = pre[:hid], pre[hid:]
        sigma = jax.nn.sigmoid(gate_pre)
        active = gate_pre * sigma
        hidden = active * up_pre
        part = jnp.sum(hidden.astype(BF).astype(F32) * back, axis=0, keepdims=True)
        score = part if score is None else score + part
        d_hidden = coef * back
        d_gate = d_hidden * up_pre * sigma * (1.0 + gate_pre * (1.0 - sigma))
        d_all[first : first + hid, :] = d_gate.astype(BF)
        d_all[first + hid : first + 2 * hid, :] = (d_hidden * active).astype(BF)
        if q == 0:
            d_refs[0][...] = d_all[: 2 * hid, :]
        else:
            size = d_refs[q].shape[0]
            for j in range(features // count):
                d_refs[q][:, j * count : (j + 1) * count] = d_all[
                    first + j * size : first + (j + 1) * size, :
                ]
        s_ref[q] = (coef * hidden).astype(BF)
    moved = dot(d_all[...], home, 1, 0).astype(BF)
    tile = 512
    for j in range(0, features, tile):
        p_ref[:, j : j + tile] = dot(moved, gu[:, j : j + tile], 0, 0).astype(BF)
    score = dot(jnp.broadcast_to(score, (LANES, count)).astype(BF), home, 1, 0)
    p_ref[:, features:] = score.T.astype(BF)


def rows_call(zs, chunks, weights):
    count = sum(c.shape[0] for c in chunks)
    width = chunks[0].shape[1]
    n, hid, features = 4, weights[0].shape[0] // 3, weights[0].shape[1]
    return pl.pallas_call(
        rows_kernel,
        out_shape=[
            jax.ShapeDtypeStruct((count, features + LANES), BF),
            jax.ShapeDtypeStruct((2 * hid, count), BF),
            *[jax.ShapeDtypeStruct((2 * hid * count // features, features), BF)] * (n - 1),
            jax.ShapeDtypeStruct((n, hid, count), BF),
        ],
        in_specs=[pl.BlockSpec(memory_space=pltpu.SMEM)] + [pl.BlockSpec(memory_space=pl.ANY)] * 8,
        out_specs=[vmem()] * (n + 2),
        scratch_shapes=[
            pltpu.VMEM((n * 2 * hid, features), BF),
            pltpu.VMEM((n, hid, features), BF),
            pltpu.VMEM((count, width), BF),
            pltpu.VMEM((n * 2 * hid, count), BF),
            pltpu.SemaphoreType.DMA((4 + 2 * n,)),
        ],
        compiler_params=pltpu.CompilerParams(vmem_limit_bytes=56 * MIB),
        cost_estimate=pl.CostEstimate(
            flops=2 * count * features * hid * n * 5,
            bytes_accessed=2 * features * hid * 12 + 6 * count * features,
            transcendentals=count * hid * n,
        ),
        name="rows",
    )(zs, *chunks, *weights)


def down_kernel(
    s_ref, a_ref, b_ref, c_ref, dl_ref, dr_ref, dt_ref, own_ref, go_ref, come_ref, right_ref, left_ref, rows
):
    quarter = a_ref.shape[0]
    rows[0:quarter, :] = a_ref[...]
    rows[quarter : 3 * quarter, :] = b_ref[...]
    rows[3 * quarter :, :] = c_ref[...]
    grads = rows[...]
    half = right_ref.shape[0]
    own_ref[...] = dot(s_ref[0], grads, 1, 0)
    left = dot(s_ref[1], grads, 1, 0).astype(BF)
    right = dot(s_ref[2], grads, 1, 0).astype(BF)
    two = dot(s_ref[3], grads, 1, 0).astype(BF)
    go_ref[:half, :] = two[:half]
    go_ref[half : 2 * half, :] = right[half:]
    end = 2 * half + dr_ref.shape[0]
    most = go_ref.shape[0] - end
    go_ref[2 * half : end, :] = dr_ref[...]
    go_ref[end:, :] = dt_ref[:most, :]
    come_ref[:half, :] = left[:half]
    come_ref[half : 2 * half, :] = two[half:]
    come_ref[2 * half : end, :] = dl_ref[...]
    come_ref[end:, :] = dt_ref[most:, :]
    right_ref[...] = right[:half]
    left_ref[...] = left[half:]


def down_call(scaled, chunks, d_left, d_right, d_two, features):
    tile = 512
    n, hid, count = scaled.shape
    first = features // tile
    tiled = [pl.BlockSpec((c.shape[0], tile), lambda j: (0, first + j)) for c in chunks]
    extra = d_left.shape[0]
    tiled += [pl.BlockSpec((extra, tile), lambda j: (0, j))] * 3
    sizes = [hid, hid + extra + 2 * extra // 3, hid + extra + extra // 3, hid // 2, hid // 2]
    return pl.pallas_call(
        down_kernel,
        grid=(features // tile,),
        out_shape=[jax.ShapeDtypeStruct((hid, features), F32)]
        + [jax.ShapeDtypeStruct((size, features), BF) for size in sizes[1:]],
        in_specs=[pl.BlockSpec(scaled.shape, lambda j: (0, 0, 0))] + tiled,
        out_specs=[pl.BlockSpec((size, tile), lambda j: (0, j)) for size in sizes],
        scratch_shapes=[pltpu.VMEM((count, tile), BF)],
        compiler_params=pltpu.CompilerParams(vmem_limit_bytes=24 * MIB),
        cost_estimate=pl.CostEstimate(
            flops=2 * n * count * features * hid,
            bytes_accessed=2 * features * (count + 5 * hid),
            transcendentals=0,
        ),
        name="down_parts",
    )(scaled, *chunks, d_left, d_right, d_two)


def weights_kernel(*refs):
    d_refs, x_refs, (gate_ref, up_ref, factors, rows) = refs[:5], refs[5:13], refs[13:]
    own, left, right, more_left, more_right, last, two_a, two_b = x_refs
    hid = gate_ref.shape[0]
    most, mid = own.shape[0], own.shape[0] // 2
    count, ends = rows.shape[1], last.shape[0]
    size = d_refs[1].shape[0]
    top = d_refs[3].shape[0]

    @pl.when(pl.program_id(0) == 0)
    def _():
        factors[0] = d_refs[0][...]
        for j in range(d_refs[1].shape[1] // count):
            part, at = slice(j * count, (j + 1) * count), j * size
            for q in (1, 2):
                factors[q, at : at + size, :] = d_refs[q][:, part]
            factors[3, at : at + top, :] = d_refs[3][:, part]
            factors[3, at + top : at + size, :] = d_refs[4][:, part]

    for q, (first, end) in enumerate(((own, last), (left, more_left), (right, more_right))):
        rows[q, :most, :] = first[...]
        rows[q, most:, :] = end[end.shape[0] - ends :, :]
    rows[3, :mid, :] = more_right[:mid, :]
    rows[3, mid:most, :] = more_left[:mid, :]
    rows[3, most : most + ends // 2, :] = two_a[two_a.shape[0] - ends // 2 :, :]
    rows[3, most + ends // 2 :, :] = two_b[two_b.shape[0] - ends // 2 :, :]
    total = sum(dot(factors[q], rows[q], 1, 0) for q in range(4)).astype(BF)
    gate_ref[...] = total[:hid]
    up_ref[...] = total[hid:]


def weights_call(d_own, from_left, from_right, two_a, two_b, half, xs):
    tile = 512
    n, (both, count), features = 4, d_own.shape, xs[0].shape[1]
    hid, size = both // 2, both * count // features
    top, low = 2 * size // 3, size // 3

    def piece(rows, first):
        return pl.BlockSpec((rows, features), lambda j: (first // rows, 0))

    packed = [piece(size, 2 * half), piece(size, 2 * half), piece(top, half), piece(low, half)]
    tiled = [pl.BlockSpec((x.shape[0], tile), lambda j: (0, j)) for x in [*xs, two_a, two_b]]
    return pl.pallas_call(
        weights_kernel,
        grid=(features // tile,),
        out_shape=[jax.ShapeDtypeStruct((hid, features), BF)] * 2,
        in_specs=[pl.BlockSpec(d_own.shape, lambda j: (0, 0)), *packed, *tiled],
        out_specs=[pl.BlockSpec((hid, tile), lambda j: (0, j))] * 2,
        scratch_shapes=[pltpu.VMEM((n, both, count), BF), pltpu.VMEM((n, count, tile), BF)],
        compiler_params=pltpu.CompilerParams(vmem_limit_bytes=24 * MIB),
        cost_estimate=pl.CostEstimate(
            flops=4 * n * count * features * hid,
            bytes_accessed=2 * features * (n * count + 2 * hid),
            transcendentals=0,
        ),
        name="weight_grads",
    )(d_own, from_left, from_right, two_a, two_b, *xs, two_a, two_b)


def home_kernel(code_ref, home_ref, grad_ref, score_ref):
    top, rows = code_ref.shape
    places = home_ref.shape[0]
    features = grad_ref.shape[1]
    wanted = (iota((places, rows), 0) + 1).astype(F32)
    hits = [jnp.where(wanted == code_ref[k : k + 1, :], 1.0, 0.0) for k in range(top)]
    score = home_ref[:, features : features + 1].astype(F32)
    score_ref[...] = jnp.concatenate(
        [jnp.sum(hit * score, axis=0, keepdims=True) for hit in hits], axis=0
    ).astype(BF)
    pick = sum(hits).astype(BF)
    grad_ref[...] = dot(pick, home_ref[:, :features], 0, 0).astype(BF)


def home_call(code, home, features):
    return pl.pallas_call(
        home_kernel,
        out_shape=[
            jax.ShapeDtypeStruct((code.shape[1], features), BF),
            jax.ShapeDtypeStruct(code.shape, BF),
        ],
        in_specs=[vmem()] * 2,
        out_specs=[vmem()] * 2,
        name="home",
    )(code, home)


def local(tokens, out_grad, expert_ids, keep_flags, route_weights, gate_w, up_w, down_w):
    nz, n = lax.axis_size(Z), lax.axis_size("x")
    step, features = tokens.shape
    zs = jnp.stack([lax.axis_index(a) for a in ("zh", ("zq", "zr"), "x")]).astype(jnp.int32)
    half = gate_w.shape[1] // 2

    joined = jnp.concatenate([gate_w[0], up_w[0], down_w[0]], axis=0)
    part = joined.shape[0] // 2
    w_left, w_right = shift(joined, 1, "x", n), shift(joined, -1, "x", n)
    own, code = payload_call(tokens, out_grad, expert_ids.T, keep_flags.T, route_weights.T)

    chunk = lax.all_gather(own, FAR, axis=0, tiled=True)
    left, right = shift(chunk, 1, Z, nz), shift(chunk, -1, Z, nz)

    def exchange(packed):
        rows, width = packed.shape
        return lax.all_to_all(
            packed.reshape(8, rows // 8, width), YC, split_axis=0, concat_axis=0, tiled=True
        ).reshape(rows, width)

    rows_a = exchange(pack_call(zs, [chunk], step))
    packed_b = pack_call(zs, [left, right], step)
    packed_b, w_left, w_right = lax.optimization_barrier((packed_b, w_left, w_right))
    w_a, w_b = shift(w_right[:part], -1, "x", n), shift(w_left[part:], 1, "x", n)
    rest_a = shift(right[: 2 * step], -1, Z, nz)
    rest_b = shift(left[2 * step :], 1, Z, nz)
    rest_a, rest_b, _ = lax.optimization_barrier((rest_a, rest_b, packed_b))
    packed_b, rows_a = lax.optimization_barrier((packed_b, rows_a))
    rows_b = exchange(packed_b)
    packed_c = pack_call(zs, [rest_a, rest_b], step)
    packed_c, rows_b = lax.optimization_barrier((packed_c, rows_b))
    rows_c = exchange(packed_c)

    chunks = [rows_a, rows_b, rows_c]
    back, d_own, d_left, d_right, d_two, scaled = rows_call(
        zs, chunks, [joined, w_left, w_right, w_a, w_b]
    )
    x_ab = jnp.concatenate([rows_a[:, :features], rows_b[:, :features]], axis=0)
    x_left, x_right = shift(x_ab, 1, "x", n), shift(x_ab, -1, "x", n)
    back, x_left, x_right = lax.optimization_barrier((back, x_left, x_right))
    home = lax.all_to_all(
        back.reshape(-1, CAPACITY, back.shape[1]), PLACE, split_axis=0, concat_axis=0, tiled=True
    ).reshape(back.shape)
    mid = x_ab.shape[0] // 2
    x_c = rows_c[:, :features]
    more_left = shift(jnp.concatenate([x_left[mid:], x_c], axis=0), 1, "x", n)
    more_right = shift(jnp.concatenate([x_right[:mid], x_c], axis=0), -1, "x", n)

    scaled, more_left, more_right = lax.optimization_barrier((scaled, more_left, more_right))
    p_own, p_go, p_come, p_right, p_left = down_call(
        scaled, chunks, d_left, d_right, d_two, features
    )
    from_left, from_right = shift(p_go, 1, "x", n), shift(p_come, -1, "x", n)
    passed = 2 * half + d_left.shape[0]
    last = x_c.shape[0] // 2
    p_right = (p_right.astype(F32) + from_left[:half].astype(F32)).astype(BF)
    p_left = (p_left.astype(F32) + from_right[half : 2 * half].astype(F32)).astype(BF)
    two_a = shift(
        jnp.concatenate([p_right, from_left[passed:], more_left[mid : mid + last]], axis=0),
        1, "x", n,
    )
    two_b = shift(
        jnp.concatenate([p_left, from_right[passed:], more_right[mid + last :]], axis=0),
        -1, "x", n,
    )
    grad_down = jnp.concatenate(
        [
            p_own[:half] + two_a[:half].astype(F32) + from_right[:half].astype(F32),
            p_own[half:] + from_left[half : 2 * half].astype(F32) + two_b[:half].astype(F32),
        ],
        axis=0,
    ).astype(BF)
    xs = [x_ab, x_left, x_right, more_left, more_right, x_c]
    grad_gate, grad_up = weights_call(d_own, from_left, from_right, two_a, two_b, half, xs)

    token_grad, slot_score = home_call(code, home, features)
    return (token_grad, slot_score.T, grad_gate[None], grad_up[None], grad_down[None])


def solution(mesh):
    fine = Mesh(mesh.devices.reshape(2, 4, 2, 2, 4, 4), (*PLACE, "x"))
    by_row = P((*PLACE, "x"), None)
    by_expert = P(PLACE, "x", None)
    return jax.shard_map(
        local,
        mesh=fine,
        in_specs=(by_row,) * 5 + (by_expert,) * 3,
        out_specs=(by_row,) * 2 + (by_expert,) * 3,
        check_vma=False,
    )
```

```python
import jax
import jax.numpy as jnp
from jax import lax
from jax.experimental import pallas as pl
from jax.experimental.pallas import tpu as pltpu
from jax.sharding import Mesh, PartitionSpec as P

BF = jnp.bfloat16
F32 = jnp.float32
LANES = 128
CAPACITY = 2
MIB = 1024 * 1024
FAR = ("zh", "zq")
Z = ("zh", "zq", "zr")
YC = ("y", "c")
PLACE = ("zh", "y", "c", "zq", "zr")


def dot(a, b, da, db):
    return lax.dot_general(a, b, (((da,), (db,)), ((), ())), preferred_element_type=F32)


def iota(shape, axis):
    return lax.broadcasted_iota(jnp.int32, shape, axis)


def shift(block, step, axes, n):
    return lax.ppermute(block, axes, [(i, (i + step) % n) for i in range(n)])


def vmem():
    return pl.BlockSpec(memory_space=pltpu.VMEM)


def payload_kernel(tok_ref, grad_ref, ids_ref, keep_ref, weight_ref, out_ref, code_ref):
    features = tok_ref.shape[1]
    top, rows = ids_ref.shape
    experts = LANES
    ids, kept = ids_ref[...], keep_ref[...] > 0
    names = iota((experts, rows), 0)
    named = [names == ids[k : k + 1, :] for k in range(top)]
    tally = sum(jnp.where(named[k] & kept[k : k + 1, :], 1.0, 0.0) for k in range(top))
    before = (iota((rows, rows), 0) < iota((rows, rows), 1)).astype(BF)
    earlier = dot(tally.astype(BF), before, 1, 0)
    position = jnp.concatenate(
        [jnp.sum(jnp.where(named[k], earlier, 0.0), axis=0, keepdims=True) for k in range(top)],
        axis=0,
    )
    code = jnp.where(kept, ids.astype(F32) * CAPACITY + position + 1.0, 0.0)
    code_ref[...] = code
    spread = (iota((rows, LANES), 0) == iota((rows, LANES), 1)).astype(BF)
    both = jnp.concatenate([code.astype(BF), weight_ref[...]], axis=0)
    out_ref[:, :features] = tok_ref[...]
    out_ref[:, features : 2 * features] = grad_ref[...]
    out_ref[:, 2 * features :] = dot(both, spread, 1, 0).astype(BF)


def payload_call(tokens, out_grad, ids, keep, weights):
    rows, features = tokens.shape
    return pl.pallas_call(
        payload_kernel,
        out_shape=[
            jax.ShapeDtypeStruct((rows, 2 * features + LANES), BF),
            jax.ShapeDtypeStruct(ids.shape, F32),
        ],
        in_specs=[vmem()] * 5,
        out_specs=[vmem()] * 2,
        name="payload",
    )(tokens, out_grad, ids, keep, weights)


def pack_kernel(step, zs_ref, *refs):
    blocks, out_ref = refs[:-1], refs[-1]
    count = sum(b.shape[0] for b in blocks)
    zn = count // step
    rows, width = out_ref.shape
    features = (width - LANES) // 2
    half = step // 2
    codes = jnp.zeros((half, count), F32)
    weights = jnp.zeros((half, count), F32)
    at = 0
    for block in blocks:
        for first in range(0, block.shape[0], step):
            place = (iota((LANES, count), 0) + at == iota((LANES, count), 1)) & (
                iota((LANES, count), 0) < step
            )
            both = dot(
                block[first : first + step, 2 * features :], place.astype(BF), 1, 0
            )
            codes = codes + both[:half]
            weights = weights + both[half:]
            at += step
    zh, zl = zs_ref[0], zs_ref[1]
    row, col = iota((rows, count), 0), iota((rows, count), 1)
    dest = row // (zn * CAPACITY)
    wanted = ((zh * 64 + dest * 8 + zl) * CAPACITY + row % CAPACITY + 1).astype(F32)
    wanted = jnp.where((row // CAPACITY) % zn == col // step, wanted, -1.0)
    pick = jnp.zeros((rows, count), F32)
    coef = jnp.zeros((rows, count), F32)
    for k in range(half):
        hit = wanted == codes[k : k + 1, :]
        pick = pick + jnp.where(hit, 1.0, 0.0)
        coef = coef + jnp.where(hit, weights[k : k + 1, :], 0.0)
    pick = pick.astype(BF)
    tile = 1024
    for j in range(0, 2 * features, tile):
        total, at = None, 0
        for block in blocks:
            size = block.shape[0]
            part = dot(pick[:, at : at + size], block[:, j : j + tile], 1, 0)
            total = part if total is None else total + part
            at += size
        out_ref[:, j : j + tile] = total.astype(BF)
    out_ref[:, 2 * features :] = jnp.broadcast_to(
        jnp.sum(coef, axis=1, keepdims=True), (rows, LANES)
    ).astype(BF)


def pack_call(zs, blocks, step):
    count, width = sum(b.shape[0] for b in blocks), blocks[0].shape[1]
    rows = 8 * (count // step) * CAPACITY

    def body(*refs):
        pack_kernel(step, *refs)

    return pl.pallas_call(
        body,
        out_shape=jax.ShapeDtypeStruct((rows, width), BF),
        in_specs=[pl.BlockSpec(memory_space=pltpu.SMEM)] + [vmem()] * len(blocks),
        out_specs=vmem(),
        name="pack",
    )(zs, *blocks)


def homes(z, rows):
    row, place = iota((rows, rows), 0), iota((rows, rows), 1)
    quarter = rows // 4
    first, last = row < quarter, row >= 3 * quarter
    inside = jnp.where(first, row, jnp.where(last, row - 3 * quarter, row - quarter))
    zn = jnp.where(first | last, 4, 8)
    source = inside // (zn * CAPACITY)
    zi = (inside // CAPACITY) % zn
    turn = jnp.where(first, 0, jnp.where(last, 2, jnp.where(zi < 4, 3, 1)))
    zed = 4 * (zi % 4) + (z + turn) % 4
    home = ((zed // 8) * 64 + source * 8 + zed % 8) * CAPACITY + inside % CAPACITY
    return (home == place).astype(BF)


def rows_kernel(zs_ref, *refs):
    (a_ref, b_ref, c_ref, *w_refs), refs = refs[:8], refs[8:]
    p_ref, d_ref, s_ref, go_ref, come_ref, right_ref, left_ref = refs[:7]
    gu, dn, rows, d_all, s_all, sems = refs[7:]
    hid = dn.shape[1]
    count, width = rows.shape
    features = (width - LANES) // 2
    quarter = count // 4
    pairs = [
        (a_ref, rows.at[pl.ds(0, quarter)]),
        (b_ref, rows.at[pl.ds(quarter, 2 * quarter)]),
        (c_ref, rows.at[pl.ds(3 * quarter, quarter)]),
    ]
    for q in range(3):
        pairs.append((w_refs[q].at[pl.ds(0, 2 * hid)], gu.at[pl.ds(q * 2 * hid, 2 * hid)]))
        pairs.append((w_refs[q].at[pl.ds(2 * hid, hid)], dn.at[q]))
    top, first = w_refs[3].shape[0], 6 * hid
    pairs.append((w_refs[3], gu.at[pl.ds(first, top)]))
    pairs.append((w_refs[4].at[pl.ds(0, 2 * hid - top)], gu.at[pl.ds(first + top, 2 * hid - top)]))
    pairs.append((w_refs[4].at[pl.ds(2 * hid - top, hid)], dn.at[3]))
    copies = [pltpu.make_async_copy(s, t, sems.at[i]) for i, (s, t) in enumerate(pairs)]
    for copy in copies:
        copy.start()
    for copy in copies[:3]:
        copy.wait()
    home = homes(zs_ref[0] * 8 + zs_ref[1], count)
    coef = rows[:, 2 * features :].astype(F32).T[0:1, :]
    score = None
    for q in range(4):
        for copy in copies[3 + 2 * q : 5 + 2 * q + q // 3]:
            copy.wait()
        first = q * 2 * hid
        pre = dot(gu[first : first + 2 * hid, :], rows[:, :features], 1, 1)
        back = dot(dn[q], rows[:, features : 2 * features], 1, 1)
        gate_pre, up_pre = pre[:hid], pre[hid:]
        sigma = jax.nn.sigmoid(gate_pre)
        active = gate_pre * sigma
        hidden = active * up_pre
        part = jnp.sum(hidden.astype(BF).astype(F32) * back, axis=0, keepdims=True)
        score = part if score is None else score + part
        d_hidden = coef * back
        d_gate = d_hidden * up_pre * sigma * (1.0 + gate_pre * (1.0 - sigma))
        d_all[first : first + hid, :] = d_gate.astype(BF)
        d_all[first + hid : first + 2 * hid, :] = (d_hidden * active).astype(BF)
        s_all[q] = (coef * hidden).astype(BF)
    moved = dot(d_all[...], home, 1, 0).astype(BF)
    tile = 512
    for j in range(0, features, tile):
        p_ref[:, j : j + tile] = dot(moved, gu[:, j : j + tile], 0, 0).astype(BF)
    score = dot(jnp.broadcast_to(score, (LANES, count)).astype(BF), home, 1, 0)
    p_ref[:, features:] = score.T.astype(BF)
    d_ref[...] = d_all[: 2 * hid, :]
    s_ref[...] = s_all[0]
    half, size = hid // 2, 2 * hid * count // features
    most, end = 2 * size // 3, hid + size
    for j in range(features // count):
        part, at = slice(j * count, (j + 1) * count), j * size
        left, right, two = 2 * hid + at, 4 * hid + at, 6 * hid + at
        come_ref[hid:end, part] = d_all[left : left + size, :]
        go_ref[hid:end, part] = d_all[right : right + size, :]
        go_ref[end : end + most, part] = d_all[two : two + most, :]
        come_ref[end : end + size - most, part] = d_all[two + most : two + size, :]
    go_ref[end + most :, :] = rows[3 * quarter :, :features]
    come_ref[end + size - most :, :] = rows[3 * quarter :, :features]
    for j in range(0, features, tile):
        part = slice(j, j + tile)
        grads = rows[:, features + j : features + j + tile]
        left, right, two = [dot(s_all[q], grads, 1, 0).astype(BF) for q in (1, 2, 3)]
        go_ref[:half, part] = two[:half]
        go_ref[half:hid, part] = right[half:]
        come_ref[:half, part] = left[:half]
        come_ref[half:hid, part] = two[half:]
        right_ref[:, part] = right[:half]
        left_ref[:, part] = left[half:]


def rows_call(zs, chunks, weights):
    count = sum(c.shape[0] for c in chunks)
    width = chunks[0].shape[1]
    n, hid, features = 4, weights[0].shape[0] // 3, weights[0].shape[1]
    size, last = 2 * hid * count // features, count // 4
    fixed = hid + size + last
    return pl.pallas_call(
        rows_kernel,
        out_shape=[
            jax.ShapeDtypeStruct((count, features + LANES), BF),
            jax.ShapeDtypeStruct((2 * hid, count), BF),
            jax.ShapeDtypeStruct((hid, count), BF),
            jax.ShapeDtypeStruct((fixed + 2 * size // 3, features), BF),
            jax.ShapeDtypeStruct((fixed + size // 3, features), BF),
            jax.ShapeDtypeStruct((hid // 2, features), BF),
            jax.ShapeDtypeStruct((hid // 2, features), BF),
        ],
        in_specs=[pl.BlockSpec(memory_space=pltpu.SMEM)] + [pl.BlockSpec(memory_space=pl.ANY)] * 8,
        out_specs=[vmem()] * 7,
        scratch_shapes=[
            pltpu.VMEM((n * 2 * hid, features), BF),
            pltpu.VMEM((n, hid, features), BF),
            pltpu.VMEM((count, width), BF),
            pltpu.VMEM((n * 2 * hid, count), BF),
            pltpu.VMEM((n, hid, count), BF),
            pltpu.SemaphoreType.DMA((4 + 2 * n,)),
        ],
        compiler_params=pltpu.CompilerParams(vmem_limit_bytes=56 * MIB),
        cost_estimate=pl.CostEstimate(
            flops=2 * count * features * hid * n * 5,
            bytes_accessed=2 * features * hid * 12 + 6 * count * features,
            transcendentals=count * hid * n,
        ),
        name="rows",
    )(zs, *chunks, *weights)


def weights_kernel(*refs):
    s_ref, d_refs, g_refs, x_refs = refs[0], refs[1:6], refs[6:9], refs[9:17]
    gate_ref, up_ref, down_ref, factors, rows, grads = refs[17:]
    own, left, right, last, from_left, from_right, two_a, two_b = x_refs
    hid = gate_ref.shape[0]
    most, half, ends = own.shape[0], hid // 2, last.shape[0]
    mid, cut = most // 2, ends // 2
    count = rows.shape[1]
    size, top = d_refs[1].shape[0], d_refs[3].shape[0]

    @pl.when(pl.program_id(0) == 0)
    def _():
        factors[0] = d_refs[0][...]
        for j in range(d_refs[1].shape[1] // count):
            part, at = slice(j * count, (j + 1) * count), j * size
            for q in (1, 2):
                factors[q, at : at + size, :] = d_refs[q][:, part]
            factors[3, at : at + top, :] = d_refs[3][:, part]
            factors[3, at + top : at + size, :] = d_refs[4][:, part]

    for q, (first, end) in enumerate(((own, last), (left, from_left), (right, from_right))):
        rows[q, :most, :] = first[...]
        rows[q, most:, :] = end[end.shape[0] - ends :, :]
    far_a, far_b = half + top, half + size - top
    rows[3, :mid, :] = two_b[far_b : far_b + mid, :]
    rows[3, mid:most, :] = two_a[far_a : far_a + mid, :]
    rows[3, most : most + cut, :] = two_a[far_a + mid :, :]
    rows[3, most + cut :, :] = two_b[far_b + mid :, :]
    total = sum(dot(factors[q], rows[q], 1, 0) for q in range(4)).astype(BF)
    gate_ref[...] = total[:hid]
    up_ref[...] = total[hid:]

    at = 0
    for ref in g_refs:
        grads[at : at + ref.shape[0], :] = ref[...]
        at += ref.shape[0]
    down = dot(s_ref[...], grads[...], 1, 0)
    upper = two_a[:half, :].astype(F32) + from_right[:half, :].astype(F32)
    lower = from_left[half:hid, :].astype(F32) + two_b[:half, :].astype(F32)
    down_ref[:half, :] = (down[:half] + upper).astype(BF)
    down_ref[half:, :] = (down[half:] + lower).astype(BF)


def weights_call(scaled, d_own, chunks, x_ab, x_left, x_right, x_c, messages):
    tile = 512
    from_left, from_right, two_a, two_b = messages
    n, (both, count), features = 4, d_own.shape, x_ab.shape[1]
    hid, size = both // 2, both * count // features
    top, low = 2 * size // 3, size // 3

    def piece(rows, first):
        return pl.BlockSpec((rows, features), lambda j: (first // rows, 0))

    packed = [piece(size, hid), piece(size, hid), piece(top, hid // 2), piece(low, hid // 2)]
    skip = features // tile
    grads = [pl.BlockSpec((c.shape[0], tile), lambda j: (0, skip + j)) for c in chunks]
    tiled = [x_ab, x_left, x_right, x_c, *messages]
    return pl.pallas_call(
        weights_kernel,
        grid=(features // tile,),
        out_shape=[jax.ShapeDtypeStruct((hid, features), BF)] * 3,
        in_specs=[
            pl.BlockSpec(scaled.shape, lambda j: (0, 0)),
            pl.BlockSpec(d_own.shape, lambda j: (0, 0)),
            *packed,
            *grads,
            *[pl.BlockSpec((x.shape[0], tile), lambda j: (0, j)) for x in tiled],
        ],
        out_specs=[pl.BlockSpec((hid, tile), lambda j: (0, j))] * 3,
        scratch_shapes=[
            pltpu.VMEM((n, both, count), BF),
            pltpu.VMEM((n, count, tile), BF),
            pltpu.VMEM((count, tile), BF),
        ],
        compiler_params=pltpu.CompilerParams(vmem_limit_bytes=32 * MIB),
        cost_estimate=pl.CostEstimate(
            flops=40 * n * count * features * hid,
            bytes_accessed=2 * features * (2 * n * count + 3 * hid),
            transcendentals=0,
        ),
        name="weight_grads",
    )(scaled, d_own, *messages, *chunks, *tiled)


def home_kernel(code_ref, home_ref, grad_ref, score_ref):
    top, rows = code_ref.shape
    places = home_ref.shape[0]
    features = grad_ref.shape[1]
    wanted = (iota((places, rows), 0) + 1).astype(F32)
    hits = [jnp.where(wanted == code_ref[k : k + 1, :], 1.0, 0.0) for k in range(top)]
    score = home_ref[:, features : features + 1].astype(F32)
    score_ref[...] = jnp.concatenate(
        [jnp.sum(hit * score, axis=0, keepdims=True) for hit in hits], axis=0
    ).astype(BF)
    pick = sum(hits).astype(BF)
    grad_ref[...] = dot(pick, home_ref[:, :features], 0, 0).astype(BF)


def home_call(code, home, features):
    return pl.pallas_call(
        home_kernel,
        out_shape=[
            jax.ShapeDtypeStruct((code.shape[1], features), BF),
            jax.ShapeDtypeStruct(code.shape, BF),
        ],
        in_specs=[vmem()] * 2,
        out_specs=[vmem()] * 2,
        name="home",
    )(code, home)


def local(tokens, out_grad, expert_ids, keep_flags, route_weights, gate_w, up_w, down_w):
    nz, n = lax.axis_size(Z), lax.axis_size("x")
    step, features = tokens.shape
    zs = jnp.stack([lax.axis_index(a) for a in ("zh", ("zq", "zr"), "x")]).astype(jnp.int32)
    half = gate_w.shape[1] // 2

    joined = jnp.concatenate([gate_w[0], up_w[0], down_w[0]], axis=0)
    part = joined.shape[0] // 2
    w_left, w_right = shift(joined, 1, "x", n), shift(joined, -1, "x", n)
    own, code = payload_call(tokens, out_grad, expert_ids.T, keep_flags.T, route_weights.T)

    chunk = lax.all_gather(own, FAR, axis=0, tiled=True)
    left, right = shift(chunk, 1, Z, nz), shift(chunk, -1, Z, nz)

    def exchange(packed):
        rows, width = packed.shape
        return lax.all_to_all(
            packed.reshape(8, rows // 8, width), YC, split_axis=0, concat_axis=0, tiled=True
        ).reshape(rows, width)

    rows_a = exchange(pack_call(zs, [chunk], step))
    packed_b = pack_call(zs, [left, right], step)
    packed_b, w_left, w_right = lax.optimization_barrier((packed_b, w_left, w_right))
    w_a, w_b = shift(w_right[:part], -1, "x", n), shift(w_left[part:], 1, "x", n)
    rest_a = shift(right[: 2 * step], -1, Z, nz)
    rest_b = shift(left[2 * step :], 1, Z, nz)
    rest_a, rest_b, _ = lax.optimization_barrier((rest_a, rest_b, packed_b))
    packed_b, rows_a = lax.optimization_barrier((packed_b, rows_a))
    rows_b = exchange(packed_b)
    packed_c = pack_call(zs, [rest_a, rest_b], step)
    packed_c, rows_b = lax.optimization_barrier((packed_c, rows_b))
    rows_c = exchange(packed_c)

    chunks = [rows_a, rows_b, rows_c]
    back, d_own, scaled, go, come, p_right, p_left = rows_call(
        zs, chunks, [joined, w_left, w_right, w_a, w_b]
    )
    x_ab = jnp.concatenate([rows_a[:, :features], rows_b[:, :features]], axis=0)
    x_left, x_right = shift(x_ab, 1, "x", n), shift(x_ab, -1, "x", n)
    go, come, x_left, x_right = lax.optimization_barrier((go, come, x_left, x_right))
    home = lax.all_to_all(
        back.reshape(-1, CAPACITY, back.shape[1]), PLACE, split_axis=0, concat_axis=0, tiled=True
    ).reshape(back.shape)

    from_left, from_right = shift(go, 1, "x", n), shift(come, -1, "x", n)
    hid, mid, cut = 2 * half, x_ab.shape[0] // 2, rows_c.shape[0] // 2
    at = hid + d_own.size // go.shape[1]
    end_a, end_b = go.shape[0] - 2 * cut, come.shape[0] - 2 * cut
    two_a = shift(
        jnp.concatenate(
            [
                (p_right.astype(F32) + from_left[:half].astype(F32)).astype(BF),
                from_left[at:end_a],
                x_left[mid:],
                from_left[end_a : end_a + cut],
            ],
            axis=0,
        ),
        1, "x", n,
    )
    two_b = shift(
        jnp.concatenate(
            [
                (p_left.astype(F32) + from_right[half:hid].astype(F32)).astype(BF),
                from_right[at:end_b],
                x_right[:mid],
                from_right[end_b + cut :],
            ],
            axis=0,
        ),
        -1, "x", n,
    )
    grad_gate, grad_up, grad_down = weights_call(
        scaled, d_own, chunks, x_ab, x_left, x_right, rows_c[:, :features],
        [from_left, from_right, two_a, two_b],
    )

    token_grad, slot_score = home_call(code, home, features)
    return (token_grad, slot_score.T, grad_gate[None], grad_up[None], grad_down[None])


def solution(mesh):
    fine = Mesh(mesh.devices.reshape(2, 4, 2, 2, 4, 4), (*PLACE, "x"))
    by_row = P((*PLACE, "x"), None)
    by_expert = P(PLACE, "x", None)
    return jax.shard_map(
        local,
        mesh=fine,
        in_specs=(by_row,) * 5 + (by_expert,) * 3,
        out_specs=(by_row,) * 2 + (by_expert,) * 3,
        check_vma=False,
    )
```

```python
import jax
import jax.numpy as jnp
from jax import lax
from jax.experimental import pallas as pl
from jax.experimental.pallas import tpu as pltpu
from jax.sharding import Mesh, PartitionSpec as P

BF = jnp.bfloat16
F32 = jnp.float32
LANES = 128
CAPACITY = 2
MIB = 1024 * 1024
FAR = ("zh", "zq")
Z = ("zh", "zq", "zr")
YC = ("y", "c")
PLACE = ("zh", "y", "c", "zq", "zr")


def dot(a, b, da, db):
    return lax.dot_general(a, b, (((da,), (db,)), ((), ())), preferred_element_type=F32)


def iota(shape, axis):
    return lax.broadcasted_iota(jnp.int32, shape, axis)


def shift(block, step, axes, n):
    return lax.ppermute(block, axes, [(i, (i + step) % n) for i in range(n)])


def vmem():
    return pl.BlockSpec(memory_space=pltpu.VMEM)


def payload_kernel(tok_ref, grad_ref, ids_ref, keep_ref, weight_ref, out_ref, code_ref):
    features = tok_ref.shape[1]
    top, rows = ids_ref.shape
    experts = LANES
    ids, kept = ids_ref[...], keep_ref[...] > 0
    names = iota((experts, rows), 0)
    named = [names == ids[k : k + 1, :] for k in range(top)]
    tally = sum(jnp.where(named[k] & kept[k : k + 1, :], 1.0, 0.0) for k in range(top))
    before = (iota((rows, rows), 0) < iota((rows, rows), 1)).astype(BF)
    earlier = dot(tally.astype(BF), before, 1, 0)
    position = jnp.concatenate(
        [jnp.sum(jnp.where(named[k], earlier, 0.0), axis=0, keepdims=True) for k in range(top)],
        axis=0,
    )
    code = jnp.where(kept, ids.astype(F32) * CAPACITY + position + 1.0, 0.0)
    code_ref[...] = code
    spread = (iota((rows, LANES), 0) == iota((rows, LANES), 1)).astype(BF)
    both = jnp.concatenate([code.astype(BF), weight_ref[...]], axis=0)
    out_ref[:, :features] = tok_ref[...]
    out_ref[:, features : 2 * features] = grad_ref[...]
    out_ref[:, 2 * features :] = dot(both, spread, 1, 0).astype(BF)


def payload_call(tokens, out_grad, ids, keep, weights):
    rows, features = tokens.shape
    return pl.pallas_call(
        payload_kernel,
        out_shape=[
            jax.ShapeDtypeStruct((rows, 2 * features + LANES), BF),
            jax.ShapeDtypeStruct(ids.shape, F32),
        ],
        in_specs=[vmem()] * 5,
        out_specs=[vmem()] * 2,
        name="payload",
    )(tokens, out_grad, ids, keep, weights)


def pack_kernel(step, zs_ref, *refs):
    blocks, out_ref = refs[:-1], refs[-1]
    count = sum(b.shape[0] for b in blocks)
    zn = count // step
    rows, width = out_ref.shape
    features = (width - LANES) // 2
    half = step // 2
    codes = jnp.zeros((half, count), F32)
    weights = jnp.zeros((half, count), F32)
    at = 0
    for block in blocks:
        for first in range(0, block.shape[0], step):
            place = (iota((LANES, count), 0) + at == iota((LANES, count), 1)) & (
                iota((LANES, count), 0) < step
            )
            both = dot(
                block[first : first + step, 2 * features :], place.astype(BF), 1, 0
            )
            codes = codes + both[:half]
            weights = weights + both[half:]
            at += step
    zh, zl = zs_ref[0], zs_ref[1]
    row, col = iota((rows, count), 0), iota((rows, count), 1)
    dest = row // (zn * CAPACITY)
    wanted = ((zh * 64 + dest * 8 + zl) * CAPACITY + row % CAPACITY + 1).astype(F32)
    wanted = jnp.where((row // CAPACITY) % zn == col // step, wanted, -1.0)
    pick = jnp.zeros((rows, count), F32)
    coef = jnp.zeros((rows, count), F32)
    for k in range(half):
        hit = wanted == codes[k : k + 1, :]
        pick = pick + jnp.where(hit, 1.0, 0.0)
        coef = coef + jnp.where(hit, weights[k : k + 1, :], 0.0)
    pick = pick.astype(BF)
    tile = 1024
    for j in range(0, 2 * features, tile):
        total, at = None, 0
        for block in blocks:
            size = block.shape[0]
            part = dot(pick[:, at : at + size], block[:, j : j + tile], 1, 0)
            total = part if total is None else total + part
            at += size
        out_ref[:, j : j + tile] = total.astype(BF)
    out_ref[:, 2 * features :] = jnp.broadcast_to(
        jnp.sum(coef, axis=1, keepdims=True), (rows, LANES)
    ).astype(BF)


def pack_call(zs, blocks, step):
    count, width = sum(b.shape[0] for b in blocks), blocks[0].shape[1]
    rows = 8 * (count // step) * CAPACITY

    def body(*refs):
        pack_kernel(step, *refs)

    return pl.pallas_call(
        body,
        out_shape=jax.ShapeDtypeStruct((rows, width), BF),
        in_specs=[pl.BlockSpec(memory_space=pltpu.SMEM)] + [vmem()] * len(blocks),
        out_specs=vmem(),
        name="pack",
    )(zs, *blocks)


def halves_kernel(*refs):
    n = len(refs) // 2
    sources, targets, sems = refs[:n], refs[n : 2 * n], refs[-1]
    copies = []
    for i, (source, target) in enumerate(zip(sources, targets)):
        size = target.shape[0]
        first = size if i % 2 == 0 else 0
        copies.append(pltpu.make_async_copy(source.at[pl.ds(first, size)], target, sems.at[i]))
    for copy in copies:
        copy.start()
    for copy in copies:
        copy.wait()


def halves_call(*blocks):
    return pl.pallas_call(
        halves_kernel,
        out_shape=[jax.ShapeDtypeStruct((b.shape[0] // 2, b.shape[1]), BF) for b in blocks],
        in_specs=[pl.BlockSpec(memory_space=pl.ANY)] * len(blocks),
        out_specs=[pl.BlockSpec(memory_space=pl.ANY)] * len(blocks),
        scratch_shapes=[pltpu.SemaphoreType.DMA((len(blocks),))],
        cost_estimate=pl.CostEstimate(
            flops=0, bytes_accessed=2 * sum(b.size for b in blocks), transcendentals=0
        ),
        name="halves",
    )(*blocks)


def homes(z, rows):
    row, place = iota((rows, rows), 0), iota((rows, rows), 1)
    quarter = rows // 4
    first, last = row < quarter, row >= 3 * quarter
    inside = jnp.where(first, row, jnp.where(last, row - 3 * quarter, row - quarter))
    zn = jnp.where(first | last, 4, 8)
    source = inside // (zn * CAPACITY)
    zi = (inside // CAPACITY) % zn
    turn = jnp.where(first, 0, jnp.where(last, 2, jnp.where(zi < 4, 3, 1)))
    zed = 4 * (zi % 4) + (z + turn) % 4
    home = ((zed // 8) * 64 + source * 8 + zed % 8) * CAPACITY + inside % CAPACITY
    return (home == place).astype(BF)


def rows_kernel(zs_ref, *refs):
    (a_ref, b_ref, c_ref, *w_refs), refs = refs[:8], refs[8:]
    p_ref, d_ref, s_ref, go_ref, come_ref, right_ref, left_ref = refs[:7]
    gu, dn, rows, d_all, s_all, sems = refs[7:]
    hid = dn.shape[1]
    count, width = rows.shape
    features = (width - LANES) // 2
    quarter = count // 4
    pairs = [
        (a_ref, rows.at[pl.ds(0, quarter)]),
        (b_ref, rows.at[pl.ds(quarter, 2 * quarter)]),
        (c_ref, rows.at[pl.ds(3 * quarter, quarter)]),
    ]
    for q in range(3):
        pairs.append((w_refs[q].at[pl.ds(0, 2 * hid)], gu.at[pl.ds(q * 2 * hid, 2 * hid)]))
        pairs.append((w_refs[q].at[pl.ds(2 * hid, hid)], dn.at[q]))
    top, first = w_refs[3].shape[0], 6 * hid
    pairs.append((w_refs[3], gu.at[pl.ds(first, top)]))
    pairs.append((w_refs[4].at[pl.ds(0, 2 * hid - top)], gu.at[pl.ds(first + top, 2 * hid - top)]))
    pairs.append((w_refs[4].at[pl.ds(2 * hid - top, hid)], dn.at[3]))
    copies = [pltpu.make_async_copy(s, t, sems.at[i]) for i, (s, t) in enumerate(pairs)]
    for copy in copies:
        copy.start()
    for copy in copies[:3]:
        copy.wait()
    home = homes(zs_ref[0] * 8 + zs_ref[1], count)
    coef = rows[:, 2 * features :].astype(F32).T[0:1, :]
    score = None
    for q in range(4):
        for copy in copies[3 + 2 * q : 5 + 2 * q + q // 3]:
            copy.wait()
        first = q * 2 * hid
        pre = dot(gu[first : first + 2 * hid, :], rows[:, :features], 1, 1)
        back = dot(dn[q], rows[:, features : 2 * features], 1, 1)
        gate_pre, up_pre = pre[:hid], pre[hid:]
        sigma = jax.nn.sigmoid(gate_pre)
        active = gate_pre * sigma
        hidden = active * up_pre
        part = jnp.sum(hidden.astype(BF).astype(F32) * back, axis=0, keepdims=True)
        score = part if score is None else score + part
        d_hidden = coef * back
        d_gate = d_hidden * up_pre * sigma * (1.0 + gate_pre * (1.0 - sigma))
        d_all[first : first + hid, :] = d_gate.astype(BF)
        d_all[first + hid : first + 2 * hid, :] = (d_hidden * active).astype(BF)
        s_all[q] = (coef * hidden).astype(BF)
    moved = dot(d_all[...], home, 1, 0).astype(BF)
    tile = 512
    for j in range(0, features, tile):
        p_ref[:, j : j + tile] = dot(moved, gu[:, j : j + tile], 0, 0).astype(BF)
    score = dot(jnp.broadcast_to(score, (LANES, count)).astype(BF), home, 1, 0)
    p_ref[:, features:] = score.T.astype(BF)
    d_ref[...] = d_all[: 2 * hid, :]
    s_ref[...] = s_all[0]
    half, size = hid // 2, 2 * hid * count // features
    most, end = 2 * size // 3, hid + size
    for j in range(features // count):
        part, at = slice(j * count, (j + 1) * count), j * size
        left, right, two = 2 * hid + at, 4 * hid + at, 6 * hid + at
        come_ref[hid:end, part] = d_all[left : left + size, :]
        go_ref[hid:end, part] = d_all[right : right + size, :]
        go_ref[end : end + most, part] = d_all[two : two + most, :]
        come_ref[end : end + size - most, part] = d_all[two + most : two + size, :]
    go_ref[end + most :, :] = rows[3 * quarter :, :features]
    come_ref[end + size - most :, :] = rows[3 * quarter :, :features]
    for j in range(0, features, tile):
        part = slice(j, j + tile)
        grads = rows[:, features + j : features + j + tile]
        left, right, two = [dot(s_all[q], grads, 1, 0).astype(BF) for q in (1, 2, 3)]
        go_ref[:half, part] = two[:half]
        go_ref[half:hid, part] = right[half:]
        come_ref[:half, part] = left[:half]
        come_ref[half:hid, part] = two[half:]
        right_ref[:, part] = right[:half]
        left_ref[:, part] = left[half:]


def rows_call(zs, chunks, weights):
    count = sum(c.shape[0] for c in chunks)
    width = chunks[0].shape[1]
    n, hid, features = 4, weights[0].shape[0] // 3, weights[0].shape[1]
    size, last = 2 * hid * count // features, count // 4
    fixed = hid + size + last
    return pl.pallas_call(
        rows_kernel,
        out_shape=[
            jax.ShapeDtypeStruct((count, features + LANES), BF),
            jax.ShapeDtypeStruct((2 * hid, count), BF),
            jax.ShapeDtypeStruct((hid, count), BF),
            jax.ShapeDtypeStruct((fixed + 2 * size // 3, features), BF),
            jax.ShapeDtypeStruct((fixed + size // 3, features), BF),
            jax.ShapeDtypeStruct((hid // 2, features), BF),
            jax.ShapeDtypeStruct((hid // 2, features), BF),
        ],
        in_specs=[pl.BlockSpec(memory_space=pltpu.SMEM)] + [pl.BlockSpec(memory_space=pl.ANY)] * 8,
        out_specs=[vmem()] * 7,
        scratch_shapes=[
            pltpu.VMEM((n * 2 * hid, features), BF),
            pltpu.VMEM((n, hid, features), BF),
            pltpu.VMEM((count, width), BF),
            pltpu.VMEM((n * 2 * hid, count), BF),
            pltpu.VMEM((n, hid, count), BF),
            pltpu.SemaphoreType.DMA((4 + 2 * n,)),
        ],
        compiler_params=pltpu.CompilerParams(vmem_limit_bytes=56 * MIB),
        cost_estimate=pl.CostEstimate(
            flops=2 * count * features * hid * n * 5,
            bytes_accessed=2 * features * hid * 12 + 6 * count * features,
            transcendentals=count * hid * n,
        ),
        name="rows",
    )(zs, *chunks, *weights)


def weights_kernel(*refs):
    s_ref, d_refs, g_refs, x_refs = refs[0], refs[1:6], refs[6:9], refs[9:17]
    gate_ref, up_ref, down_ref, factors, rows, grads = refs[17:]
    own, left, right, last, from_left, from_right, two_a, two_b = x_refs
    hid = gate_ref.shape[0]
    most, half, ends = own.shape[0], hid // 2, last.shape[0]
    mid, cut = most // 2, ends // 2
    count = rows.shape[1]
    size, top = d_refs[1].shape[0], d_refs[3].shape[0]

    @pl.when(pl.program_id(0) == 0)
    def _():
        factors[0] = d_refs[0][...]
        for j in range(d_refs[1].shape[1] // count):
            part, at = slice(j * count, (j + 1) * count), j * size
            for q in (1, 2):
                factors[q, at : at + size, :] = d_refs[q][:, part]
            factors[3, at : at + top, :] = d_refs[3][:, part]
            factors[3, at + top : at + size, :] = d_refs[4][:, part]

    for q, (first, end) in enumerate(((own, last), (left, from_left), (right, from_right))):
        rows[q, :most, :] = first[...]
        rows[q, most:, :] = end[end.shape[0] - ends :, :]
    far_a, far_b = half + top, half + size - top
    rows[3, :mid, :] = two_b[far_b : far_b + mid, :]
    rows[3, mid:most, :] = two_a[far_a : far_a + mid, :]
    rows[3, most : most + cut, :] = two_a[far_a + mid :, :]
    rows[3, most + cut :, :] = two_b[far_b + mid :, :]
    total = sum(dot(factors[q], rows[q], 1, 0) for q in range(4)).astype(BF)
    gate_ref[...] = total[:hid]
    up_ref[...] = total[hid:]

    at = 0
    for ref in g_refs:
        grads[at : at + ref.shape[0], :] = ref[...]
        at += ref.shape[0]
    down = dot(s_ref[...], grads[...], 1, 0)
    upper = two_a[:half, :].astype(F32) + from_right[:half, :].astype(F32)
    lower = from_left[half:hid, :].astype(F32) + two_b[:half, :].astype(F32)
    down_ref[:half, :] = (down[:half] + upper).astype(BF)
    down_ref[half:, :] = (down[half:] + lower).astype(BF)


def weights_call(scaled, d_own, chunks, x_ab, x_left, x_right, x_c, messages):
    tile = 512
    from_left, from_right, two_a, two_b = messages
    n, (both, count), features = 4, d_own.shape, x_ab.shape[1]
    hid, size = both // 2, both * count // features
    top, low = 2 * size // 3, size // 3

    def piece(rows, first):
        return pl.BlockSpec((rows, features), lambda j: (first // rows, 0))

    packed = [piece(size, hid), piece(size, hid), piece(top, hid // 2), piece(low, hid // 2)]
    skip = features // tile
    grads = [pl.BlockSpec((c.shape[0], tile), lambda j: (0, skip + j)) for c in chunks]
    tiled = [x_ab, x_left, x_right, x_c, *messages]
    return pl.pallas_call(
        weights_kernel,
        grid=(features // tile,),
        out_shape=[jax.ShapeDtypeStruct((hid, features), BF)] * 3,
        in_specs=[
            pl.BlockSpec(scaled.shape, lambda j: (0, 0)),
            pl.BlockSpec(d_own.shape, lambda j: (0, 0)),
            *packed,
            *grads,
            *[pl.BlockSpec((x.shape[0], tile), lambda j: (0, j)) for x in tiled],
        ],
        out_specs=[pl.BlockSpec((hid, tile), lambda j: (0, j))] * 3,
        scratch_shapes=[
            pltpu.VMEM((n, both, count), BF),
            pltpu.VMEM((n, count, tile), BF),
            pltpu.VMEM((count, tile), BF),
        ],
        compiler_params=pltpu.CompilerParams(vmem_limit_bytes=32 * MIB),
        cost_estimate=pl.CostEstimate(
            flops=40 * n * count * features * hid,
            bytes_accessed=2 * features * (2 * n * count + 3 * hid),
            transcendentals=0,
        ),
        name="weight_grads",
    )(scaled, d_own, *messages, *chunks, *tiled)


def home_kernel(code_ref, home_ref, grad_ref, score_ref):
    top, rows = code_ref.shape
    places = home_ref.shape[0]
    features = grad_ref.shape[1]
    wanted = (iota((places, rows), 0) + 1).astype(F32)
    hits = [jnp.where(wanted == code_ref[k : k + 1, :], 1.0, 0.0) for k in range(top)]
    score = home_ref[:, features : features + 1].astype(F32)
    score_ref[...] = jnp.concatenate(
        [jnp.sum(hit * score, axis=0, keepdims=True) for hit in hits], axis=0
    ).astype(BF)
    pick = sum(hits).astype(BF)
    grad_ref[...] = dot(pick, home_ref[:, :features], 0, 0).astype(BF)


def home_call(code, home, features):
    return pl.pallas_call(
        home_kernel,
        out_shape=[
            jax.ShapeDtypeStruct((code.shape[1], features), BF),
            jax.ShapeDtypeStruct(code.shape, BF),
        ],
        in_specs=[vmem()] * 2,
        out_specs=[vmem()] * 2,
        name="home",
    )(code, home)


def local(tokens, out_grad, expert_ids, keep_flags, route_weights, gate_w, up_w, down_w):
    nz, n = lax.axis_size(Z), lax.axis_size("x")
    step, features = tokens.shape
    zs = jnp.stack([lax.axis_index(a) for a in ("zh", ("zq", "zr"), "x")]).astype(jnp.int32)
    half = gate_w.shape[1] // 2

    joined = jnp.concatenate([gate_w[0], up_w[0], down_w[0]], axis=0)
    w_left, w_right = shift(joined, 1, "x", n), shift(joined, -1, "x", n)
    own, code = payload_call(tokens, out_grad, expert_ids.T, keep_flags.T, route_weights.T)

    chunk = lax.all_gather(own, FAR, axis=0, tiled=True)
    left, right = shift(chunk, 1, Z, nz), shift(chunk, -1, Z, nz)

    def exchange(packed):
        rows, width = packed.shape
        return lax.all_to_all(
            packed.reshape(8, rows // 8, width), YC, split_axis=0, concat_axis=0, tiled=True
        ).reshape(rows, width)

    rows_a = exchange(pack_call(zs, [chunk], step))
    packed_b = pack_call(zs, [left, right], step)
    packed_b, w_left, w_right = lax.optimization_barrier((packed_b, w_left, w_right))
    w_low, w_top, low, top = halves_call(w_left, w_right, left, right)
    w_a, w_b = shift(w_top, -1, "x", n), shift(w_low, 1, "x", n)
    rest_a, rest_b = shift(top, -1, Z, nz), shift(low, 1, Z, nz)
    rest_a, rest_b, _ = lax.optimization_barrier((rest_a, rest_b, packed_b))
    packed_b, rows_a = lax.optimization_barrier((packed_b, rows_a))
    rows_b = exchange(packed_b)
    packed_c = pack_call(zs, [rest_a, rest_b], step)
    packed_c, rows_b = lax.optimization_barrier((packed_c, rows_b))
    rows_c = exchange(packed_c)

    chunks = [rows_a, rows_b, rows_c]
    back, d_own, scaled, go, come, p_right, p_left = rows_call(
        zs, chunks, [joined, w_left, w_right, w_a, w_b]
    )
    x_ab = jnp.concatenate([rows_a[:, :features], rows_b[:, :features]], axis=0)
    x_left, x_right = shift(x_ab, 1, "x", n), shift(x_ab, -1, "x", n)
    go, come, x_left, x_right = lax.optimization_barrier((go, come, x_left, x_right))
    home = lax.all_to_all(
        back.reshape(-1, CAPACITY, back.shape[1]), PLACE, split_axis=0, concat_axis=0, tiled=True
    ).reshape(back.shape)

    from_left, from_right = shift(go, 1, "x", n), shift(come, -1, "x", n)
    hid, mid, cut = 2 * half, x_ab.shape[0] // 2, rows_c.shape[0] // 2
    at = hid + d_own.size // go.shape[1]
    end_a, end_b = go.shape[0] - 2 * cut, come.shape[0] - 2 * cut
    two_a = shift(
        jnp.concatenate(
            [
                (p_right.astype(F32) + from_left[:half].astype(F32)).astype(BF),
                from_left[at:end_a],
                x_left[mid:],
                from_left[end_a : end_a + cut],
            ],
            axis=0,
        ),
        1, "x", n,
    )
    two_b = shift(
        jnp.concatenate(
            [
                (p_left.astype(F32) + from_right[half:hid].astype(F32)).astype(BF),
                from_right[at:end_b],
                x_right[:mid],
                from_right[end_b + cut :],
            ],
            axis=0,
        ),
        -1, "x", n,
    )
    grad_gate, grad_up, grad_down = weights_call(
        scaled, d_own, chunks, x_ab, x_left, x_right, rows_c[:, :features],
        [from_left, from_right, two_a, two_b],
    )

    token_grad, slot_score = home_call(code, home, features)
    return (token_grad, slot_score.T, grad_gate[None], grad_up[None], grad_down[None])


def solution(mesh):
    fine = Mesh(mesh.devices.reshape(2, 4, 2, 2, 4, 4), (*PLACE, "x"))
    by_row = P((*PLACE, "x"), None)
    by_expert = P(PLACE, "x", None)
    return jax.shard_map(
        local,
        mesh=fine,
        in_specs=(by_row,) * 5 + (by_expert,) * 3,
        out_specs=(by_row,) * 2 + (by_expert,) * 3,
        check_vma=False,
    )
```

```python
import jax
import jax.numpy as jnp
from jax import lax
from jax.experimental import pallas as pl
from jax.experimental.pallas import tpu as pltpu
from jax.sharding import Mesh, PartitionSpec as P

BF = jnp.bfloat16
F32 = jnp.float32
LANES = 128
CAPACITY = 2
MIB = 1024 * 1024
FAR = ("zh", "zq")
Z = ("zh", "zq", "zr")
YC = ("y", "c")
PLACE = ("zh", "y", "c", "zq", "zr")


def dot(a, b, da, db):
    return lax.dot_general(a, b, (((da,), (db,)), ((), ())), preferred_element_type=F32)


def iota(shape, axis):
    return lax.broadcasted_iota(jnp.int32, shape, axis)


def shift(block, step, axes, n):
    return lax.ppermute(block, axes, [(i, (i + step) % n) for i in range(n)])


def vmem():
    return pl.BlockSpec(memory_space=pltpu.VMEM)


def payload_kernel(tok_ref, grad_ref, ids_ref, keep_ref, weight_ref, out_ref, code_ref):
    features = tok_ref.shape[1]
    top, rows = ids_ref.shape
    experts = LANES
    ids, kept = ids_ref[...], keep_ref[...] > 0
    names = iota((experts, rows), 0)
    named = [names == ids[k : k + 1, :] for k in range(top)]
    tally = sum(jnp.where(named[k] & kept[k : k + 1, :], 1.0, 0.0) for k in range(top))
    before = (iota((rows, rows), 0) < iota((rows, rows), 1)).astype(BF)
    earlier = dot(tally.astype(BF), before, 1, 0)
    position = jnp.concatenate(
        [jnp.sum(jnp.where(named[k], earlier, 0.0), axis=0, keepdims=True) for k in range(top)],
        axis=0,
    )
    code = jnp.where(kept, ids.astype(F32) * CAPACITY + position + 1.0, 0.0)
    code_ref[...] = code
    spread = (iota((rows, LANES), 0) == iota((rows, LANES), 1)).astype(BF)
    both = jnp.concatenate([code.astype(BF), weight_ref[...]], axis=0)
    out_ref[:, :features] = tok_ref[...]
    out_ref[:, features : 2 * features] = grad_ref[...]
    out_ref[:, 2 * features :] = dot(both, spread, 1, 0).astype(BF)


def payload_call(tokens, out_grad, ids, keep, weights):
    rows, features = tokens.shape
    return pl.pallas_call(
        payload_kernel,
        out_shape=[
            jax.ShapeDtypeStruct((rows, 2 * features + LANES), BF),
            jax.ShapeDtypeStruct(ids.shape, F32),
        ],
        in_specs=[vmem()] * 5,
        out_specs=[vmem()] * 2,
        name="payload",
    )(tokens, out_grad, ids, keep, weights)


def pack_kernel(step, zs_ref, *refs):
    blocks, out_ref = refs[:-1], refs[-1]
    count = sum(b.shape[0] for b in blocks)
    zn = count // step
    rows, width = out_ref.shape
    features = (width - LANES) // 2
    half = step // 2
    codes = jnp.zeros((half, count), F32)
    weights = jnp.zeros((half, count), F32)
    at = 0
    for block in blocks:
        for first in range(0, block.shape[0], step):
            place = (iota((LANES, count), 0) + at == iota((LANES, count), 1)) & (
                iota((LANES, count), 0) < step
            )
            both = dot(
                block[first : first + step, 2 * features :], place.astype(BF), 1, 0
            )
            codes = codes + both[:half]
            weights = weights + both[half:]
            at += step
    zh, zl = zs_ref[0], zs_ref[1]
    row, col = iota((rows, count), 0), iota((rows, count), 1)
    dest = row // (zn * CAPACITY)
    wanted = ((zh * 64 + dest * 8 + zl) * CAPACITY + row % CAPACITY + 1).astype(F32)
    wanted = jnp.where((row // CAPACITY) % zn == col // step, wanted, -1.0)
    pick = jnp.zeros((rows, count), F32)
    coef = jnp.zeros((rows, count), F32)
    for k in range(half):
        hit = wanted == codes[k : k + 1, :]
        pick = pick + jnp.where(hit, 1.0, 0.0)
        coef = coef + jnp.where(hit, weights[k : k + 1, :], 0.0)
    pick = pick.astype(BF)
    tile = 1024
    for j in range(0, 2 * features, tile):
        total, at = None, 0
        for block in blocks:
            size = block.shape[0]
            part = dot(pick[:, at : at + size], block[:, j : j + tile], 1, 0)
            total = part if total is None else total + part
            at += size
        out_ref[:, j : j + tile] = total.astype(BF)
    out_ref[:, 2 * features :] = jnp.broadcast_to(
        jnp.sum(coef, axis=1, keepdims=True), (rows, LANES)
    ).astype(BF)


def pack_call(zs, blocks, step):
    count, width = sum(b.shape[0] for b in blocks), blocks[0].shape[1]
    rows = 8 * (count // step) * CAPACITY

    def body(*refs):
        pack_kernel(step, *refs)

    return pl.pallas_call(
        body,
        out_shape=jax.ShapeDtypeStruct((rows, width), BF),
        in_specs=[pl.BlockSpec(memory_space=pltpu.SMEM)] + [vmem()] * len(blocks),
        out_specs=vmem(),
        name="pack",
    )(zs, *blocks)


def halves_kernel(*refs):
    n = len(refs) // 2
    sources, targets, sems = refs[:n], refs[n : 2 * n], refs[-1]
    copies = []
    for i, (source, target) in enumerate(zip(sources, targets)):
        size = target.shape[0]
        first = size if i % 2 == 0 else 0
        copies.append(pltpu.make_async_copy(source.at[pl.ds(first, size)], target, sems.at[i]))
    for copy in copies:
        copy.start()
    for copy in copies:
        copy.wait()


def halves_call(*blocks):
    return pl.pallas_call(
        halves_kernel,
        out_shape=[jax.ShapeDtypeStruct((b.shape[0] // 2, b.shape[1]), BF) for b in blocks],
        in_specs=[pl.BlockSpec(memory_space=pl.ANY)] * len(blocks),
        out_specs=[vmem()] * len(blocks),
        scratch_shapes=[pltpu.SemaphoreType.DMA((len(blocks),))],
        cost_estimate=pl.CostEstimate(
            flops=0, bytes_accessed=2 * sum(b.size for b in blocks), transcendentals=0
        ),
        name="halves",
    )(*blocks)


def homes(z, rows):
    row, place = iota((rows, rows), 0), iota((rows, rows), 1)
    quarter = rows // 4
    first, last = row < quarter, row >= 3 * quarter
    inside = jnp.where(first, row, jnp.where(last, row - 3 * quarter, row - quarter))
    zn = jnp.where(first | last, 4, 8)
    source = inside // (zn * CAPACITY)
    zi = (inside // CAPACITY) % zn
    turn = jnp.where(first, 0, jnp.where(last, 2, jnp.where(zi < 4, 3, 1)))
    zed = 4 * (zi % 4) + (z + turn) % 4
    home = ((zed // 8) * 64 + source * 8 + zed % 8) * CAPACITY + inside % CAPACITY
    return (home == place).astype(BF)


def rows_kernel(zs_ref, *refs):
    (a_ref, b_ref, c_ref, *w_refs), refs = refs[:8], refs[8:]
    p_ref, d_ref, s_ref, go_ref, come_ref, right_ref, left_ref = refs[:7]
    gu, dn, rows, d_all, s_all, sems = refs[7:]
    hid = dn.shape[1]
    count, width = rows.shape
    features = (width - LANES) // 2
    quarter = count // 4
    pairs = [
        (a_ref, rows.at[pl.ds(0, quarter)]),
        (b_ref, rows.at[pl.ds(quarter, 2 * quarter)]),
        (c_ref, rows.at[pl.ds(3 * quarter, quarter)]),
    ]
    for q in range(3):
        pairs.append((w_refs[q].at[pl.ds(0, 2 * hid)], gu.at[pl.ds(q * 2 * hid, 2 * hid)]))
        pairs.append((w_refs[q].at[pl.ds(2 * hid, hid)], dn.at[q]))
    top, first = w_refs[3].shape[0], 6 * hid
    pairs.append((w_refs[3], gu.at[pl.ds(first, top)]))
    pairs.append((w_refs[4].at[pl.ds(0, 2 * hid - top)], gu.at[pl.ds(first + top, 2 * hid - top)]))
    pairs.append((w_refs[4].at[pl.ds(2 * hid - top, hid)], dn.at[3]))
    copies = [pltpu.make_async_copy(s, t, sems.at[i]) for i, (s, t) in enumerate(pairs)]
    for copy in copies:
        copy.start()
    for copy in copies[:3]:
        copy.wait()
    home = homes(zs_ref[0] * 8 + zs_ref[1], count)
    coef = rows[:, 2 * features :].astype(F32).T[0:1, :]
    score = None
    for q in range(4):
        for copy in copies[3 + 2 * q : 5 + 2 * q + q // 3]:
            copy.wait()
        first = q * 2 * hid
        pre = dot(gu[first : first + 2 * hid, :], rows[:, :features], 1, 1)
        back = dot(dn[q], rows[:, features : 2 * features], 1, 1)
        gate_pre, up_pre = pre[:hid], pre[hid:]
        sigma = jax.nn.sigmoid(gate_pre)
        active = gate_pre * sigma
        hidden = active * up_pre
        part = jnp.sum(hidden.astype(BF).astype(F32) * back, axis=0, keepdims=True)
        score = part if score is None else score + part
        d_hidden = coef * back
        d_gate = d_hidden * up_pre * sigma * (1.0 + gate_pre * (1.0 - sigma))
        d_all[first : first + hid, :] = d_gate.astype(BF)
        d_all[first + hid : first + 2 * hid, :] = (d_hidden * active).astype(BF)
        s_all[q] = (coef * hidden).astype(BF)
    moved = dot(d_all[...], home, 1, 0).astype(BF)
    tile = 512
    for j in range(0, features, tile):
        p_ref[:, j : j + tile] = dot(moved, gu[:, j : j + tile], 0, 0).astype(BF)
    score = dot(jnp.broadcast_to(score, (LANES, count)).astype(BF), home, 1, 0)
    p_ref[:, features:] = score.T.astype(BF)
    d_ref[...] = d_all[: 2 * hid, :]
    s_ref[...] = s_all[0]
    half, size = hid // 2, 2 * hid * count // features
    most, end = 2 * size // 3, hid + size
    for j in range(features // count):
        part, at = slice(j * count, (j + 1) * count), j * size
        left, right, two = 2 * hid + at, 4 * hid + at, 6 * hid + at
        come_ref[hid:end, part] = d_all[left : left + size, :]
        go_ref[hid:end, part] = d_all[right : right + size, :]
        go_ref[end : end + most, part] = d_all[two : two + most, :]
        come_ref[end : end + size - most, part] = d_all[two + most : two + size, :]
    go_ref[end + most :, :] = rows[3 * quarter :, :features]
    come_ref[end + size - most :, :] = rows[3 * quarter :, :features]
    for j in range(0, features, tile):
        part = slice(j, j + tile)
        grads = rows[:, features + j : features + j + tile]
        left, right, two = [dot(s_all[q], grads, 1, 0).astype(BF) for q in (1, 2, 3)]
        go_ref[:half, part] = two[:half]
        go_ref[half:hid, part] = right[half:]
        come_ref[:half, part] = left[:half]
        come_ref[half:hid, part] = two[half:]
        right_ref[:, part] = right[:half]
        left_ref[:, part] = left[half:]


def rows_call(zs, chunks, weights):
    count = sum(c.shape[0] for c in chunks)
    width = chunks[0].shape[1]
    n, hid, features = 4, weights[0].shape[0] // 3, weights[0].shape[1]
    size, last = 2 * hid * count // features, count // 4
    fixed = hid + size + last
    return pl.pallas_call(
        rows_kernel,
        out_shape=[
            jax.ShapeDtypeStruct((count, features + LANES), BF),
            jax.ShapeDtypeStruct((2 * hid, count), BF),
            jax.ShapeDtypeStruct((hid, count), BF),
            jax.ShapeDtypeStruct((fixed + 2 * size // 3, features), BF),
            jax.ShapeDtypeStruct((fixed + size // 3, features), BF),
            jax.ShapeDtypeStruct((hid // 2, features), BF),
            jax.ShapeDtypeStruct((hid // 2, features), BF),
        ],
        in_specs=[pl.BlockSpec(memory_space=pltpu.SMEM)] + [pl.BlockSpec(memory_space=pl.ANY)] * 8,
        out_specs=[vmem()] * 7,
        scratch_shapes=[
            pltpu.VMEM((n * 2 * hid, features), BF),
            pltpu.VMEM((n, hid, features), BF),
            pltpu.VMEM((count, width), BF),
            pltpu.VMEM((n * 2 * hid, count), BF),
            pltpu.VMEM((n, hid, count), BF),
            pltpu.SemaphoreType.DMA((4 + 2 * n,)),
        ],
        compiler_params=pltpu.CompilerParams(vmem_limit_bytes=56 * MIB),
        cost_estimate=pl.CostEstimate(
            flops=2 * count * features * hid * n * 5,
            bytes_accessed=2 * features * hid * 12 + 6 * count * features,
            transcendentals=count * hid * n,
        ),
        name="rows",
    )(zs, *chunks, *weights)


def weights_kernel(*refs):
    s_ref, d_refs, g_refs, x_refs = refs[0], refs[1:6], refs[6:9], refs[9:17]
    gate_ref, up_ref, down_ref, factors, rows, grads = refs[17:]
    own, left, right, last, from_left, from_right, two_a, two_b = x_refs
    hid = gate_ref.shape[0]
    most, half, ends = own.shape[0], hid // 2, last.shape[0]
    mid, cut = most // 2, ends // 2
    count = rows.shape[1]
    size, top = d_refs[1].shape[0], d_refs[3].shape[0]

    @pl.when(pl.program_id(0) == 0)
    def _():
        factors[0] = d_refs[0][...]
        for j in range(d_refs[1].shape[1] // count):
            part, at = slice(j * count, (j + 1) * count), j * size
            for q in (1, 2):
                factors[q, at : at + size, :] = d_refs[q][:, part]
            factors[3, at : at + top, :] = d_refs[3][:, part]
            factors[3, at + top : at + size, :] = d_refs[4][:, part]

    for q, (first, end) in enumerate(((own, last), (left, from_left), (right, from_right))):
        rows[q, :most, :] = first[...]
        rows[q, most:, :] = end[end.shape[0] - ends :, :]
    far_a, far_b = half + top, half + size - top
    rows[3, :mid, :] = two_b[far_b : far_b + mid, :]
    rows[3, mid:most, :] = two_a[far_a : far_a + mid, :]
    rows[3, most : most + cut, :] = two_a[far_a + mid :, :]
    rows[3, most + cut :, :] = two_b[far_b + mid :, :]
    total = sum(dot(factors[q], rows[q], 1, 0) for q in range(4)).astype(BF)
    gate_ref[...] = total[:hid]
    up_ref[...] = total[hid:]

    at = 0
    for ref in g_refs:
        grads[at : at + ref.shape[0], :] = ref[...]
        at += ref.shape[0]
    down = dot(s_ref[...], grads[...], 1, 0)
    upper = two_a[:half, :].astype(F32) + from_right[:half, :].astype(F32)
    lower = from_left[half:hid, :].astype(F32) + two_b[:half, :].astype(F32)
    down_ref[:half, :] = (down[:half] + upper).astype(BF)
    down_ref[half:, :] = (down[half:] + lower).astype(BF)


def weights_call(scaled, d_own, chunks, x_ab, x_left, x_right, x_c, messages):
    tile = 512
    from_left, from_right, two_a, two_b = messages
    n, (both, count), features = 4, d_own.shape, x_ab.shape[1]
    hid, size = both // 2, both * count // features
    top, low = 2 * size // 3, size // 3

    def piece(rows, first):
        return pl.BlockSpec((rows, features), lambda j: (first // rows, 0))

    packed = [piece(size, hid), piece(size, hid), piece(top, hid // 2), piece(low, hid // 2)]
    skip = features // tile
    grads = [pl.BlockSpec((c.shape[0], tile), lambda j: (0, skip + j)) for c in chunks]
    tiled = [x_ab, x_left, x_right, x_c, *messages]
    return pl.pallas_call(
        weights_kernel,
        grid=(features // tile,),
        out_shape=[jax.ShapeDtypeStruct((hid, features), BF)] * 3,
        in_specs=[
            pl.BlockSpec(scaled.shape, lambda j: (0, 0)),
            pl.BlockSpec(d_own.shape, lambda j: (0, 0)),
            *packed,
            *grads,
            *[pl.BlockSpec((x.shape[0], tile), lambda j: (0, j)) for x in tiled],
        ],
        out_specs=[pl.BlockSpec((hid, tile), lambda j: (0, j))] * 3,
        scratch_shapes=[
            pltpu.VMEM((n, both, count), BF),
            pltpu.VMEM((n, count, tile), BF),
            pltpu.VMEM((count, tile), BF),
        ],
        compiler_params=pltpu.CompilerParams(vmem_limit_bytes=32 * MIB),
        cost_estimate=pl.CostEstimate(
            flops=40 * n * count * features * hid,
            bytes_accessed=2 * features * (2 * n * count + 3 * hid),
            transcendentals=0,
        ),
        name="weight_grads",
    )(scaled, d_own, *messages, *chunks, *tiled)


def home_kernel(code_ref, home_ref, grad_ref, score_ref):
    top, rows = code_ref.shape
    places = home_ref.shape[0]
    features = grad_ref.shape[1]
    wanted = (iota((places, rows), 0) + 1).astype(F32)
    hits = [jnp.where(wanted == code_ref[k : k + 1, :], 1.0, 0.0) for k in range(top)]
    score = home_ref[:, features : features + 1].astype(F32)
    score_ref[...] = jnp.concatenate(
        [jnp.sum(hit * score, axis=0, keepdims=True) for hit in hits], axis=0
    ).astype(BF)
    pick = sum(hits).astype(BF)
    grad_ref[...] = dot(pick, home_ref[:, :features], 0, 0).astype(BF)


def home_call(code, home, features):
    return pl.pallas_call(
        home_kernel,
        out_shape=[
            jax.ShapeDtypeStruct((code.shape[1], features), BF),
            jax.ShapeDtypeStruct(code.shape, BF),
        ],
        in_specs=[vmem()] * 2,
        out_specs=[vmem()] * 2,
        name="home",
    )(code, home)


def local(tokens, out_grad, expert_ids, keep_flags, route_weights, gate_w, up_w, down_w):
    nz, n = lax.axis_size(Z), lax.axis_size("x")
    step, features = tokens.shape
    zs = jnp.stack([lax.axis_index(a) for a in ("zh", ("zq", "zr"), "x")]).astype(jnp.int32)
    half = gate_w.shape[1] // 2

    joined = jnp.concatenate([gate_w[0], up_w[0], down_w[0]], axis=0)
    w_left, w_right = shift(joined, 1, "x", n), shift(joined, -1, "x", n)
    own, code = payload_call(tokens, out_grad, expert_ids.T, keep_flags.T, route_weights.T)

    chunk = lax.all_gather(own, FAR, axis=0, tiled=True)
    left, right = shift(chunk, 1, Z, nz), shift(chunk, -1, Z, nz)

    def exchange(packed):
        rows, width = packed.shape
        return lax.all_to_all(
            packed.reshape(8, rows // 8, width), YC, split_axis=0, concat_axis=0, tiled=True
        ).reshape(rows, width)

    rows_a = exchange(pack_call(zs, [chunk], step))
    packed_b = pack_call(zs, [left, right], step)
    packed_b, w_left, w_right = lax.optimization_barrier((packed_b, w_left, w_right))
    w_low, w_top, low, top = halves_call(w_left, w_right, left, right)
    w_a, w_b = shift(w_top, -1, "x", n), shift(w_low, 1, "x", n)
    rest_a, rest_b = shift(top, -1, Z, nz), shift(low, 1, Z, nz)
    rest_a, rest_b, _ = lax.optimization_barrier((rest_a, rest_b, packed_b))
    packed_b, rows_a = lax.optimization_barrier((packed_b, rows_a))
    rows_b = exchange(packed_b)
    packed_c = pack_call(zs, [rest_a, rest_b], step)
    packed_c, rows_b = lax.optimization_barrier((packed_c, rows_b))
    rows_c = exchange(packed_c)

    chunks = [rows_a, rows_b, rows_c]
    back, d_own, scaled, go, come, p_right, p_left = rows_call(
        zs, chunks, [joined, w_left, w_right, w_a, w_b]
    )
    x_ab = jnp.concatenate([rows_a[:, :features], rows_b[:, :features]], axis=0)
    x_left, x_right = shift(x_ab, 1, "x", n), shift(x_ab, -1, "x", n)
    go, come, x_left, x_right = lax.optimization_barrier((go, come, x_left, x_right))
    home = lax.all_to_all(
        back.reshape(-1, CAPACITY, back.shape[1]), PLACE, split_axis=0, concat_axis=0, tiled=True
    ).reshape(back.shape)

    from_left, from_right = shift(go, 1, "x", n), shift(come, -1, "x", n)
    hid, mid, cut = 2 * half, x_ab.shape[0] // 2, rows_c.shape[0] // 2
    at = hid + d_own.size // go.shape[1]
    end_a, end_b = go.shape[0] - 2 * cut, come.shape[0] - 2 * cut
    two_a = shift(
        jnp.concatenate(
            [
                (p_right.astype(F32) + from_left[:half].astype(F32)).astype(BF),
                from_left[at:end_a],
                x_left[mid:],
                from_left[end_a : end_a + cut],
            ],
            axis=0,
        ),
        1, "x", n,
    )
    two_b = shift(
        jnp.concatenate(
            [
                (p_left.astype(F32) + from_right[half:hid].astype(F32)).astype(BF),
                from_right[at:end_b],
                x_right[:mid],
                from_right[end_b + cut :],
            ],
            axis=0,
        ),
        -1, "x", n,
    )
    grad_gate, grad_up, grad_down = weights_call(
        scaled, d_own, chunks, x_ab, x_left, x_right, rows_c[:, :features],
        [from_left, from_right, two_a, two_b],
    )

    token_grad, slot_score = home_call(code, home, features)
    return (token_grad, slot_score.T, grad_gate[None], grad_up[None], grad_down[None])


def solution(mesh):
    fine = Mesh(mesh.devices.reshape(2, 4, 2, 2, 4, 4), (*PLACE, "x"))
    by_row = P((*PLACE, "x"), None)
    by_expert = P(PLACE, "x", None)
    return jax.shard_map(
        local,
        mesh=fine,
        in_specs=(by_row,) * 5 + (by_expert,) * 3,
        out_specs=(by_row,) * 2 + (by_expert,) * 3,
        check_vma=False,
    )
```
